32 devices in a mesh: section: 4 (over y, x), batch: 8 (over z, core).
Axes of the slice: x: 2, y: 2, z: 4, core: 2. Of those that a mesh axis runs over, the one named last changes fastest.
Arguments:
- tokens: bfloat16 [4, 2048, 512], P('section', 'batch'), may hold values from -6 to 6
- cotangent: bfloat16 [4, 2048, 512], P('section', 'batch'), may hold values from -6 to 6
- weights: bfloat16 [4, 4, 512, 1024], P('section'), may hold values from -0.25 to 0.25
- biases: float32 [4, 2, 1024], P('section'), may hold values from -8 to 8
- gains: float32 [4, 512], P('section'), may hold values from 0.5 to 1.5
- lengths: int32 [4, 16], P(None, 'batch'), may hold values from 0 to 256, as said below
Outputs:
- final: bfloat16 [4, 2048, 512], P('section', 'batch')
- input_grad: bfloat16 [4, 2048, 512], P('section', 'batch')
- weight_grad: float32 [4, 4, 512, 1024], P('section')
- bias_grad: float32 [4, 2, 1024], P('section')
- gain_grad: float32 [4, 512], P('section')
The draws below stay inside these ranges and needn't reach their ends.
Inputs may be any that keep to these rules, and one draw needn't show every extreme that they name: `lengths`: each group of 2 consecutive entries of a row belongs to one slot of 256 rows and sums to at most 256. Its first entry is nonzero, and a zero is followed only by zeros. In a slot with two sequences each has 128 rows or more. In every draw some slot holds a single sequence of exactly 256 rows.
All inputs are finite; a program needn't handle non-finite values.
Results may differ from the reference program's by a relative error of at most 0.015.
Values may be sent and summed in bfloat16 or wider, within the bound.
A program may use at most 384 MiB of HBM per device.

```python
import math
import jax
import jax.numpy as jnp
from jax import lax

D = 512
H = 1024
TOK_MB = 256
MICRO = 4
SEQ_SLOT = 2
LEAST = 128
ROWS = 2048
N_SECTION = 4
N_BATCH = 8


def draw_lengths(key, part):
    key = jax.random.fold_in(key, 11)
    first_key, second_key, third_key, fourth_key = jax.random.split(key, 4)
    raw = jax.random.randint(first_key, (MICRO, N_BATCH, SEQ_SLOT), LEAST, TOK_MB // SEQ_SLOT + 1)
    dropped = jax.random.randint(fourth_key, (MICRO, N_BATCH, 1), 0, 4) == 0
    count = SEQ_SLOT - dropped.astype(jnp.int32)
    present = jnp.arange(SEQ_SLOT)[None, None, :] < count
    raw = jnp.where(present, raw, 0)
    pick_micro = jax.random.randint(second_key, (), 0, MICRO)
    pick_batch = jax.random.randint(third_key, (), 0, N_BATCH)
    filled = jnp.where(jnp.arange(SEQ_SLOT) == 0, TOK_MB, 0)
    chosen = (jnp.arange(MICRO)[:, None] == pick_micro) & (jnp.arange(N_BATCH)[None, :] == pick_batch)
    raw = jnp.where(chosen[:, :, None], filled[None, None, :], raw)
    return raw.reshape(MICRO, N_BATCH * SEQ_SLOT).astype(jnp.int32)


def block_levels(own_key, shape, cuts, low, top_value):
    level, own = 1.0, jax.random.fold_in(own_key, 6)
    for dim, shards_of in cuts:
        steps = jnp.exp(jax.random.uniform(jax.random.fold_in(own, dim), (shards_of,), jnp.float32, low / len(cuts), top_value / len(cuts)))
        level = level * jnp.repeat(steps, shape[dim] // shards_of).reshape([-1 if axis == dim else 1 for axis in range(len(shape))])
    return level


def centred(own_key, shape, scale, limit, shards=(), kind=jnp.bfloat16):
    drawn = scale * jax.random.normal(own_key, shape, jnp.float32)
    if shards:
        drawn = drawn * block_levels(own_key, shape, shards, -0.22, 0.18)
    return jnp.clip(drawn, -limit, limit).astype(kind)


def setup_inputs(seed: int = 0) -> dict:
    keys = jax.random.split(jax.random.key(seed), 7)
    tokens = centred(keys[0], (MICRO, ROWS, D), 1.0, 6.0, ((0, 4), (1, 8)))
    cotangent = centred(keys[1], (MICRO, ROWS, D), 1.0, 6.0, ((0, 4), (1, 8)))
    weights = centred(keys[2], (N_SECTION, 4, D, H), D ** -0.5, 0.25, ((0, 4),))
    biases = centred(keys[3], (N_SECTION, 2, H), 2.0, 8.0, ((0, 4),), jnp.float32)
    gains = jnp.clip(1.0 + 0.1 * jax.random.normal(keys[4], (N_SECTION, D), jnp.float32), 0.5, 1.5)
    lengths = draw_lengths(jax.random.fold_in(keys[6], 71), 0)
    return dict(tokens=tokens, cotangent=cotangent, weights=weights, biases=biases, gains=gains, lengths=lengths)


@jax.custom_vjp
def low(v):
    return lax.optimization_barrier(v.astype(jnp.bfloat16)).astype(jnp.float32)

@jax.custom_vjp
def low_back(v):
    return v

def low_keep(v):
    return (low(v), None)

def low_pass(kept, grad):
    return (grad,)

def back_keep(v):
    return (v, None)

def back_low(kept, grad):
    return (low(grad),)
low.defvjp(low_keep, low_pass)
low_back.defvjp(back_keep, back_low)
epsilon = 1e-05
highest = lax.Precision.HIGHEST

def normalize(x, gain):
    return x * lax.rsqrt(lax.optimization_barrier(jnp.mean(x * x, axis=-1, keepdims=True)) + epsilon) * gain

def gate_scan(projected, valid, keep):
    forget = -jax.nn.softplus(-projected[..., 0, :])
    admit = -jax.nn.softplus(-projected[..., 1, :])
    total = jnp.logaddexp(forget, admit)
    decay = keep[..., None] * jnp.exp(forget - total)
    inflow = valid[..., None] * jnp.exp(admit - total) * projected[..., 2, :]

    def advance(state, pair):
        state = pair[0] * state + pair[1]
        return (state, state)
    start = jnp.zeros(decay[:, 0].shape, jnp.float32)
    unused, states = lax.scan(advance, start, (jnp.swapaxes(decay, 0, 1), jnp.swapaxes(inflow, 0, 1)))
    return jnp.swapaxes(states, 0, 1)

def mixer(x, weight, bias, gain, valid, keep):
    normed = low(normalize(x, gain))
    bias_full = jnp.concatenate([bias, jnp.zeros((1, bias.shape[1]), jnp.float32)], axis=0)
    projected = low_back(jnp.einsum('gtd,kdh->gtkh', normed, weight[:3], precision=highest) + bias_full)
    state = low(gate_scan(projected, valid, keep))
    branch = jnp.einsum('gth,dh->gtd', state, weight[3], precision=highest)
    return x + valid[..., None] * branch

def feed_forward(x, weight, bias, gain, valid):
    normed = low(normalize(x, gain))
    hidden = low_back(jnp.einsum('gtd,kdh->gtkh', normed, weight[:2], precision=highest) + bias)
    active = low(jax.nn.gelu(hidden, approximate=False))
    branch = jnp.einsum('gtkh,kdh->gtd', active, weight[2:], precision=highest)
    return x + valid[..., None] * branch

def forward(inputs, weights, biases, gains, valid, keep):

    def group(x, valid_group, keep_group):
        for index in range(N_SECTION):
            if index % 2 == 0:
                x = mixer(x, weights[index], biases[index], gains[index], valid_group, keep_group)
            else:
                x = feed_forward(x, weights[index], biases[index], gains[index], valid_group)
            if index < N_SECTION - 1:
                x = low_back(low(x))
        return low(x) * valid_group[..., None]
    checked = jax.checkpoint(group)

    def advance(carry, items):
        return (carry, checked(items[0], items[1], items[2]))
    unused, finals = lax.scan(advance, jnp.zeros((), jnp.float32), (inputs, valid, keep))
    return finals

def reference(tokens, cotangent, weights, biases, gains, lengths):
    sizes = lengths.reshape(MICRO, N_BATCH, SEQ_SLOT)
    ends = jnp.cumsum(sizes, axis=-1)
    starts = ends - sizes
    places = jnp.arange(TOK_MB, dtype=jnp.int32)
    inside = places[None, None, :] < ends[:, :, -1:]
    first = jnp.any((places[None, None, None, :] == starts[..., None]) & (sizes[..., None] > 0), axis=2)
    valid = inside.astype(jnp.float32)
    keep = valid * (1.0 - first.astype(jnp.float32))
    valid = jnp.swapaxes(valid, 0, 1)
    keep = jnp.swapaxes(keep, 0, 1)

    def order(a):
        return jnp.swapaxes(a.astype(jnp.float32).reshape(MICRO, N_BATCH, TOK_MB, D), 0, 1)

    def back(a):
        return jnp.swapaxes(a, 0, 1).reshape(MICRO, ROWS, D)

    def run(inputs, weight_all, bias_all, gain_all):
        return forward(inputs, weight_all, bias_all, gain_all, valid, keep)
    finals, pull = jax.vjp(run, order(tokens), weights.astype(jnp.float32), biases, gains)
    grad_x, grad_w, grad_b, grad_g = pull(order(cotangent))
    scale = 1.0 / math.sqrt(MICRO * ROWS)
    return (back(finals).astype(jnp.bfloat16), back(grad_x).astype(jnp.bfloat16), grad_w * scale, grad_b * scale, grad_g * scale)
```

```python
import functools
import math

import jax
import jax.numpy as jnp
from jax import lax
from jax.experimental import pallas as pl
from jax.experimental.pallas import tpu as pltpu
from jax.sharding import PartitionSpec as P

MESH = pl.DeviceIdType.MESH
EPS = 1e-05
PART = 64
LANES = 256
TILE = (128, 256)
F32 = jnp.float32
BF16 = jnp.bfloat16


def dot(a, b):
    return jnp.dot(a, b, preferred_element_type=F32)


def dot_nt(a, b):
    return lax.dot_general(a, b, (((1,), (1,)), ((), ())), preferred_element_type=F32)


def dot_tn(a, b):
    return lax.dot_general(a, b, (((0,), (0,)), ((), ())), preferred_element_type=F32)


def order_matrix(rows, back):
    new = lax.broadcasted_iota(jnp.int32, (rows, rows), 1 if back else 0)
    old = lax.broadcasted_iota(jnp.int32, (rows, rows), 0 if back else 1)
    hit = (lax.rem(new, 8) * (rows // 8) + new // 8) == old
    return jnp.where(hit, 1.0, 0.0).astype(BF16)


def groups(value):
    return [value[8 * g : 8 * g + 8] for g in range(value.shape[0] // 8)]


def chain(gain, add, carry, back):
    row = lax.broadcasted_iota(jnp.int32, gain.shape, 0)
    for step in (1, 2, 4):
        shift = 8 - step if back else step
        inside = (row < 8 - step) if back else (row >= step)
        add = jnp.where(inside, gain * pltpu.roll(add, shift, 0) + add, add)
        gain = jnp.where(inside, gain * pltpu.roll(gain, shift, 0), gain)
    whole = gain * carry + add
    edge = 7 if back else 0
    enter = jnp.where(row == edge, carry, pltpu.roll(whole, 7 if back else 1, 0))
    last = whole[0:1] if back else whole[7:8]
    return enter, jnp.broadcast_to(last, gain.shape)


def relay_kernel(
    lengths,
    tokens,
    cotangent,
    weights,
    biases,
    gains,
    final_out,
    grad_out,
    wide_out,
    small_out,
    w,
    stage,
    x_in,
    do_in,
    x_out,
    dx_out,
    fin,
    gin,
    valid_s,
    keep_s,
    normed,
    down,
    right,
    coef,
    h_carry,
    e_carry,
    gain_acc,
    sib_out,
    sib_in,
    own,
    up_out,
    up_in,
    ret_in,
    tot_out,
    tot_in,
    small,
    load_sem,
    tok_sem,
    fwd_send,
    fwd_recv,
    bwd_send,
    bwd_recv,
    fin_recv,
    gin_recv,
    tail_sem,
    small_sem,
    out_sem,
):
    micro, rows, width = x_in.shape
    parts = rows // PART
    hidden = w.shape[2]
    section, batch = lax.axis_index("section"), lax.axis_index("batch")
    sections, batches = lax.axis_size("section"), lax.axis_size("batch")
    last = sections - 1
    mixer = lax.rem(section, 2) == 0
    feed = lax.rem(section, 2) == 1
    chips = batches // 2
    chip, core = batch // 2, lax.rem(batch, 2)
    sibling = batch + 1 - 2 * core
    half = chips // 2
    low_side = chip < half
    step_in = jnp.where(low_side, 2, -2)
    inner = batch + step_in
    outer = batch - step_in
    middle = (chip == half - 1) | (chip == half)
    has_outer = (chip > 0) & (chip < chips - 1)
    depth = jnp.where(low_side, half - 1 - chip, chip - half)

    def remote(src, dst, send, recv, to_section, to_batch):
        return pltpu.make_async_remote_copy(
            src_ref=src,
            dst_ref=dst,
            send_sem=send,
            recv_sem=recv,
            device_id=(to_section, to_batch),
            device_id_type=MESH,
        )

    loads = [pltpu.make_async_copy(tokens.at[0], stage.at[0], load_sem.at[4])]
    loads.append(pltpu.make_async_copy(cotangent.at[0], stage.at[1], load_sem.at[5]))
    for j in range(4):
        loads.append(pltpu.make_async_copy(weights.at[0, j], w.at[j], load_sem.at[j]))
    for copy in loads:
        copy.start()

    barrier = pltpu.get_barrier_semaphore()
    for other in range(1, sections):
        pl.semaphore_signal(
            barrier, inc=1, device_id=(lax.rem(section + other, sections), batch), device_id_type=MESH
        )
    pl.semaphore_signal(barrier, inc=1, device_id=(section, sibling), device_id_type=MESH)
    pl.semaphore_signal(barrier, inc=1, device_id=(section, inner), device_id_type=MESH)

    @pl.when(has_outer)
    def _():
        pl.semaphore_signal(barrier, inc=1, device_id=(section, outer), device_id_type=MESH)

    spot = lax.broadcasted_iota(jnp.int32, (rows, 128), 0)
    spot_in = lax.rem(spot, PART)
    spot = spot - spot_in + lax.rem(spot_in, 8) * (PART // 8) + spot_in // 8
    for m in range(micro):
        end = jnp.int32(0)
        start_hit = jnp.zeros((rows, 128), F32)
        for k in range(lengths.shape[1]):
            start_hit = jnp.where(spot == end, 1.0, start_hit)
            end = end + lengths[m, k]
        valid = jnp.where(spot < end, 1.0, 0.0)
        valid_s[m] = valid
        keep_s[m] = valid * (1.0 - start_hit)
    h_carry[...] = jnp.zeros_like(h_carry)
    e_carry[...] = jnp.zeros_like(e_carry)
    gain_acc[...] = jnp.zeros_like(gain_acc)

    perm = order_matrix(PART, False)
    loads[0].wait()
    for c in range(parts):
        span = pl.ds(c * PART, PART)
        ordered = dot(perm, stage[0, span, :]).astype(BF16)
        stage[2, span, :] = ordered

        @pl.when(section == 0)
        def _():
            x_in[0, span, :] = ordered

    loads[1].wait()
    for c in range(parts):
        span = pl.ds(c * PART, PART)
        ordered = dot(perm, stage[1, span, :]).astype(BF16)
        stage[3, span, :] = ordered

        @pl.when(section == last)
        def _():
            do_in[last, span, :] = ordered

    pl.semaphore_wait(barrier, sections + 1 + jnp.where(has_outer, 1, 0))

    def token_copy(m):
        return remote(stage.at[2], x_in.at[m], tok_sem.at[0], tok_sem.at[2 + m], 0, batch)

    def cot_copy(m):
        return remote(stage.at[3], do_in.at[m], tok_sem.at[1], tok_sem.at[2 + micro + m], last, batch)

    @pl.when(section != 0)
    def _():
        token_copy(section).start()

    @pl.when(section != last)
    def _():
        cot_copy(section).start()

    for copy in loads[2:]:
        copy.wait()

    def wide(mask):
        return jnp.concatenate([mask] * (width // 128), axis=1)

    def slab(mask):
        return jnp.concatenate([mask] * (LANES // 128), axis=1)

    def fwd_copy(m, c):
        span = pl.ds(pl.multiple_of(c * PART, PART), PART)
        return remote(
            x_out.at[m, span],
            x_in.at[m, span],
            fwd_send.at[m, c],
            fwd_recv.at[m, c],
            jnp.minimum(section + 1, last),
            batch,
        )

    def fin_copy(m, c):
        span = pl.ds(pl.multiple_of(c * PART, PART), PART)
        return remote(x_out.at[m, span], fin.at[span], fwd_send.at[m, c], fin_recv.at[c], m, batch)

    def bwd_copy(m, c):
        span = pl.ds(pl.multiple_of(c * PART, PART), PART)
        return remote(
            dx_out.at[m, span],
            do_in.at[m, span],
            bwd_send.at[m, c],
            bwd_recv.at[m, c],
            jnp.maximum(section - 1, 0),
            batch,
        )

    def gin_copy(m, c):
        span = pl.ds(pl.multiple_of(c * PART, PART), PART)
        return remote(dx_out.at[m, span], gin.at[span], bwd_send.at[m, c], gin_recv.at[c], m, batch)

    def forward(m, c):
        span = pl.ds(pl.multiple_of(c * PART, PART), PART)
        line = pl.ds(pl.multiple_of(m * rows + c * PART, PART), PART)

        @pl.when(section > 0)
        def _():
            fwd_copy(m, c).wait_recv()

        @pl.when((section == 0) & (c == 0) & (m > 0))
        def _():
            token_copy(m).wait_recv()

        x = x_in[m, span, :].astype(F32)
        valid = valid_s[m, span, :]
        scale = lax.rsqrt(jnp.mean(x * x, axis=-1, keepdims=True) + EPS)
        nb = (x * scale * gains[...]).astype(BF16)
        normed[line, :] = nb

        @pl.when(mixer)
        def _():
            keep_l = slab(keep_s[m, span, :])
            valid_l = slab(valid)
            for blk in range(hidden // LANES):
                cols = slice(blk * LANES, (blk + 1) * LANES)
                zf = dot(nb, w[0, :, cols]) + biases[0, 0:1, cols]
                zi = dot(nb, w[1, :, cols]) + biases[0, 1:2, cols]
                zh = dot(nb, w[2, :, cols])
                low = jnp.minimum(jnp.minimum(zf, zi), 0.0)
                e0 = jnp.exp(low)
                top = e0 + jnp.exp(low - zi)
                bot = e0 + jnp.exp(low - zf)
                inv = 1.0 / (top + bot)
                decay = top * inv
                admit = bot * inv
                a = keep_l * decay
                iv = valid_l * admit
                b = iv * zh
                a_g, b_g = groups(a), groups(b)
                state, product = b_g[0], a_g[0]
                states, products = [state], [product]
                for g in range(1, len(a_g)):
                    state = a_g[g] * state + b_g[g]
                    product = a_g[g] * product
                    states.append(state)
                    products.append(product)
                enter, leave = chain(product, state, h_carry[:, cols], False)
                h_carry[:, cols] = leave
                hs = [s + p * enter for s, p in zip(states, products)]
                h_prev = jnp.concatenate([enter] + hs[:-1], axis=0)
                right[3, line, cols] = jnp.concatenate(hs, axis=0).astype(BF16)
                both = decay * admit * (keep_l * h_prev - valid_l * zh)
                coef[0, line, cols] = a
                coef[1, line, cols] = both / (1.0 + jnp.exp(zf))
                coef[2, line, cols] = -both / (1.0 + jnp.exp(zi))
                coef[3, line, cols] = iv
            y = dot_nt(right[3, line, :], w[3])
            x_out[m, span, :] = (x + wide(valid) * y).astype(BF16)

        @pl.when(feed)
        def _():
            for k in range(2):
                for blk in range(hidden // LANES):
                    cols = slice(blk * LANES, (blk + 1) * LANES)
                    u = dot(nb, w[k, :, cols]) + biases[0, k : k + 1, cols]
                    phi = 0.5 + 0.5 * lax.erf(u * math.sqrt(0.5))
                    right[2 + k, line, cols] = (u * phi).astype(BF16)
                    coef[k, line, cols] = phi + u * jnp.exp(-0.5 * u * u) * (1.0 / math.sqrt(2.0 * math.pi))
            y = dot_nt(right[2, line, :], w[2]) + dot_nt(right[3, line, :], w[3])
            x_out[m, span, :] = (x + wide(valid) * y).astype(BF16)

        @pl.when(section < last)
        def _():
            fwd_copy(m, c).start()

        @pl.when(section == last)
        def _():
            done = x_out[m, span, :].astype(F32) * wide(valid)
            x_out[m, span, :] = done.astype(BF16)

            @pl.when(m == section)
            def _():
                fin[span, :] = done.astype(BF16)

            @pl.when(m != section)
            def _():
                fin_copy(m, c).start()

    def backward(m, c):
        span = pl.ds(pl.multiple_of(c * PART, PART), PART)
        line = pl.ds(pl.multiple_of(m * rows + c * PART, PART), PART)

        @pl.when(section < last)
        def _():
            bwd_copy(m, c).wait_recv()

        @pl.when((section == last) & (c == parts - 1) & (m != last))
        def _():
            cot_copy(m).wait_recv()

        do = do_in[m, span, :].astype(F32) * wide(valid_s[m, span, :])
        dy = do.astype(BF16)
        down[line, :] = dy

        @pl.when(mixer)
        def _():
            for blk in range(hidden // LANES):
                cols = slice(blk * LANES, (blk + 1) * LANES)
                d_g = groups(dot(dy, w[3, :, cols]))
                a_g = groups(coef[0, line, cols])
                count = len(a_g)
                dhs, spread = [None] * count, [None] * count
                dhs[-1] = d_g[-1]
                for g in range(count - 2, -1, -1):
                    dhs[g] = d_g[g] + a_g[g + 1] * dhs[g + 1]
                    spread[g] = a_g[g + 1] if g == count - 2 else a_g[g + 1] * spread[g + 1]
                enter, leave = chain(a_g[0] * spread[0], a_g[0] * dhs[0], e_carry[:, cols], True)
                e_carry[:, cols] = leave
                dhs = [d + s * enter for d, s in zip(dhs[:-1], spread[:-1])] + [dhs[-1] + enter]
                dh = jnp.concatenate(dhs, axis=0)
                for j in range(3):
                    right[j, line, cols] = (dh * coef[1 + j, line, cols]).astype(BF16)

        @pl.when(feed)
        def _():
            for k in range(2):
                for blk in range(hidden // LANES):
                    cols = slice(blk * LANES, (blk + 1) * LANES)
                    da = dot(dy, w[2 + k, :, cols])
                    right[k, line, cols] = (da * coef[k, line, cols]).astype(BF16)

        def finish(dn):
            x = x_in[m, span, :].astype(F32)
            scale = lax.rsqrt(jnp.mean(x * x, axis=-1, keepdims=True) + EPS)
            xr = x * scale
            part = dn * xr
            gain_acc[...] += sum(groups(part))
            dng = dn * gains[...]
            mean = jnp.mean(dng * xr, axis=-1, keepdims=True)
            dx_out[m, span, :] = (do + scale * (dng - xr * mean)).astype(BF16)

        @pl.when(mixer)
        def _():
            finish(
                dot_nt(right[0, line, :], w[0])
                + dot_nt(right[1, line, :], w[1])
                + dot_nt(right[2, line, :], w[2])
            )

        @pl.when(feed)
        def _():
            finish(dot_nt(right[0, line, :], w[0]) + dot_nt(right[1, line, :], w[1]))

        @pl.when(section > 0)
        def _():
            bwd_copy(m, c).start()

        @pl.when(section == 0)
        def _():
            @pl.when(m == section)
            def _():
                gin[span, :] = dx_out[m, span, :]

            @pl.when(m != section)
            def _():
                gin_copy(m, c).start()

    ahead = jnp.minimum(sections - section, micro)

    @pl.loop(0, 2 * micro * parts)
    def _(step):
        q = step // parts
        c = lax.rem(step, parts)
        i = jnp.maximum(q - ahead, 0)
        mixed = i < 2 * (micro - ahead)
        is_fwd = (q < ahead) | (mixed & (lax.rem(i, 2) == 1))

        @pl.when(is_fwd)
        def _():
            forward(jnp.where(q < ahead, q, ahead + i // 2), c)

        @pl.when(jnp.logical_not(is_fwd))
        def _():
            backward(jnp.where(mixed, i // 2, i - (micro - ahead)), parts - 1 - c)

    high, broad = TILE
    down_n, across = width // high, hidden // broad
    pieces = 4 * down_n * across // 2

    def place(piece):
        j = 3 - piece // (down_n * across)
        rest = lax.rem(piece, down_n * across)
        row = pl.multiple_of(lax.rem(rest, down_n) * high, high)
        col = pl.multiple_of((rest // down_n) * broad, broad)
        return j, row, col

    def partial(piece):
        j, row, col = place(piece)
        source = right[j, :, pl.ds(col, broad)]
        from_down = (j == 3) | (feed & (j == 2))
        return lax.cond(
            from_down,
            lambda: dot_tn(down[:, pl.ds(row, high)], source),
            lambda: dot_tn(normed[:, pl.ds(row, high)], source),
        )

    def sib_copy(t):
        return remote(sib_out.at[t], sib_in.at[t], tail_sem.at[0, t], tail_sem.at[1, t], section, sibling)

    def up_copy(t):
        return remote(up_out.at[t], up_in.at[t], tail_sem.at[2, t], tail_sem.at[3, t], section, inner)

    def mirror_copy(t):
        return remote(up_out.at[t], ret_in.at[t], tail_sem.at[2, t], tail_sem.at[4, t], section, inner)

    def ret_copy(t):
        return remote(tot_out.at[t], ret_in.at[t], tail_sem.at[5, t], tail_sem.at[4, t], section, outer)

    def share_copy(t):
        return remote(tot_out.at[t], tot_in.at[t], tail_sem.at[6, t], tail_sem.at[7, t], section, sibling)

    def store(source, t, who, k):
        j, row, col = place(2 * t + who)
        return pltpu.make_async_copy(
            source.at[t], wide_out.at[j, pl.ds(row, high), pl.ds(col, broad)], out_sem.at[k, t]
        )

    lag = jnp.minimum(2 + 6 * depth, pieces)
    most = min(2 + 6 * max(chips - half - 1, half - 1), pieces)
    back_order = order_matrix(PART, True)

    @pl.loop(0, pieces + most + 2)
    def _(t):
        @pl.when(t < pieces)
        def _():
            sib_out[t] = partial(2 * t + 1 - core).astype(BF16)
            sib_copy(t).start()
            own[lax.rem(t, 2)] = partial(2 * t + core)

        @pl.when((t >= 1) & (t <= pieces))
        def _():
            k = t - 1
            sib_copy(k).wait_recv()
            total = own[lax.rem(k, 2)] + sib_in[k].astype(F32)

            @pl.when(has_outer)
            def _():
                up_copy(k).wait_recv()
                up_out[k] = (total + up_in[k].astype(F32)).astype(BF16)

            @pl.when(jnp.logical_not(has_outer))
            def _():
                up_out[k] = total.astype(BF16)

            @pl.when(middle)
            def _():
                mirror_copy(k).start()

            @pl.when(jnp.logical_not(middle))
            def _():
                up_copy(k).start()

        @pl.when((t >= lag) & (t < pieces + lag))
        def _():
            k = t - lag
            mirror_copy(k).wait_recv()

            @pl.when(middle)
            def _():
                tot_out[k] = (up_out[k].astype(F32) + ret_in[k].astype(F32)).astype(BF16)

            @pl.when(jnp.logical_not(middle))
            def _():
                tot_out[k] = ret_in[k]

            @pl.when(has_outer)
            def _():
                ret_copy(k).start()

            share_copy(k).start()
            store(tot_out, k, core, 0).start()

        @pl.when((t >= lag + 2) & (t < pieces + lag + 2))
        def _():
            k = t - lag - 2
            share_copy(k).wait_recv()
            store(tot_in, k, 1 - core, 1).start()

        @pl.when(t == pieces // 2)
        def _():
            @pl.loop(0, parts)
            def _(c):
                span = pl.ds(pl.multiple_of(c * PART, PART), PART)

                @pl.when(section != last)
                def _():
                    fin_copy(section, c).wait_recv()

                @pl.when(section != 0)
                def _():
                    gin_copy(section, c).wait_recv()

                stage[0, span, :] = dot(back_order, fin[span, :]).astype(BF16)
                stage[1, span, :] = dot(back_order, gin[span, :]).astype(BF16)

            pltpu.make_async_copy(stage.at[0], final_out.at[0], load_sem.at[4]).start()
            pltpu.make_async_copy(stage.at[1], grad_out.at[0], load_sem.at[5]).start()

    ones = jnp.ones((16, micro * rows), BF16)
    small[0] = jnp.zeros((8, hidden), F32)
    for k in range(2):
        small[0, k : k + 1, :] = dot(ones, right[k])[0:1]
    small[0, 2:3, 0:width] = jnp.sum(gain_acc[...], axis=0, keepdims=True)

    def small_sib():
        return remote(small.at[0], small.at[1], small_sem.at[0], small_sem.at[1], section, sibling)

    def small_up(to):
        return remote(small.at[2], small.at[to], small_sem.at[2], small_sem.at[to], section, inner)

    def small_ret():
        return remote(small.at[5], small.at[4], small_sem.at[5], small_sem.at[4], section, outer)

    small_sib().start()
    small_sib().wait_recv()
    chip_sum = small[0] + small[1]

    @pl.when(has_outer)
    def _():
        small_up(3).wait_recv()
        small[2] = chip_sum + small[3]

    @pl.when(jnp.logical_not(has_outer))
    def _():
        small[2] = chip_sum

    @pl.when(middle)
    def _():
        small_up(4).start()
        small_up(4).wait_recv()
        small[5] = small[2] + small[4]

    @pl.when(jnp.logical_not(middle))
    def _():
        small_up(3).start()
        small_up(4).wait_recv()
        small[5] = small[4]

    @pl.when(has_outer)
    def _():
        small_ret().start()

    small_out[...] = small[5] * (1.0 / math.sqrt(micro * rows * batches))

    small_sib().wait_send()
    small_up(3).wait_send()

    @pl.when(has_outer)
    def _():
        small_ret().wait_send()

    @pl.when(section != 0)
    def _():
        token_copy(section).wait_send()

    @pl.when(section != last)
    def _():
        cot_copy(section).wait_send()

    @pl.loop(0, micro * parts)
    def _(step):
        m, c = step // parts, lax.rem(step, parts)

        @pl.when((section != last) | (m != section))
        def _():
            fwd_copy(m, c).wait_send()

        @pl.when((section != 0) | (m != section))
        def _():
            bwd_copy(m, c).wait_send()

    @pl.loop(0, pieces)
    def _(t):
        sib_copy(t).wait_send()
        up_copy(t).wait_send()

        @pl.when(has_outer)
        def _():
            ret_copy(t).wait_send()

        share_copy(t).wait_send()
        store(tot_out, t, core, 0).wait()
        store(tot_in, t, 1 - core, 1).wait()

    pltpu.make_async_copy(stage.at[0], final_out.at[0], load_sem.at[4]).wait()
    pltpu.make_async_copy(stage.at[1], grad_out.at[0], load_sem.at[5]).wait()


def local(tokens, cotangent, weights, biases, gains, lengths):
    micro = lengths.shape[0]
    _, rows, width = tokens.shape
    hidden = weights.shape[3]
    parts = rows // PART
    pieces = 4 * width * hidden // (TILE[0] * TILE[1]) // 2
    any_spec = pl.BlockSpec(memory_space=pl.ANY)
    vmem = pl.BlockSpec(memory_space=pltpu.VMEM)
    dma = pltpu.SemaphoreType.DMA
    relay = pltpu.VMEM((micro, rows, width), BF16)
    tiles = pltpu.VMEM((pieces, *TILE), BF16)
    final, grad, wide, small = pl.pallas_call(
        relay_kernel,
        name="relay",
        out_shape=(
            jax.ShapeDtypeStruct(tokens.shape, BF16),
            jax.ShapeDtypeStruct(tokens.shape, BF16),
            jax.ShapeDtypeStruct((4, width, hidden), BF16),
            jax.ShapeDtypeStruct((8, hidden), F32),
        ),
        in_specs=[pl.BlockSpec(memory_space=pltpu.SMEM), any_spec, any_spec, any_spec, vmem, vmem],
        out_specs=(any_spec, any_spec, any_spec, vmem),
        scratch_shapes=[
            pltpu.VMEM((4, width, hidden), BF16),
            pltpu.VMEM((4, rows, width), BF16),
            relay,
            relay,
            relay,
            relay,
            pltpu.VMEM((rows, width), BF16),
            pltpu.VMEM((rows, width), BF16),
            pltpu.VMEM((micro, rows, 128), F32),
            pltpu.VMEM((micro, rows, 128), F32),
            pltpu.VMEM((micro * rows, width), BF16),
            pltpu.VMEM((micro * rows, width), BF16),
            pltpu.VMEM((4, micro * rows, hidden), BF16),
            pltpu.VMEM((4, micro * rows, hidden), F32),
            pltpu.VMEM((8, hidden), F32),
            pltpu.VMEM((8, hidden), F32),
            pltpu.VMEM((8, width), F32),
            tiles,
            tiles,
            pltpu.VMEM((2, *TILE), F32),
            tiles,
            tiles,
            tiles,
            tiles,
            tiles,
            pltpu.VMEM((6, 8, hidden), F32),
            dma((6,)),
            dma((2 + 2 * micro,)),
            dma((micro, parts)),
            dma((micro, parts)),
            dma((micro, parts)),
            dma((micro, parts)),
            dma((parts,)),
            dma((parts,)),
            dma((8, pieces)),
            dma((6,)),
            dma((2, pieces)),
        ],
        compiler_params=pltpu.CompilerParams(
            collective_id=0, has_side_effects=True, vmem_limit_bytes=60 * 2**20
        ),
    )(lengths, tokens, cotangent, weights, biases, gains)
    scale = 1.0 / math.sqrt(micro * rows * lax.axis_size("batch"))
    return (
        final,
        grad,
        (wide.astype(F32) * scale)[None],
        small[None, 0:2],
        small[2:3, 0:width],
    )


def solution(mesh):
    row = P("section", "batch", None)
    placed = (
        row,
        row,
        P("section", None, None, None),
        P("section", None, None),
        P("section", None),
        P(None, "batch"),
    )
    return jax.shard_map(
        local,
        mesh=mesh,
        in_specs=placed,
        out_specs=(row, row, *placed[2:5]),
        check_vma=False,
    )
```

```python
import functools
import math

import jax
import jax.numpy as jnp
from jax import lax
from jax.experimental import pallas as pl
from jax.experimental.pallas import tpu as pltpu
from jax.sharding import PartitionSpec as P

MESH = pl.DeviceIdType.MESH
EPS = 1e-05
PART = 64
CUTS = 4
SENDS = 4
LANES = 256
TILE = (128, 256)
F32 = jnp.float32
BF16 = jnp.bfloat16


def dot(a, b):
    return jnp.dot(a, b, preferred_element_type=F32)


def dot_tn(a, b):
    return lax.dot_general(a, b, (((0,), (0,)), ((), ())), preferred_element_type=F32)


def order_matrix(rows, back):
    new = lax.broadcasted_iota(jnp.int32, (rows, rows), 1 if back else 0)
    old = lax.broadcasted_iota(jnp.int32, (rows, rows), 0 if back else 1)
    hit = (lax.rem(new, 8) * (rows // 8) + new // 8) == old
    return jnp.where(hit, 1.0, 0.0).astype(BF16)


def groups(value):
    return [value[8 * g : 8 * g + 8] for g in range(value.shape[0] // 8)]


def chain(gain, add, carry, back):
    row = lax.broadcasted_iota(jnp.int32, gain.shape, 0)
    for step in (1, 2, 4):
        shift = 8 - step if back else step
        inside = (row < 8 - step) if back else (row >= step)
        add = jnp.where(inside, gain * pltpu.roll(add, shift, 0) + add, add)
        gain = jnp.where(inside, gain * pltpu.roll(gain, shift, 0), gain)
    whole = gain * carry + add
    edge = 7 if back else 0
    enter = jnp.where(row == edge, carry, pltpu.roll(whole, 7 if back else 1, 0))
    last = whole[0:1] if back else whole[7:8]
    return enter, jnp.broadcast_to(last, gain.shape)


def furthest(chips, pieces):
    return min(3 + 7 * (chips - chips // 2 - 1), pieces)


def relay_kernel(
    lengths,
    tokens,
    cotangent,
    weights,
    biases,
    gains,
    final_out,
    grad_out,
    wide_out,
    small_out,
    w,
    wt,
    bias,
    gain,
    stage,
    x_in,
    do_in,
    x_out,
    dx_out,
    valid_s,
    keep_s,
    normed,
    down,
    right,
    coef,
    h_carry,
    e_carry,
    gain_acc,
    bias_acc,
    sib_out,
    sib_in,
    own,
    up_out,
    up_in,
    ret_in,
    tot_out,
    tot_in,
    small,
    load_sem,
    tok_sem,
    fwd_send,
    fwd_recv,
    bwd_send,
    bwd_recv,
    home_sem,
    near_sem,
    far_sem,
    small_sem,
):
    micro, rows, width = x_in.shape
    parts = rows // PART
    hidden = w.shape[2]
    section, batch = lax.axis_index("section"), lax.axis_index("batch")
    sections, batches = lax.axis_size("section"), lax.axis_size("batch")
    last = sections - 1
    mixer = lax.rem(section, 2) == 0
    feed = lax.rem(section, 2) == 1
    chips = batches // 2
    chip, core = batch // 2, lax.rem(batch, 2)
    sibling = batch + 1 - 2 * core
    half = chips // 2
    low_side = chip < half
    step_in = jnp.where(low_side, 2, -2)
    inner = batch + step_in
    outer = batch - step_in
    middle = (chip == half - 1) | (chip == half)
    has_outer = (chip > 0) & (chip < chips - 1)
    depth = jnp.where(low_side, half - 1 - chip, chip - half)

    def remote(src, dst, send, recv, to_section, to_batch):
        return pltpu.make_async_remote_copy(
            src_ref=src,
            dst_ref=dst,
            send_sem=send,
            recv_sem=recv,
            device_id=(to_section, to_batch),
            device_id_type=MESH,
        )

    sources = [
        (tokens.at[0], stage.at[0]),
        (cotangent.at[0], stage.at[1]),
        (biases.at[0], bias),
        (gains, gain),
        *[(weights.at[0, j], w.at[j]) for j in (3, 0, 1, 2)],
    ]
    loads = [pltpu.make_async_copy(src, dst, load_sem.at[i]) for i, (src, dst) in enumerate(sources)]
    for copy in loads:
        copy.start()

    barrier = pltpu.get_barrier_semaphore()
    for other in range(1, sections):
        pl.semaphore_signal(
            barrier, inc=1, device_id=(lax.rem(section + other, sections), batch), device_id_type=MESH
        )
    pl.semaphore_signal(barrier, inc=1, device_id=(section, sibling), device_id_type=MESH)
    pl.semaphore_signal(barrier, inc=1, device_id=(section, inner), device_id_type=MESH)

    @pl.when(has_outer)
    def _():
        pl.semaphore_signal(barrier, inc=1, device_id=(section, outer), device_id_type=MESH)

    spot = lax.broadcasted_iota(jnp.int32, (rows, 128), 0)
    spot_in = lax.rem(spot, PART)
    spot = spot - spot_in + lax.rem(spot_in, 8) * (PART // 8) + spot_in // 8
    for m in range(micro):
        end = jnp.zeros((1, 1), jnp.int32)
        start_hit = jnp.zeros((rows, 128), F32)
        for k in range(lengths.shape[1]):
            start_hit = jnp.where(spot == end, 1.0, start_hit)
            end = end + lengths[m : m + 1, k : k + 1]
        valid = jnp.where(spot < end, 1.0, 0.0)
        valid_s[m] = valid
        keep_s[m] = valid * (1.0 - start_hit)
    h_carry[...] = jnp.zeros_like(h_carry)
    e_carry[...] = jnp.zeros_like(e_carry)
    gain_acc[...] = jnp.zeros_like(gain_acc)
    bias_acc[...] = jnp.zeros_like(bias_acc)

    perm = order_matrix(PART, False)
    loads[0].wait()
    for c in range(parts):
        span = pl.ds(c * PART, PART)
        ordered = dot(perm, stage[0, span, :]).astype(BF16)
        stage[2, span, :] = ordered

        @pl.when(section == 0)
        def _():
            x_in[0, span, :] = ordered

    loads[1].wait()
    for c in range(parts):
        span = pl.ds(c * PART, PART)
        ordered = dot(perm, stage[1, span, :]).astype(BF16)
        stage[3, span, :] = ordered

        @pl.when(section == last)
        def _():
            do_in[last, span, :] = ordered

    pl.semaphore_wait(barrier, sections + 1 + jnp.where(has_outer, 1, 0))

    def token_copy(m):
        return remote(stage.at[2], x_in.at[m], tok_sem.at[0], tok_sem.at[2 + m], 0, batch)

    def cot_copy(m):
        return remote(stage.at[3], do_in.at[m], tok_sem.at[1], tok_sem.at[2 + micro + m], last, batch)

    @pl.when(section != 0)
    def _():
        token_copy(section).start()

    @pl.when(section != last)
    def _():
        cot_copy(section).start()

    for copy in loads[2:]:
        copy.wait()

    wt[3] = w[3].T

    def flip():
        for j in range(3):
            wt[j] = w[j].T

    pl.when(section > 0)(flip)

    def wide(mask):
        return jnp.concatenate([mask] * (width // 128), axis=1)

    def slab(mask):
        return jnp.concatenate([mask] * (LANES // 128), axis=1)

    def fwd_copy(m, c):
        span = pl.ds(pl.multiple_of(c * PART, PART), PART)
        return remote(
            x_out.at[m, span],
            x_in.at[m, span],
            fwd_send.at[lax.rem(c, SENDS)],
            fwd_recv.at[m, c],
            jnp.minimum(section + 1, last),
            batch,
        )

    def bwd_copy(m, c):
        span = pl.ds(pl.multiple_of(c * PART, PART), PART)
        return remote(
            dx_out.at[m, span],
            do_in.at[m, span],
            bwd_send.at[lax.rem(c, SENDS)],
            bwd_recv.at[m, c],
            jnp.maximum(section - 1, 0),
            batch,
        )

    def home_copy(source, result, k, m):
        return remote(source.at[m], result.at[0], home_sem.at[k, m], home_sem.at[k, micro], m, batch)

    def keep_copy(source, result, k, m):
        return pltpu.make_async_copy(source.at[m], result.at[0], home_sem.at[k, m])

    def forward(m, c):
        span = pl.ds(pl.multiple_of(c * PART, PART), PART)
        line = pl.ds(pl.multiple_of(m * rows + c * PART, PART), PART)

        @pl.when(section > 0)
        def _():
            fwd_copy(m, c).wait_recv()

        @pl.when((section == 0) & (c == 0) & (m > 0))
        def _():
            token_copy(m).wait_recv()

        x = x_in[m, span, :].astype(F32)
        valid = valid_s[m, span, :]
        scale = lax.rsqrt(jnp.mean(x * x, axis=-1, keepdims=True) + EPS)
        nb = (x * scale * gain[...]).astype(BF16)
        normed[line, :] = nb

        @pl.when(mixer)
        def _():
            keep_l = slab(keep_s[m, span, :])
            valid_l = slab(valid)
            for blk in range(hidden // LANES):
                cols = slice(blk * LANES, (blk + 1) * LANES)
                zf = dot(nb, w[0, :, cols]) + bias[0:1, cols]
                zi = dot(nb, w[1, :, cols]) + bias[1:2, cols]
                zh = dot(nb, w[2, :, cols])
                low = jnp.minimum(jnp.minimum(zf, zi), 0.0)
                e0 = jnp.exp(low)
                ei, ef = jnp.exp(low - zi), jnp.exp(low - zf)
                top, bot = e0 + ei, e0 + ef
                inv = 1.0 / (top + bot)
                decay = top * inv
                admit = bot * inv
                a = keep_l * decay
                iv = valid_l * admit
                b = iv * zh
                a_g, b_g = groups(a), groups(b)
                state, product = b_g[0], a_g[0]
                states, products = [state], [product]
                for g in range(1, len(a_g)):
                    state = a_g[g] * state + b_g[g]
                    product = a_g[g] * product
                    states.append(state)
                    products.append(product)
                enter, leave = chain(product, state, h_carry[:, cols], False)
                h_carry[:, cols] = leave
                hs = [s + p * enter for s, p in zip(states, products)]
                h_prev = jnp.concatenate([enter] + hs[:-1], axis=0)
                right[3, line, cols] = jnp.concatenate(hs, axis=0).astype(BF16)
                turn = (keep_l * h_prev - valid_l * zh) * inv
                coef[0, line, cols] = a
                coef[1, line, cols] = decay * ef * turn
                coef[2, line, cols] = -admit * ei * turn
                coef[3, line, cols] = iv
            y = dot(right[3, line, :], wt[3])
            x_out[m, span, :] = (x + wide(valid) * y).astype(BF16)

        @pl.when(feed)
        def _():
            for k in range(2):
                for blk in range(hidden // LANES):
                    cols = slice(blk * LANES, (blk + 1) * LANES)
                    u = dot(nb, w[k, :, cols]) + bias[k : k + 1, cols]
                    phi = 0.5 + 0.5 * lax.erf(u * math.sqrt(0.5))
                    right[2 + k, line, cols] = (u * phi).astype(BF16)
                    coef[k, line, cols] = phi + u * jnp.exp(-0.5 * u * u) * (1.0 / math.sqrt(2.0 * math.pi))
            y = dot(right[2, line, :], wt[2]) + dot(right[3, line, :], wt[3])
            x_out[m, span, :] = (x + wide(valid) * y).astype(BF16)

        @pl.when(section < last)
        def _():
            @pl.when(m * parts + c >= SENDS)
            def _():
                fwd_copy(m, c).wait_send()

            fwd_copy(m, c).start()

        @pl.when(section == last)
        def _():
            x_out[m, span, :] = (x_out[m, span, :].astype(F32) * wide(valid)).astype(BF16)

    def backward(m, c):
        span = pl.ds(pl.multiple_of(c * PART, PART), PART)
        line = pl.ds(pl.multiple_of(m * rows + c * PART, PART), PART)

        @pl.when(section < last)
        def _():
            bwd_copy(m, c).wait_recv()

        @pl.when((section == last) & (c == parts - 1) & (m != last))
        def _():
            cot_copy(m).wait_recv()

        do = do_in[m, span, :].astype(F32) * wide(valid_s[m, span, :])
        dy = do.astype(BF16)
        down[line, :] = dy

        @pl.when(mixer)
        def _():
            for blk in range(hidden // LANES):
                cols = slice(blk * LANES, (blk + 1) * LANES)
                d_g = groups(dot(dy, w[3, :, cols]))
                a_g = groups(coef[0, line, cols])
                count = len(a_g)
                dhs, spread = [None] * count, [None] * count
                dhs[-1] = d_g[-1]
                for g in range(count - 2, -1, -1):
                    dhs[g] = d_g[g] + a_g[g + 1] * dhs[g + 1]
                    spread[g] = a_g[g + 1] if g == count - 2 else a_g[g + 1] * spread[g + 1]
                enter, leave = chain(a_g[0] * spread[0], a_g[0] * dhs[0], e_carry[:, cols], True)
                e_carry[:, cols] = leave
                dhs = [d + s * enter for d, s in zip(dhs[:-1], spread[:-1])] + [dhs[-1] + enter]
                dh = jnp.concatenate(dhs, axis=0)
                for j in range(3):
                    dz = dh * coef[1 + j, line, cols]
                    right[j, line, cols] = dz.astype(BF16)
                    if j < 2:
                        bias_acc[j, :, cols] += sum(groups(dz))

        @pl.when(feed)
        def _():
            for k in range(2):
                for blk in range(hidden // LANES):
                    cols = slice(blk * LANES, (blk + 1) * LANES)
                    du = dot(dy, w[2 + k, :, cols]) * coef[k, line, cols]
                    right[k, line, cols] = du.astype(BF16)
                    bias_acc[k, :, cols] += sum(groups(du))

        def finish(dn):
            x = x_in[m, span, :].astype(F32)
            scale = lax.rsqrt(jnp.mean(x * x, axis=-1, keepdims=True) + EPS)
            xr = x * scale
            part = dn * xr
            gain_acc[...] += sum(groups(part))
            dng = dn * gain[...]
            mean = jnp.mean(dng * xr, axis=-1, keepdims=True)
            dx_out[m, span, :] = (do + scale * (dng - xr * mean)).astype(BF16)

        @pl.when(mixer)
        def _():
            finish(
                dot(right[0, line, :], wt[0])
                + dot(right[1, line, :], wt[1])
                + dot(right[2, line, :], wt[2])
            )

        @pl.when(feed)
        def _():
            finish(dot(right[0, line, :], wt[0]) + dot(right[1, line, :], wt[1]))

        @pl.when(section > 0)
        def _():
            @pl.when(m * parts + parts - 1 - c >= SENDS)
            def _():
                bwd_copy(m, c).wait_send()

            bwd_copy(m, c).start()

    ahead = jnp.where(section == last, 1, micro)

    @pl.loop(0, 2 * micro * parts)
    def _(step):
        q = step // parts
        c = lax.rem(step, parts)
        i = jnp.maximum(q - ahead, 0)
        mixed = i < 2 * (micro - ahead)
        is_fwd = (q < ahead) | (mixed & (lax.rem(i, 2) == 1))

        pl.when((section == 0) & (step == parts))(flip)

        @pl.when(is_fwd)
        def _():
            forward(jnp.where(q < ahead, q, ahead + i // 2), c)

        @pl.when(jnp.logical_not(is_fwd))
        def _():
            backward(jnp.where(mixed, i // 2, i - (micro - ahead)), parts - 1 - c)

    def homeward(act):
        for m in range(micro):
            for k, source, result, at in ((0, x_out, final_out, last), (1, dx_out, grad_out, 0)):

                @pl.when((section == at) & (section != m))
                def _():
                    act(home_copy(source, result, k, m), True)

                @pl.when((section == at) & (section == m))
                def _():
                    act(keep_copy(source, result, k, m), False)

    homeward(lambda copy, far: copy.start())

    high, broad = TILE
    down_n, across = width // high, hidden // broad
    pieces = 4 * down_n * across // 2
    near, far = sib_in.shape[0], up_in.shape[0]

    def place(piece):
        j = 3 - piece // (down_n * across)
        rest = lax.rem(piece, down_n * across)
        row = pl.multiple_of(lax.rem(rest, down_n) * high, high)
        col = pl.multiple_of((rest // down_n) * broad, broad)
        return j, row, col

    def partial(piece):
        j, row, col = place(piece)
        source = right[j, :, pl.ds(col, broad)]
        from_down = (j == 3) | (feed & (j == 2))
        return lax.cond(
            from_down,
            lambda: dot_tn(down[:, pl.ds(row, high)], source),
            lambda: dot_tn(normed[:, pl.ds(row, high)], source),
        )

    def sib_copy(t):
        k = lax.rem(t, near)
        return remote(sib_out.at[k], sib_in.at[k], near_sem.at[0, k], near_sem.at[1, k], section, sibling)

    def up_copy(t):
        k = lax.rem(t, far)
        return remote(up_out.at[k], up_in.at[k], far_sem.at[0, k], far_sem.at[1, k], section, inner)

    def mirror_copy(t):
        k = lax.rem(t, far)
        return remote(up_out.at[k], ret_in.at[k], far_sem.at[0, k], far_sem.at[2, k], section, inner)

    def ret_copy(t):
        k = lax.rem(t, far)
        return remote(tot_out.at[k], ret_in.at[k], far_sem.at[3, k], far_sem.at[2, k], section, outer)

    def share_copy(t):
        k = lax.rem(t, far)
        return remote(
            tot_out.at[k], tot_in.at[lax.rem(t, near)], far_sem.at[4, k], near_sem.at[2, lax.rem(t, near)], section, sibling
        )

    def store_own(t):
        j, row, col = place(2 * t + core)
        k = lax.rem(t, far)
        return pltpu.make_async_copy(
            tot_out.at[k], wide_out.at[j, pl.ds(row, high), pl.ds(col, broad)], far_sem.at[5, k]
        )

    def store_other(t):
        j, row, col = place(2 * t + 1 - core)
        k = lax.rem(t, near)
        return pltpu.make_async_copy(
            tot_in.at[k], wide_out.at[j, pl.ds(row, high), pl.ds(col, broad)], near_sem.at[3, k]
        )

    lag = jnp.minimum(3 + 7 * depth, pieces)
    most = furthest(chips, pieces)
    small_at = 2 + 4 * (half - 1 - depth)
    small_back = 2 + 4 * half + 4 * depth

    for k in range(2):
        small[0, k : k + 1, :] = jnp.sum(bias_acc[k], axis=0, keepdims=True)
    small[0, 2:3, 0:width] = jnp.sum(gain_acc[...], axis=0, keepdims=True)
    small[0, 2:3, width:] = jnp.zeros((1, hidden - width), F32)
    small[0, 3:8, :] = jnp.zeros((5, hidden), F32)

    def small_sib():
        return remote(small.at[0], small.at[1], small_sem.at[0], small_sem.at[1], section, sibling)

    def small_up(to):
        return remote(small.at[2], small.at[to], small_sem.at[2], small_sem.at[to], section, inner)

    def small_ret():
        return remote(small.at[5], small.at[4], small_sem.at[5], small_sem.at[4], section, outer)

    def small_step(t):
        @pl.when(t == 0)
        def _():
            small_sib().start()

        @pl.when(t == small_at)
        def _():
            small_sib().wait_recv()
            small[2] = small[0] + small[1]

            @pl.when(has_outer)
            def _():
                small_up(3).wait_recv()
                small[2] = small[2] + small[3]

            @pl.when(middle)
            def _():
                small_up(4).start()

            @pl.when(jnp.logical_not(middle))
            def _():
                small_up(3).start()

        @pl.when(t == small_back)
        def _():
            small_up(4).wait_recv()

            @pl.when(middle)
            def _():
                small[5] = small[2] + small[4]

            @pl.when(jnp.logical_not(middle))
            def _():
                small[5] = small[4]

            @pl.when(has_outer)
            def _():
                small_ret().start()

    @pl.loop(0, max(pieces + most + 4, 3 + 8 * half))
    def _(t):
        @pl.when(t < pieces)
        def _():
            @pl.when(t >= near)
            def _():
                sib_copy(t).wait_send()

            sib_out[lax.rem(t, near)] = partial(2 * t + 1 - core).astype(BF16)
            sib_copy(t).start()
            own[lax.rem(t, 2)] = partial(2 * t + core)

        @pl.when((t >= 1) & (t <= pieces))
        def _():
            k = t - 1
            slot = lax.rem(k, far)

            @pl.when(k >= far)
            def _():
                up_copy(k).wait_send()

            sib_copy(k).wait_recv()
            total = own[lax.rem(k, 2)] + sib_in[lax.rem(k, near)].astype(F32)

            @pl.when(has_outer)
            def _():
                up_copy(k).wait_recv()
                up_out[slot] = (total + up_in[slot].astype(F32)).astype(BF16)

            @pl.when(jnp.logical_not(has_outer))
            def _():
                up_out[slot] = total.astype(BF16)

            @pl.when(middle)
            def _():
                mirror_copy(k).start()

            @pl.when(jnp.logical_not(middle))
            def _():
                up_copy(k).start()

        @pl.when((t >= lag) & (t < pieces + lag))
        def _():
            k = t - lag
            slot = lax.rem(k, far)

            @pl.when(k >= far)
            def _():
                share_copy(k).wait_send()
                store_own(k).wait()

                @pl.when(has_outer)
                def _():
                    ret_copy(k).wait_send()

            mirror_copy(k).wait_recv()

            @pl.when(middle)
            def _():
                tot_out[slot] = (up_out[slot].astype(F32) + ret_in[slot].astype(F32)).astype(BF16)

            @pl.when(jnp.logical_not(middle))
            def _():
                tot_out[slot] = ret_in[slot]

            @pl.when(has_outer)
            def _():
                ret_copy(k).start()

            share_copy(k).start()
            store_own(k).start()

        @pl.when((t >= lag + 2) & (t < pieces + lag + 2))
        def _():
            k = t - lag - 2
            share_copy(k).wait_recv()
            store_other(k).start()

        @pl.when((t >= lag + 4) & (t < pieces + lag + 4))
        def _():
            store_other(t - lag - 4).wait()

        small_step(t)

    small_out[...] = small[5] * (1.0 / math.sqrt(micro * rows * batches))

    small_sib().wait_send()
    small_up(3).wait_send()

    @pl.when(has_outer)
    def _():
        small_ret().wait_send()

    @pl.when(section != 0)
    def _():
        token_copy(section).wait_send()

    @pl.when(section != last)
    def _():
        cot_copy(section).wait_send()

    for c in range(SENDS):

        @pl.when(section != last)
        def _():
            fwd_copy(0, c).wait_send()

        @pl.when(section != 0)
        def _():
            bwd_copy(0, c).wait_send()

    for k in range(near):
        sib_copy(k).wait_send()

    for k in range(far):
        up_copy(k).wait_send()
        share_copy(k).wait_send()
        store_own(k).wait()

        @pl.when(has_outer)
        def _():
            ret_copy(k).wait_send()

    homeward(lambda copy, far: copy.wait_send() if far else copy.wait())

    @pl.when(section != last)
    def _():
        home_copy(x_out, final_out, 0, section).wait_recv()

    @pl.when(section != 0)
    def _():
        home_copy(dx_out, grad_out, 1, section).wait_recv()


def finish_kernel(scale, wide, small, final_in, grad_in, final, grad, weight, bias, gain, narrow, full, sem):
    blocks, depth = wide.shape[0], wide.shape[1] // CUTS
    loads, stores = [], []
    for n in range(blocks * CUTS):
        j, span = n // CUTS, pl.ds((n % CUTS) * depth, depth)
        loads.append(pltpu.make_async_copy(wide.at[j, span], narrow.at[j, span], sem.at[0, n]))
        stores.append(pltpu.make_async_copy(full.at[j, span], weight.at[0, j, span], sem.at[1, n]))
    for copy in loads:
        copy.start()
    for n, (load, store) in enumerate(zip(loads, stores)):
        j, span = n // CUTS, pl.ds((n % CUTS) * depth, depth)
        load.wait()
        full[j, span, :] = narrow[j, span, :].astype(F32) * scale
        store.start()
    order = order_matrix(PART, True)
    for c in range(final.shape[1] // PART):
        span = slice(c * PART, (c + 1) * PART)
        final[0, span, :] = dot(order, final_in[0, span, :]).astype(BF16)
        grad[0, span, :] = dot(order, grad_in[0, span, :]).astype(BF16)
    bias[0] = small[0:2, :]
    gain[...] = small[2:3, 0 : gain.shape[1]]
    for copy in stores:
        copy.wait()


def local(tokens, cotangent, weights, biases, gains, lengths):
    micro = lengths.shape[0]
    _, rows, width = tokens.shape
    hidden = weights.shape[3]
    parts = rows // PART
    pieces = 4 * width * hidden // (TILE[0] * TILE[1]) // 2
    any_spec = pl.BlockSpec(memory_space=pl.ANY)
    vmem = pl.BlockSpec(memory_space=pltpu.VMEM)
    dma = pltpu.SemaphoreType.DMA
    relay = pltpu.VMEM((micro, rows, width), BF16)
    near = min(8, pieces)
    far = min(furthest(lax.axis_size("batch") // 2, pieces) + 6, pieces)
    close = pltpu.VMEM((near, *TILE), BF16)
    wait = pltpu.VMEM((far, *TILE), BF16)
    final, grad, wide, small = pl.pallas_call(
        relay_kernel,
        name="relay",
        out_shape=(
            jax.ShapeDtypeStruct(tokens.shape, BF16),
            jax.ShapeDtypeStruct(tokens.shape, BF16),
            jax.ShapeDtypeStruct((4, width, hidden), BF16),
            jax.ShapeDtypeStruct((8, hidden), F32),
        ),
        in_specs=[vmem, *[any_spec] * 5],
        out_specs=(any_spec, any_spec, any_spec, vmem),
        scratch_shapes=[
            pltpu.VMEM((4, width, hidden), BF16),
            pltpu.VMEM((4, hidden, width), BF16),
            pltpu.VMEM((2, hidden), F32),
            pltpu.VMEM((1, width), F32),
            pltpu.VMEM((4, rows, width), BF16),
            relay,
            relay,
            relay,
            relay,
            pltpu.VMEM((micro, rows, 128), F32),
            pltpu.VMEM((micro, rows, 128), F32),
            pltpu.VMEM((micro * rows, width), BF16),
            pltpu.VMEM((micro * rows, width), BF16),
            pltpu.VMEM((4, micro * rows, hidden), BF16),
            pltpu.VMEM((4, micro * rows, hidden), F32),
            pltpu.VMEM((8, hidden), F32),
            pltpu.VMEM((8, hidden), F32),
            pltpu.VMEM((8, width), F32),
            pltpu.VMEM((2, 8, hidden), F32),
            close,
            close,
            pltpu.VMEM((2, *TILE), F32),
            wait,
            wait,
            wait,
            wait,
            close,
            pltpu.VMEM((6, 8, hidden), F32),
            dma((8,)),
            dma((2 + 2 * micro,)),
            dma((SENDS,)),
            dma((micro, parts)),
            dma((SENDS,)),
            dma((micro, parts)),
            dma((2, micro + 1)),
            dma((4, near)),
            dma((6, far)),
            dma((6,)),
        ],
        compiler_params=pltpu.CompilerParams(
            collective_id=0, has_side_effects=True, vmem_limit_bytes=60 * 2**20
        ),
    )(lengths, tokens, cotangent, weights, biases, gains)
    scale = 1.0 / math.sqrt(micro * rows * lax.axis_size("batch"))
    return pl.pallas_call(
        functools.partial(finish_kernel, scale),
        name="finish",
        out_shape=(
            jax.ShapeDtypeStruct(tokens.shape, BF16),
            jax.ShapeDtypeStruct(tokens.shape, BF16),
            jax.ShapeDtypeStruct(weights.shape, F32),
            jax.ShapeDtypeStruct(biases.shape, F32),
            jax.ShapeDtypeStruct(gains.shape, F32),
        ),
        in_specs=[any_spec, vmem, vmem, vmem],
        out_specs=(vmem, vmem, any_spec, vmem, vmem),
        scratch_shapes=[
            pltpu.VMEM((4, width, hidden), BF16),
            pltpu.VMEM((4, width, hidden), F32),
            dma((2, 4 * CUTS)),
        ],
        compiler_params=pltpu.CompilerParams(vmem_limit_bytes=60 * 2**20),
    )(wide, small, final, grad)


def solution(mesh):
    row = P("section", "batch", None)
    placed = (
        row,
        row,
        P("section", None, None, None),
        P("section", None, None),
        P("section", None),
        P(None, "batch"),
    )
    return jax.shard_map(
        local,
        mesh=mesh,
        in_specs=placed,
        out_specs=(row, row, *placed[2:5]),
        check_vma=False,
    )
```

```python
import functools
import math

import jax
import jax.numpy as jnp
from jax import lax
from jax.experimental import pallas as pl
from jax.experimental.pallas import tpu as pltpu
from jax.sharding import PartitionSpec as P

MESH = pl.DeviceIdType.MESH
EPS = 1e-05
PART = 64
PAIR = 2
GIVE = (10, 0)
LAG = 12
CUTS = 4
SENDS = 2
LANES = 256
TILE = (128, 256)
F32 = jnp.float32
BF16 = jnp.bfloat16


def dot(a, b):
    return jnp.dot(a, b, preferred_element_type=F32)


def over(value, count):
    return lax.shift_right_logical(value, count.bit_length() - 1)


def within(value, count):
    return lax.bitwise_and(value, count - 1)


def order_matrix(rows, back):
    new = lax.broadcasted_iota(jnp.int32, (rows, rows), 1 if back else 0)
    old = lax.broadcasted_iota(jnp.int32, (rows, rows), 0 if back else 1)
    hit = (within(new, 8) * (rows // 8) + over(new, 8)) == old
    return jnp.where(hit, 1.0, 0.0).astype(BF16)


def groups(value):
    return [value[8 * g : 8 * g + 8] for g in range(value.shape[0] // 8)]


def chain(gain, add, carry, back):
    row = lax.broadcasted_iota(jnp.int32, gain.shape, 0)
    for step in (1, 2, 4):
        shift = 8 - step if back else step
        inside = (row < 8 - step) if back else (row >= step)
        add = jnp.where(inside, gain * pltpu.roll(add, shift, 0) + add, add)
        gain = jnp.where(inside, gain * pltpu.roll(gain, shift, 0), gain)
    whole = gain * carry + add
    edge = 7 if back else 0
    enter = jnp.where(row == edge, carry, pltpu.roll(whole, 7 if back else 1, 0))
    last = whole[0:1] if back else whole[7:8]
    return enter, jnp.broadcast_to(last, gain.shape)


def relay_kernel(
    lengths,
    tokens,
    cotangent,
    weights,
    biases,
    gains,
    final_out,
    grad_out,
    wide_out,
    small_out,
    w,
    wt,
    bias,
    gain,
    stage,
    x_in,
    do_in,
    x_out,
    dx_out,
    valid_s,
    keep_s,
    normed,
    down,
    right,
    coef,
    h_carry,
    e_carry,
    gain_acc,
    bias_acc,
    sib_out,
    sib_in,
    own,
    up_out,
    up_in,
    ret_in,
    tot_out,
    tot_in,
    small,
    left,
    gift_out,
    gift_in,
    back_in,
    load_sem,
    tok_sem,
    fwd_send,
    fwd_recv,
    bwd_send,
    bwd_recv,
    home_sem,
    near_sem,
    far_sem,
    gift_sem,
    small_sem,
):
    micro, rows, width = x_in.shape
    parts = rows // PART
    hidden = w.shape[2]
    section, batch = lax.axis_index("section"), lax.axis_index("batch")
    sections, batches = lax.axis_size("section"), lax.axis_size("batch")
    last = sections - 1
    mixer = lax.rem(section, 2) == 0
    feed = lax.rem(section, 2) == 1
    chips = batches // 2
    chip, core = batch // 2, lax.rem(batch, 2)
    sibling = batch + 1 - 2 * core
    half = chips // 2
    low_side = chip < half
    step_in = jnp.where(low_side, 2, -2)
    inner = batch + step_in
    outer = batch - step_in
    middle = (chip == half - 1) | (chip == half)
    has_outer = (chip > 0) & (chip < chips - 1)
    depth = jnp.where(low_side, half - 1 - chip, chip - half)

    def remote(src, dst, send, recv, to_section, to_batch):
        return pltpu.make_async_remote_copy(
            src_ref=src,
            dst_ref=dst,
            send_sem=send,
            recv_sem=recv,
            device_id=(to_section, to_batch),
            device_id_type=MESH,
        )

    sources = [
        (tokens.at[0], stage.at[0]),
        (cotangent.at[0], stage.at[1]),
        (biases.at[0], bias),
        (gains, gain),
        *[(weights.at[0, j], w.at[j]) for j in (3, 0, 1, 2)],
    ]
    loads = [pltpu.make_async_copy(src, dst, load_sem.at[i]) for i, (src, dst) in enumerate(sources)]
    for copy in loads:
        copy.start()

    barrier = pltpu.get_barrier_semaphore()
    for other in range(1, sections):
        pl.semaphore_signal(
            barrier, inc=1, device_id=(lax.rem(section + other, sections), batch), device_id_type=MESH
        )
    pl.semaphore_signal(barrier, inc=1, device_id=(section, sibling), device_id_type=MESH)
    pl.semaphore_signal(barrier, inc=1, device_id=(section, inner), device_id_type=MESH)

    @pl.when(has_outer)
    def _():
        pl.semaphore_signal(barrier, inc=1, device_id=(section, outer), device_id_type=MESH)

    spot = lax.broadcasted_iota(jnp.int32, (rows, 128), 0)
    spot_in = within(spot, PART)
    spot = spot - spot_in + within(spot_in, 8) * (PART // 8) + over(spot_in, 8)
    for m in range(micro):
        end = jnp.zeros((1, 1), jnp.int32)
        start_hit = jnp.zeros((rows, 128), F32)
        for k in range(lengths.shape[1]):
            start_hit = jnp.where(spot == end, 1.0, start_hit)
            end = end + lengths[m : m + 1, k : k + 1]
        valid = jnp.where(spot < end, 1.0, 0.0)
        valid_s[m] = valid
        keep_s[m] = valid * (1.0 - start_hit)
    h_carry[...] = jnp.zeros_like(h_carry)
    e_carry[...] = jnp.zeros_like(e_carry)
    gain_acc[...] = jnp.zeros_like(gain_acc)
    bias_acc[...] = jnp.zeros_like(bias_acc)

    perm = order_matrix(PART, False)
    loads[0].wait()
    for c in range(parts):
        span = pl.ds(c * PART, PART)
        ordered = dot(perm, stage[0, span, :]).astype(BF16)
        stage[2, span, :] = ordered

        @pl.when(section == 0)
        def _():
            x_in[0, span, :] = ordered

    loads[1].wait()
    for c in range(parts):
        span = pl.ds(c * PART, PART)
        ordered = dot(perm, stage[1, span, :]).astype(BF16)
        stage[3, span, :] = ordered

        @pl.when(section == last)
        def _():
            do_in[last, span, :] = ordered

    pl.semaphore_wait(barrier, sections + 1 + jnp.where(has_outer, 1, 0))

    def token_copy(m):
        return remote(stage.at[2], x_in.at[m], tok_sem.at[0], tok_sem.at[2 + m], 0, batch)

    def cot_copy(m):
        return remote(stage.at[3], do_in.at[m], tok_sem.at[1], tok_sem.at[2 + micro + m], last, batch)

    def side_copy():
        return remote(stage.at[3], stage.at[4], tok_sem.at[1], tok_sem.at[2 + 2 * micro], last - 1, batch)

    def side_last():
        return remote(stage.at[4], do_in.at[0], tok_sem.at[2 + 2 * micro + 1], tok_sem.at[2 + micro], last, batch)

    @pl.when(section != 0)
    def _():
        token_copy(section).start()

    pl.when(section == 0)(lambda: side_copy().start())

    @pl.when((section != last) & (section != 0))
    def _():
        cot_copy(section).start()

    for copy in loads[2:]:
        copy.wait()

    wt[3] = w[3].T

    def flip():
        for j in range(3):
            wt[j] = w[j].T

    pl.when(section > 0)(flip)

    @pl.when(section == last - 1)
    def _():
        side_copy().wait_recv()
        side_last().start()

    def wide(mask):
        return jnp.concatenate([mask] * (width // 128), axis=1)

    def slab(mask):
        return jnp.concatenate([mask] * (LANES // 128), axis=1)

    def fwd_copy(m, c):
        span = pl.ds(pl.multiple_of(c * PART, PART), PART)
        return remote(
            x_out.at[m, span],
            x_in.at[m, span],
            fwd_send.at[within(c, SENDS)],
            fwd_recv.at[m, c],
            jnp.minimum(section + 1, last),
            batch,
        )

    def bwd_copy(m, c):
        span = pl.ds(pl.multiple_of(c * PAIR * PART, PAIR * PART), PAIR * PART)
        return remote(
            dx_out.at[m, span],
            do_in.at[m, span],
            bwd_send.at[within(c, SENDS)],
            bwd_recv.at[m, c],
            jnp.maximum(section - 1, 0),
            batch,
        )

    def home_copy(source, result, k, m):
        return remote(source.at[m], result.at[0], home_sem.at[k, m], home_sem.at[k, micro], m, batch)

    def keep_copy(source, result, k, m):
        return pltpu.make_async_copy(source.at[m], result.at[0], home_sem.at[k, m])

    def forward(m, c, count):
        size = count * PART
        span = pl.ds(pl.multiple_of(c * size, size), size)
        line = pl.ds(pl.multiple_of(m * rows + c * size, size), size)

        @pl.when(section > 0)
        def _():
            for k in range(count):
                fwd_copy(m, c * count + k).wait_recv()

        @pl.when((section == 0) & (c == 0) & (m > 0))
        def _():
            token_copy(m).wait_recv()

        x = x_in[m, span, :].astype(F32)
        valid = valid_s[m, span, :]
        scale = lax.rsqrt(jnp.mean(x * x, axis=-1, keepdims=True) + EPS)
        nb = (x * scale * gain[...]).astype(BF16)
        normed[line, :] = nb

        def mix():
            keep_l = slab(keep_s[m, span, :])
            valid_l = slab(valid)
            for blk in range(hidden // LANES):
                cols = slice(blk * LANES, (blk + 1) * LANES)
                zf = dot(nb, w[0, :, cols]) + bias[0:1, cols]
                zi = dot(nb, w[1, :, cols]) + bias[1:2, cols]
                zh = dot(nb, w[2, :, cols])
                low = jnp.minimum(jnp.minimum(zf, zi), 0.0)
                e0 = jnp.exp(low)
                ei, ef = jnp.exp(low - zi), jnp.exp(low - zf)
                top, bot = e0 + ei, e0 + ef
                inv = 1.0 / (top + bot)
                decay = top * inv
                admit = bot * inv
                a = keep_l * decay
                iv = valid_l * admit
                b = iv * zh
                a_g, b_g = groups(a), groups(b)
                state, product = b_g[0], a_g[0]
                states, products = [state], [product]
                for g in range(1, len(a_g)):
                    state = a_g[g] * state + b_g[g]
                    product = a_g[g] * product
                    states.append(state)
                    products.append(product)
                enter, leave = chain(product, state, h_carry[:, cols], False)
                h_carry[:, cols] = leave
                hs = [s + p * enter for s, p in zip(states, products)]
                h_prev = jnp.concatenate([enter] + hs[:-1], axis=0)
                right[3, line, cols] = jnp.concatenate(hs, axis=0).astype(BF16)
                turn = (keep_l * h_prev - valid_l * zh) * inv
                coef[0, line, cols] = a
                coef[1, line, cols] = decay * ef * turn
                coef[2, line, cols] = -admit * ei * turn
                coef[3, line, cols] = iv
            y = dot(right[3, line, :], wt[3])
            x_out[m, span, :] = (x + wide(valid) * y).astype(BF16)

        def feed_on():
            for k in range(2):
                for blk in range(hidden // LANES):
                    cols = slice(blk * LANES, (blk + 1) * LANES)
                    u = dot(nb, w[k, :, cols]) + bias[k : k + 1, cols]
                    phi = 0.5 + 0.5 * lax.erf(u * math.sqrt(0.5))
                    right[2 + k, line, cols] = (u * phi).astype(BF16)
                    coef[k, line, cols] = phi + u * jnp.exp(-0.5 * u * u) * (1.0 / math.sqrt(2.0 * math.pi))
            y = dot(right[2, line, :], wt[2]) + dot(right[3, line, :], wt[3])
            x_out[m, span, :] = (x + wide(valid) * y).astype(BF16)

        if count == 1:
            pl.when(mixer)(mix)
            pl.when(feed)(feed_on)

            @pl.when(m * parts + c >= SENDS)
            def _():
                fwd_copy(m, c).wait_send()

            fwd_copy(m, c).start()
        else:
            feed_on()
            x_out[m, span, :] = (x_out[m, span, :].astype(F32) * wide(valid)).astype(BF16)

    def backward(m, c):
        size = PAIR * PART
        span = pl.ds(pl.multiple_of(c * size, size), size)
        line = pl.ds(pl.multiple_of(m * rows + c * size, size), size)

        @pl.when(section < last)
        def _():
            bwd_copy(m, c).wait_recv()

        @pl.when((section == last) & (c == 0) & (m != last))
        def _():
            cot_copy(m).wait_recv()

        do = do_in[m, span, :].astype(F32) * wide(valid_s[m, span, :])
        dy = do.astype(BF16)
        down[line, :] = dy

        @pl.when(mixer)
        def _():
            for blk in range(hidden // LANES):
                cols = slice(blk * LANES, (blk + 1) * LANES)
                d_all, a_all = dot(dy, w[3, :, cols]), coef[0, line, cols]
                pieces_dh = []
                for part in range(PAIR - 1, -1, -1):
                    spot = slice(part * PART, (part + 1) * PART)
                    d_g, a_g = groups(d_all[spot]), groups(a_all[spot])
                    count = len(a_g)
                    dhs, spread = [None] * count, [None] * count
                    dhs[-1] = d_g[-1]
                    for g in range(count - 2, -1, -1):
                        dhs[g] = d_g[g] + a_g[g + 1] * dhs[g + 1]
                        spread[g] = a_g[g + 1] if g == count - 2 else a_g[g + 1] * spread[g + 1]
                    enter, leave = chain(a_g[0] * spread[0], a_g[0] * dhs[0], e_carry[:, cols], True)
                    e_carry[:, cols] = leave
                    dhs = [d + s * enter for d, s in zip(dhs[:-1], spread[:-1])] + [dhs[-1] + enter]
                    pieces_dh = dhs + pieces_dh
                dh = jnp.concatenate(pieces_dh, axis=0)
                for j in range(3):
                    dz = dh * coef[1 + j, line, cols]
                    right[j, line, cols] = dz.astype(BF16)
                    if j < 2:
                        bias_acc[j, :, cols] += sum(groups(dz))

        @pl.when(feed)
        def _():
            for k in range(2):
                for blk in range(hidden // LANES):
                    cols = slice(blk * LANES, (blk + 1) * LANES)
                    du = dot(dy, w[2 + k, :, cols]) * coef[k, line, cols]
                    right[k, line, cols] = du.astype(BF16)
                    bias_acc[k, :, cols] += sum(groups(du))

        def finish(dn):
            x = x_in[m, span, :].astype(F32)
            scale = lax.rsqrt(jnp.mean(x * x, axis=-1, keepdims=True) + EPS)
            xr = x * scale
            part = dn * xr
            gain_acc[...] += sum(groups(part))
            dng = dn * gain[...]
            mean = jnp.mean(dng * xr, axis=-1, keepdims=True)
            dx_out[m, span, :] = (do + scale * (dng - xr * mean)).astype(BF16)

        @pl.when(mixer)
        def _():
            finish(
                dot(right[0, line, :], wt[0])
                + dot(right[1, line, :], wt[1])
                + dot(right[2, line, :], wt[2])
            )

        @pl.when(feed)
        def _():
            finish(dot(right[0, line, :], wt[0]) + dot(right[1, line, :], wt[1]))

        @pl.when(section > 0)
        def _():
            @pl.when((m > 0) if SENDS >= parts // PAIR else (m * (parts // PAIR) + parts // PAIR - 1 - c >= SENDS))
            def _():
                bwd_copy(m, c).wait_send()

            bwd_copy(m, c).start()

    halves = parts // PAIR

    @pl.loop(0, micro * (parts + halves))
    def _(step):
        pl.when((section == 0) & (step == parts))(flip)

        @pl.when((section < last) & (step < micro * parts))
        def _():
            forward(over(step, parts), within(step, parts), 1)

        turn = over(step, 2)
        late = step - micro * parts

        @pl.when((section == last) & (within(step, 2) == 0) & (turn < micro * halves))
        def _():
            forward(over(turn, halves), within(turn, halves), PAIR)

        @pl.when(jnp.where(section == last, (within(step, 2) == 1) & (turn < micro * halves), late >= 0))
        def _():
            q = jnp.where(section == last, turn, jnp.maximum(late, 0))
            c = within(q, halves)
            backward(over(q, halves), jnp.where(section == last, c, halves - 1 - c))

    def homeward(act):
        for m in range(micro):
            for k, source, result, at in ((0, x_out, final_out, last), (1, dx_out, grad_out, 0)):

                @pl.when((section == at) & (section != m))
                def _():
                    act(home_copy(source, result, k, m), True)

                @pl.when((section == at) & (section == m))
                def _():
                    act(keep_copy(source, result, k, m), False)

    high, broad = TILE
    down_n, across = width // high, hidden // broad
    pieces = 4 * down_n * across // 2
    near, far, gifts = sib_in.shape[0], up_in.shape[0], gift_in.shape[0]
    friend = last - section
    give = jnp.where(section == 0, GIVE[0], jnp.where(section == 1, GIVE[1], 0))
    take = jnp.where(friend == 0, GIVE[0], jnp.where(friend == 1, GIVE[1], 0))

    left[0] = normed[...].T
    left[1] = down[...].T

    def is_given(t):
        return (within(t, 2) == 1) & (over(t, 2) < give)

    def chain_index(t):
        return t - jnp.minimum(over(t, 2), give)

    def place(piece):
        j = 3 - over(piece, down_n * across)
        rest = within(piece, down_n * across)
        row = pl.multiple_of(within(rest, down_n) * high, high)
        col = pl.multiple_of(over(rest, down_n) * broad, broad)
        return j, row, col

    def partial(piece):
        j, row, col = place(piece)
        from_down = (j == 3) | (feed & (j == 2))
        return dot(left[jnp.where(from_down, 1, 0), pl.ds(row, high), :], right[j, :, pl.ds(col, broad)])

    def sib_copy(t):
        k = within(t, near)
        return remote(sib_out.at[k], sib_in.at[k], near_sem.at[0, k], near_sem.at[1, k], section, sibling)

    def gift_copy(d):
        return remote(gift_out.at[d], gift_in.at[d], gift_sem.at[0, d], gift_sem.at[1, d], friend, batch)

    def back_copy(k, d):
        return remote(tot_out.at[within(k, far)], back_in.at[d], gift_sem.at[2, d], gift_sem.at[3, d], friend, batch)

    def up_copy(k):
        k = within(k, far)
        return remote(up_out.at[k], up_in.at[k], far_sem.at[0, k], far_sem.at[1, k], section, inner)

    def mirror_copy(k):
        k = within(k, far)
        return remote(up_out.at[k], ret_in.at[k], far_sem.at[0, k], far_sem.at[2, k], section, inner)

    def ret_copy(k):
        k = within(k, far)
        return remote(tot_out.at[k], ret_in.at[k], far_sem.at[3, k], far_sem.at[2, k], section, outer)

    def share_copy(n):
        k, at = within(n, far), within(n, near)
        return remote(tot_out.at[k], tot_in.at[at], far_sem.at[4, k], near_sem.at[2, at], section, sibling)

    def store_own(n, piece):
        j, row, col = place(2 * piece + core)
        k = within(n, far)
        return pltpu.make_async_copy(
            tot_out.at[k], wide_out.at[j, pl.ds(row, high), pl.ds(col, broad)], far_sem.at[5, k]
        )

    def store_other(n, piece):
        j, row, col = place(2 * piece + 1 - core)
        k = within(n, near)
        return pltpu.make_async_copy(
            tot_in.at[k], wide_out.at[j, pl.ds(row, high), pl.ds(col, broad)], near_sem.at[3, k]
        )

    def result_at(r):
        ready = (r >= 0) & (r < pieces)
        there = ready & (r >= pieces - give)
        taken = (r >= pieces) & (r < pieces + take)
        d = r - pieces + give
        piece = jnp.where(there, 2 * d + 1, jnp.where(r < give, 2 * r, r + give))
        return ready, there, taken, d, piece

    lag = jnp.minimum(4 + 8 * depth, LAG)
    most = LAG
    small_at = 2 + 4 * (half - 1 - depth)
    small_back = 2 + 4 * half + 4 * depth

    for k in range(2):
        small[0, k : k + 1, :] = jnp.sum(bias_acc[k], axis=0, keepdims=True)
    small[0, 2:3, 0:width] = jnp.sum(gain_acc[...], axis=0, keepdims=True)
    small[0, 2:3, width:] = jnp.zeros((1, hidden - width), F32)
    small[0, 3:8, :] = jnp.zeros((5, hidden), F32)

    def small_sib():
        return remote(small.at[0], small.at[1], small_sem.at[0], small_sem.at[1], section, sibling)

    def small_up(to):
        return remote(small.at[2], small.at[to], small_sem.at[2], small_sem.at[to], section, inner)

    def small_ret():
        return remote(small.at[5], small.at[4], small_sem.at[5], small_sem.at[4], section, outer)

    def small_step(t):
        @pl.when(t == 0)
        def _():
            small_sib().start()

        @pl.when(t == small_at)
        def _():
            small_sib().wait_recv()
            small[2] = small[0] + small[1]

            @pl.when(has_outer)
            def _():
                small_up(3).wait_recv()
                small[2] = small[2] + small[3]

            @pl.when(middle)
            def _():
                small_up(4).start()

            @pl.when(jnp.logical_not(middle))
            def _():
                small_up(3).start()

        @pl.when(t == small_back)
        def _():
            small_up(4).wait_recv()

            @pl.when(middle)
            def _():
                small[5] = small[2] + small[4]

            @pl.when(jnp.logical_not(middle))
            def _():
                small[5] = small[4]

            @pl.when(has_outer)
            def _():
                small_ret().start()

    @pl.loop(0, max(pieces + gifts + most + 6, 3 + 8 * half))
    def _(t):
        @pl.when(t < pieces)
        def _():
            sib_out[within(t, near)] = partial(2 * t + 1 - core).astype(BF16)
            sib_copy(t).start()
            own[within(t, 2)] = partial(2 * t + core)

        @pl.when((t >= 1) & (t <= pieces + take))
        def _():
            s = t - 1
            k = chain_index(s)
            slot = within(k, far)

            def onward(total):
                @pl.when(has_outer)
                def _():
                    up_copy(k).wait_recv()
                    up_out[slot] = (total + up_in[slot].astype(F32)).astype(BF16)

                @pl.when(jnp.logical_not(has_outer))
                def _():
                    up_out[slot] = total.astype(BF16)

                @pl.when(middle)
                def _():
                    mirror_copy(k).start()

                @pl.when(jnp.logical_not(middle))
                def _():
                    up_copy(k).start()

            @pl.when(s < pieces)
            def _():
                sib_copy(s).wait()
                total = own[within(s, 2)] + sib_in[within(s, near)].astype(F32)

                @pl.when(is_given(s))
                def _():
                    d = over(s, 2)
                    gift_out[d] = total.astype(BF16)
                    gift_copy(d).start()

                @pl.when(jnp.logical_not(is_given(s)))
                def _():
                    onward(total)

            @pl.when(s >= pieces)
            def _():
                d = s - pieces
                gift_copy(d).wait_recv()
                onward(gift_in[d].astype(F32))

        on = jnp.logical_not(is_given(t))
        r = chain_index(t) - lag
        ready, there, taken, d, piece = result_at(r)
        slot = within(r, far)

        @pl.when(on & ((ready & jnp.logical_not(there)) | taken))
        def _():
            mirror_copy(r).wait()

            @pl.when(middle)
            def _():
                tot_out[slot] = (up_out[slot].astype(F32) + ret_in[slot].astype(F32)).astype(BF16)

            @pl.when(jnp.logical_not(middle))
            def _():
                tot_out[slot] = ret_in[slot]

            @pl.when(has_outer)
            def _():
                ret_copy(r).start()

            @pl.when(taken)
            def _():
                back_copy(r, d).start()

        @pl.when(on & there)
        def _():
            back_copy(r, d).wait_recv()
            tot_out[slot] = back_in[d]

        @pl.when(on & ready)
        def _():
            share_copy(r).start()
            store_own(r, piece).start()

        ready2, _, _, _, piece2 = result_at(r - 2)

        @pl.when(on & ready2)
        def _():
            share_copy(r - 2).wait_recv()
            store_other(r - 2, piece2).start()

        ready4, there4, taken4, d4, piece4 = result_at(r - 4)

        @pl.when(on & ready4)
        def _():
            share_copy(r - 4).wait_send()
            store_own(r - 4, piece4).wait()
            store_other(r - 4, piece4).wait()

        @pl.when(on & taken4)
        def _():
            back_copy(r - 4, d4).wait_send()

        @pl.when(on & there4)
        def _():
            gift_copy(d4).wait_send()

        @pl.when(on & ((ready4 & jnp.logical_not(there4)) | taken4) & has_outer)
        def _():
            ret_copy(r - 4).wait_send()

        pl.when(t == 2 * gifts + 2)(lambda: homeward(lambda copy, far: copy.start()))
        small_step(t)

    small_out[...] = small[5] * (1.0 / math.sqrt(micro * rows * batches))

    small_sib().wait_send()
    small_up(3).wait_send()

    @pl.when(has_outer)
    def _():
        small_ret().wait_send()

    @pl.when(section != 0)
    def _():
        token_copy(section).wait_send()

    pl.when(section == 0)(lambda: side_copy().wait_send())
    pl.when(section == last - 1)(lambda: side_last().wait_send())

    @pl.when((section != last) & (section != 0))
    def _():
        cot_copy(section).wait_send()

    for c in range(SENDS):

        @pl.when(section != last)
        def _():
            fwd_copy(0, c).wait_send()

        @pl.when(section != 0)
        def _():
            bwd_copy(0, c).wait_send()

    homeward(lambda copy, far: copy.wait_send() if far else copy.wait())

    @pl.when(section != last)
    def _():
        home_copy(x_out, final_out, 0, section).wait_recv()

    @pl.when(section != 0)
    def _():
        home_copy(dx_out, grad_out, 1, section).wait_recv()


def finish_kernel(scale, wide, small, final_in, grad_in, final, grad, weight, bias, gain, narrow, full, sem):
    blocks, depth = wide.shape[0], wide.shape[1] // CUTS
    loads, stores = [], []
    for n in range(blocks * CUTS):
        j, span = n // CUTS, pl.ds((n % CUTS) * depth, depth)
        loads.append(pltpu.make_async_copy(wide.at[j, span], narrow.at[j, span], sem.at[0, n]))
        stores.append(pltpu.make_async_copy(full.at[j, span], weight.at[0, j, span], sem.at[1, n]))
    for copy in loads:
        copy.start()
    for n, (load, store) in enumerate(zip(loads, stores)):
        j, span = n // CUTS, pl.ds((n % CUTS) * depth, depth)
        load.wait()
        full[j, span, :] = narrow[j, span, :].astype(F32) * scale
        store.start()
    order = order_matrix(PART, True)
    for c in range(final.shape[1] // PART):
        span = slice(c * PART, (c + 1) * PART)
        final[0, span, :] = dot(order, final_in[0, span, :]).astype(BF16)
        grad[0, span, :] = dot(order, grad_in[0, span, :]).astype(BF16)
    bias[0] = small[0:2, :]
    gain[...] = small[2:3, 0 : gain.shape[1]]
    for copy in stores:
        copy.wait()


def local(tokens, cotangent, weights, biases, gains, lengths):
    micro = lengths.shape[0]
    _, rows, width = tokens.shape
    hidden = weights.shape[3]
    parts = rows // PART
    pieces = 4 * width * hidden // (TILE[0] * TILE[1]) // 2
    any_spec = pl.BlockSpec(memory_space=pl.ANY)
    vmem = pl.BlockSpec(memory_space=pltpu.VMEM)
    dma = pltpu.SemaphoreType.DMA
    relay = pltpu.VMEM((micro, rows, width), BF16)
    near = min(8, pieces)
    far = 16
    close = pltpu.VMEM((near, *TILE), BF16)
    wait = pltpu.VMEM((far, *TILE), BF16)
    final, grad, wide, small = pl.pallas_call(
        relay_kernel,
        name="relay",
        out_shape=(
            jax.ShapeDtypeStruct(tokens.shape, BF16),
            jax.ShapeDtypeStruct(tokens.shape, BF16),
            jax.ShapeDtypeStruct((4, width, hidden), BF16),
            jax.ShapeDtypeStruct((8, hidden), F32),
        ),
        in_specs=[vmem, *[any_spec] * 5],
        out_specs=(any_spec, any_spec, any_spec, vmem),
        scratch_shapes=[
            pltpu.VMEM((4, width, hidden), BF16),
            pltpu.VMEM((4, hidden, width), BF16),
            pltpu.VMEM((2, hidden), F32),
            pltpu.VMEM((1, width), F32),
            pltpu.VMEM((5, rows, width), BF16),
            relay,
            relay,
            relay,
            relay,
            pltpu.VMEM((micro, rows, 128), F32),
            pltpu.VMEM((micro, rows, 128), F32),
            pltpu.VMEM((micro * rows, width), BF16),
            pltpu.VMEM((micro * rows, width), BF16),
            pltpu.VMEM((4, micro * rows, hidden), BF16),
            pltpu.VMEM((4, micro * rows, hidden), F32),
            pltpu.VMEM((8, hidden), F32),
            pltpu.VMEM((8, hidden), F32),
            pltpu.VMEM((8, width), F32),
            pltpu.VMEM((2, 8, hidden), F32),
            close,
            close,
            pltpu.VMEM((2, *TILE), F32),
            wait,
            wait,
            wait,
            wait,
            close,
            pltpu.VMEM((6, 8, hidden), F32),
            pltpu.VMEM((2, width, micro * rows), BF16),
            *[pltpu.VMEM((max(GIVE), *TILE), BF16)] * 3,
            dma((8,)),
            dma((4 + 2 * micro,)),
            dma((SENDS,)),
            dma((micro, parts)),
            dma((SENDS,)),
            dma((micro, parts // PAIR)),
            dma((2, micro + 1)),
            dma((4, near)),
            dma((6, far)),
            dma((4, max(GIVE))),
            dma((6,)),
        ],
        compiler_params=pltpu.CompilerParams(
            collective_id=0, has_side_effects=True, vmem_limit_bytes=60 * 2**20
        ),
    )(lengths, tokens, cotangent, weights, biases, gains)
    scale = 1.0 / math.sqrt(micro * rows * lax.axis_size("batch"))
    return pl.pallas_call(
        functools.partial(finish_kernel, scale),
        name="finish",
        out_shape=(
            jax.ShapeDtypeStruct(tokens.shape, BF16),
            jax.ShapeDtypeStruct(tokens.shape, BF16),
            jax.ShapeDtypeStruct(weights.shape, F32),
            jax.ShapeDtypeStruct(biases.shape, F32),
            jax.ShapeDtypeStruct(gains.shape, F32),
        ),
        in_specs=[any_spec, vmem, vmem, vmem],
        out_specs=(vmem, vmem, any_spec, vmem, vmem),
        scratch_shapes=[
            pltpu.VMEM((4, width, hidden), BF16),
            pltpu.VMEM((4, width, hidden), F32),
            dma((2, 4 * CUTS)),
        ],
        compiler_params=pltpu.CompilerParams(vmem_limit_bytes=60 * 2**20),
    )(wide, small, final, grad)


def solution(mesh):
    row = P("section", "batch", None)
    placed = (
        row,
        row,
        P("section", None, None, None),
        P("section", None, None),
        P("section", None),
        P(None, "batch"),
    )
    return jax.shard_map(
        local,
        mesh=mesh,
        in_specs=placed,
        out_specs=(row, row, *placed[2:5]),
        check_vma=False,
    )
```

```python
import functools
import math

import jax
import jax.numpy as jnp
from jax import lax
from jax.experimental import pallas as pl
from jax.experimental.pallas import tpu as pltpu
from jax.sharding import PartitionSpec as P

MESH = pl.DeviceIdType.MESH
EPS = 1e-05
PART = 64
PAIR = 2
GIVE = (10, 3)
JOIN = (24, 14)
LATE = 34
LAG = 12
CUTS = 4
SENDS = 2
LANES = 256
TILE = (128, 256)
F32 = jnp.float32
BF16 = jnp.bfloat16


def dot(a, b):
    return jnp.dot(a, b, preferred_element_type=F32)


def over(value, count):
    return lax.shift_right_logical(value, count.bit_length() - 1)


def within(value, count):
    return lax.bitwise_and(value, count - 1)


def order_matrix(rows, back):
    new = lax.broadcasted_iota(jnp.int32, (rows, rows), 1 if back else 0)
    old = lax.broadcasted_iota(jnp.int32, (rows, rows), 0 if back else 1)
    hit = (within(new, 8) * (rows // 8) + over(new, 8)) == old
    return jnp.where(hit, 1.0, 0.0).astype(BF16)


def groups(value):
    return [value[8 * g : 8 * g + 8] for g in range(value.shape[0] // 8)]


def chain(gain, add, carry, back):
    row = lax.broadcasted_iota(jnp.int32, gain.shape, 0)
    for step in (1, 2, 4):
        shift = 8 - step if back else step
        inside = (row < 8 - step) if back else (row >= step)
        add = jnp.where(inside, gain * pltpu.roll(add, shift, 0) + add, add)
        gain = jnp.where(inside, gain * pltpu.roll(gain, shift, 0), gain)
    whole = gain * carry + add
    edge = 7 if back else 0
    enter = jnp.where(row == edge, carry, pltpu.roll(whole, 7 if back else 1, 0))
    last = whole[0:1] if back else whole[7:8]
    return enter, jnp.broadcast_to(last, gain.shape)


def relay_kernel(
    lengths,
    tokens,
    cotangent,
    weights,
    biases,
    gains,
    final_out,
    grad_out,
    wide_out,
    small_out,
    w,
    wt,
    bias,
    gain,
    stage,
    x_in,
    do_in,
    x_out,
    dx_out,
    valid_s,
    keep_s,
    normed,
    down,
    right,
    coef,
    h_carry,
    e_carry,
    gain_acc,
    bias_acc,
    sib_out,
    sib_in,
    own,
    up_out,
    up_in,
    ret_in,
    tot_out,
    tot_in,
    small,
    left,
    gift_out,
    gift_in,
    back_in,
    back_sib,
    load_sem,
    tok_sem,
    fwd_send,
    fwd_recv,
    bwd_send,
    bwd_recv,
    home_sem,
    near_sem,
    far_sem,
    gift_sem,
    small_sem,
):
    micro, rows, width = x_in.shape
    parts = rows // PART
    hidden = w.shape[2]
    section, batch = lax.axis_index("section"), lax.axis_index("batch")
    sections, batches = lax.axis_size("section"), lax.axis_size("batch")
    last = sections - 1
    mixer = lax.rem(section, 2) == 0
    feed = lax.rem(section, 2) == 1
    chips = batches // 2
    chip, core = batch // 2, lax.rem(batch, 2)
    sibling = batch + 1 - 2 * core
    half = chips // 2
    low_side = chip < half
    step_in = jnp.where(low_side, 2, -2)
    inner = batch + step_in
    outer = batch - step_in
    middle = (chip == half - 1) | (chip == half)
    has_outer = (chip > 0) & (chip < chips - 1)
    depth = jnp.where(low_side, half - 1 - chip, chip - half)

    def remote(src, dst, send, recv, to_section, to_batch):
        return pltpu.make_async_remote_copy(
            src_ref=src,
            dst_ref=dst,
            send_sem=send,
            recv_sem=recv,
            device_id=(to_section, to_batch),
            device_id_type=MESH,
        )

    sources = [
        (tokens.at[0], stage.at[0]),
        (cotangent.at[0], stage.at[1]),
        (biases.at[0], bias),
        (gains, gain),
        *[(weights.at[0, j], w.at[j]) for j in (3, 0, 1, 2)],
    ]
    loads = [pltpu.make_async_copy(src, dst, load_sem.at[i]) for i, (src, dst) in enumerate(sources)]
    for copy in loads:
        copy.start()

    barrier = pltpu.get_barrier_semaphore()
    for other in range(1, sections):
        pl.semaphore_signal(
            barrier, inc=1, device_id=(lax.rem(section + other, sections), batch), device_id_type=MESH
        )
    pl.semaphore_signal(barrier, inc=1, device_id=(section, sibling), device_id_type=MESH)
    pl.semaphore_signal(barrier, inc=1, device_id=(section, inner), device_id_type=MESH)

    @pl.when(has_outer)
    def _():
        pl.semaphore_signal(barrier, inc=1, device_id=(section, outer), device_id_type=MESH)

    spot = lax.broadcasted_iota(jnp.int32, (rows, 128), 0)
    spot_in = within(spot, PART)
    spot = spot - spot_in + within(spot_in, 8) * (PART // 8) + over(spot_in, 8)
    for m in range(micro):
        end = jnp.zeros((1, 1), jnp.int32)
        start_hit = jnp.zeros((rows, 128), F32)
        for k in range(lengths.shape[0]):
            start_hit = jnp.where(spot == end, 1.0, start_hit)
            end = end + lengths[k : k + 1, m : m + 1]
        valid = jnp.where(spot < end, 1.0, 0.0)
        valid_s[m] = valid
        keep_s[m] = valid * (1.0 - start_hit)
    h_carry[...] = jnp.zeros_like(h_carry)
    e_carry[...] = jnp.zeros_like(e_carry)
    gain_acc[...] = jnp.zeros_like(gain_acc)
    bias_acc[...] = jnp.zeros_like(bias_acc)

    perm = order_matrix(PART, False)
    loads[0].wait()
    for c in range(parts):
        span = pl.ds(c * PART, PART)
        ordered = dot(perm, stage[0, span, :]).astype(BF16)
        stage[2, span, :] = ordered

        @pl.when(section == 0)
        def _():
            x_in[0, span, :] = ordered

    loads[1].wait()
    for c in range(parts):
        span = pl.ds(c * PART, PART)
        ordered = dot(perm, stage[1, span, :]).astype(BF16)
        stage[3, span, :] = ordered

        @pl.when(section == last)
        def _():
            do_in[last, span, :] = ordered

    pl.semaphore_wait(barrier, sections + 1 + jnp.where(has_outer, 1, 0))

    def token_copy(m):
        return remote(stage.at[2], x_in.at[m], tok_sem.at[0], tok_sem.at[2 + m], 0, batch)

    def cot_copy(m):
        return remote(stage.at[3], do_in.at[m], tok_sem.at[1], tok_sem.at[2 + micro + m], last, batch)

    def side_copy():
        return remote(stage.at[3], stage.at[4], tok_sem.at[1], tok_sem.at[2 + 2 * micro], last - 1, batch)

    def side_last():
        return remote(stage.at[4], do_in.at[0], tok_sem.at[2 + 2 * micro + 1], tok_sem.at[2 + micro], last, batch)

    @pl.when(section != 0)
    def _():
        token_copy(section).start()

    pl.when(section == 0)(lambda: side_copy().start())

    @pl.when((section != last) & (section != 0))
    def _():
        cot_copy(section).start()

    for copy in loads[2:]:
        copy.wait()

    wt[3] = w[3].T

    def flip():
        for j in range(3):
            wt[j] = w[j].T

    pl.when(section > 0)(flip)

    @pl.when(section == last - 1)
    def _():
        side_copy().wait_recv()
        side_last().start()

    def wide(mask):
        return jnp.concatenate([mask] * (width // 128), axis=1)

    def slab(mask):
        return jnp.concatenate([mask] * (LANES // 128), axis=1)

    def fwd_copy(m, c):
        span = pl.ds(pl.multiple_of(c * PART, PART), PART)
        return remote(
            x_out.at[m, span],
            x_in.at[m, span],
            fwd_send.at[within(c, SENDS)],
            fwd_recv.at[m, c],
            jnp.minimum(section + 1, last),
            batch,
        )

    def bwd_copy(m, c):
        span = pl.ds(pl.multiple_of(c * PAIR * PART, PAIR * PART), PAIR * PART)
        return remote(
            dx_out.at[m, span],
            do_in.at[m, span],
            bwd_send.at[within(c, SENDS)],
            bwd_recv.at[m, c],
            jnp.maximum(section - 1, 0),
            batch,
        )

    def home_copy(source, result, k, m):
        return remote(source.at[m], result.at[0], home_sem.at[k, m], home_sem.at[k, micro], m, batch)

    def keep_copy(source, result, k, m):
        return pltpu.make_async_copy(source.at[m], result.at[0], home_sem.at[k, m])

    def forward(m, c, count):
        size = count * PART
        span = pl.ds(pl.multiple_of(c * size, size), size)
        line = pl.ds(pl.multiple_of(m * rows + c * size, size), size)

        @pl.when(section > 0)
        def _():
            for k in range(count):
                fwd_copy(m, c * count + k).wait_recv()

        @pl.when((section == 0) & (c == 0) & (m > 0))
        def _():
            token_copy(m).wait_recv()

        x = x_in[m, span, :].astype(F32)
        valid = valid_s[m, span, :]
        scale = lax.rsqrt(jnp.mean(x * x, axis=-1, keepdims=True) + EPS)
        nb = (x * scale * gain[...]).astype(BF16)
        normed[line, :] = nb

        def mix():
            keep_l = slab(keep_s[m, span, :])
            valid_l = slab(valid)
            for blk in range(hidden // LANES):
                cols = slice(blk * LANES, (blk + 1) * LANES)
                zf = dot(nb, w[0, :, cols]) + bias[0:1, cols]
                zi = dot(nb, w[1, :, cols]) + bias[1:2, cols]
                zh = dot(nb, w[2, :, cols])
                low = jnp.minimum(jnp.minimum(zf, zi), 0.0)
                e0 = jnp.exp(low)
                ei, ef = jnp.exp(low - zi), jnp.exp(low - zf)
                top, bot = e0 + ei, e0 + ef
                inv = 1.0 / (top + bot)
                decay = top * inv
                admit = bot * inv
                a = keep_l * decay
                iv = valid_l * admit
                b = iv * zh
                a_g, b_g = groups(a), groups(b)
                state, product = b_g[0], a_g[0]
                states, products = [state], [product]
                for g in range(1, len(a_g)):
                    state = a_g[g] * state + b_g[g]
                    product = a_g[g] * product
                    states.append(state)
                    products.append(product)
                enter, leave = chain(product, state, h_carry[:, cols], False)
                h_carry[:, cols] = leave
                hs = [s + p * enter for s, p in zip(states, products)]
                h_prev = jnp.concatenate([enter] + hs[:-1], axis=0)
                right[3, line, cols] = jnp.concatenate(hs, axis=0).astype(BF16)
                turn = (keep_l * h_prev - valid_l * zh) * inv
                coef[0, line, cols] = a
                coef[1, line, cols] = decay * ef * turn
                coef[2, line, cols] = -admit * ei * turn
                coef[3, line, cols] = iv
            y = dot(right[3, line, :], wt[3])
            x_out[m, span, :] = (x + wide(valid) * y).astype(BF16)

        def feed_on():
            for k in range(2):
                for blk in range(hidden // LANES):
                    cols = slice(blk * LANES, (blk + 1) * LANES)
                    u = dot(nb, w[k, :, cols]) + bias[k : k + 1, cols]
                    phi = 0.5 + 0.5 * lax.erf(u * math.sqrt(0.5))
                    right[2 + k, line, cols] = (u * phi).astype(BF16)
                    coef[k, line, cols] = phi + u * jnp.exp(-0.5 * u * u) * (1.0 / math.sqrt(2.0 * math.pi))
            y = dot(right[2, line, :], wt[2]) + dot(right[3, line, :], wt[3])
            x_out[m, span, :] = (x + wide(valid) * y).astype(BF16)

        if count == 1:
            pl.when(mixer)(mix)
            pl.when(feed)(feed_on)

            @pl.when(m * parts + c >= SENDS)
            def _():
                fwd_copy(m, c).wait_send()

            fwd_copy(m, c).start()
        else:
            feed_on()
            x_out[m, span, :] = (x_out[m, span, :].astype(F32) * wide(valid)).astype(BF16)

    def backward(m, c):
        size = PAIR * PART
        span = pl.ds(pl.multiple_of(c * size, size), size)
        line = pl.ds(pl.multiple_of(m * rows + c * size, size), size)

        @pl.when(section < last)
        def _():
            bwd_copy(m, c).wait_recv()

        @pl.when((section == last) & (c == 0) & (m != last))
        def _():
            cot_copy(m).wait_recv()

        do = do_in[m, span, :].astype(F32) * wide(valid_s[m, span, :])
        dy = do.astype(BF16)
        down[line, :] = dy

        @pl.when(mixer)
        def _():
            for blk in range(hidden // LANES):
                cols = slice(blk * LANES, (blk + 1) * LANES)
                d_all, a_all = dot(dy, w[3, :, cols]), coef[0, line, cols]
                pieces_dh = []
                for part in range(PAIR - 1, -1, -1):
                    spot = slice(part * PART, (part + 1) * PART)
                    d_g, a_g = groups(d_all[spot]), groups(a_all[spot])
                    count = len(a_g)
                    dhs, spread = [None] * count, [None] * count
                    dhs[-1] = d_g[-1]
                    for g in range(count - 2, -1, -1):
                        dhs[g] = d_g[g] + a_g[g + 1] * dhs[g + 1]
                        spread[g] = a_g[g + 1] if g == count - 2 else a_g[g + 1] * spread[g + 1]
                    enter, leave = chain(a_g[0] * spread[0], a_g[0] * dhs[0], e_carry[:, cols], True)
                    e_carry[:, cols] = leave
                    dhs = [d + s * enter for d, s in zip(dhs[:-1], spread[:-1])] + [dhs[-1] + enter]
                    pieces_dh = dhs + pieces_dh
                dh = jnp.concatenate(pieces_dh, axis=0)
                for j in range(3):
                    dz = dh * coef[1 + j, line, cols]
                    right[j, line, cols] = dz.astype(BF16)
                    if j < 2:
                        bias_acc[j, :, cols] += sum(groups(dz))

        @pl.when(feed)
        def _():
            for k in range(2):
                for blk in range(hidden // LANES):
                    cols = slice(blk * LANES, (blk + 1) * LANES)
                    du = dot(dy, w[2 + k, :, cols]) * coef[k, line, cols]
                    right[k, line, cols] = du.astype(BF16)
                    bias_acc[k, :, cols] += sum(groups(du))

        def finish(dn):
            x = x_in[m, span, :].astype(F32)
            scale = lax.rsqrt(jnp.mean(x * x, axis=-1, keepdims=True) + EPS)
            xr = x * scale
            part = dn * xr
            gain_acc[...] += sum(groups(part))
            dng = dn * gain[...]
            mean = jnp.mean(dng * xr, axis=-1, keepdims=True)
            dx_out[m, span, :] = (do + scale * (dng - xr * mean)).astype(BF16)

        @pl.when(mixer)
        def _():
            finish(
                dot(right[0, line, :], wt[0])
                + dot(right[1, line, :], wt[1])
                + dot(right[2, line, :], wt[2])
            )

        @pl.when(feed)
        def _():
            finish(dot(right[0, line, :], wt[0]) + dot(right[1, line, :], wt[1]))

        @pl.when(section > 0)
        def _():
            @pl.when((m > 0) if SENDS >= parts // PAIR else (m * (parts // PAIR) + parts // PAIR - 1 - c >= SENDS))
            def _():
                bwd_copy(m, c).wait_send()

            bwd_copy(m, c).start()

    halves = parts // PAIR

    @pl.loop(0, micro * (parts + halves))
    def _(step):
        pl.when((section == 0) & (step == parts))(flip)

        @pl.when((section < last) & (step < micro * parts))
        def _():
            forward(over(step, parts), within(step, parts), 1)

        turn = over(step, 2)
        late = step - micro * parts

        @pl.when((section == last) & (within(step, 2) == 0) & (turn < micro * halves))
        def _():
            forward(over(turn, halves), within(turn, halves), PAIR)

        @pl.when(jnp.where(section == last, (within(step, 2) == 1) & (turn < micro * halves), late >= 0))
        def _():
            q = jnp.where(section == last, turn, jnp.maximum(late, 0))
            c = within(q, halves)
            backward(over(q, halves), jnp.where(section == last, c, halves - 1 - c))

    def homeward(act):
        for m in range(micro):
            for k, source, result, at in ((0, x_out, final_out, last), (1, dx_out, grad_out, 0)):

                @pl.when((section == at) & (section != m))
                def _():
                    act(home_copy(source, result, k, m), True)

                @pl.when((section == at) & (section == m))
                def _():
                    act(keep_copy(source, result, k, m), False)

    high, broad = TILE
    down_n, across = width // high, hidden // broad
    pieces = 4 * down_n * across // 2
    near, far, gifts = sib_in.shape[0], up_in.shape[0], gift_in.shape[0]
    friend = last - section
    give = jnp.where(section == 0, GIVE[0], jnp.where(section == 1, GIVE[1], 0))
    take = jnp.where(friend == 0, GIVE[0], jnp.where(friend == 1, GIVE[1], 0))

    left[0] = normed[...].T
    left[1] = down[...].T

    start = jnp.where(section == last, JOIN[0], JOIN[1])

    def is_given(t):
        return (within(t, 2) == 1) & (over(t, 2) < give)

    def chain_index(t):
        return t - jnp.minimum(over(t, 2), give)

    def is_taken(t):
        return (t >= start) & (t < start + take)

    def own_index(t):
        return t - jnp.clip(t - start, 0, take)

    def place(piece):
        j = 3 - over(piece, down_n * across)
        rest = within(piece, down_n * across)
        row = pl.multiple_of(within(rest, down_n) * high, high)
        col = pl.multiple_of(over(rest, down_n) * broad, broad)
        return j, row, col

    def partial(t):
        j, row, col = place(2 * t)
        from_down = (j == 3) | (feed & (j == 2))
        return dot(left[jnp.where(from_down, 1, 0), pl.ds(row, 2 * high), :], right[j, :, pl.ds(col, broad)])

    def sib_copy(t):
        k = within(t, near)
        return remote(sib_out.at[k], sib_in.at[k], near_sem.at[0, k], near_sem.at[1, k], section, sibling)

    def gift_copy(d):
        return remote(gift_out.at[d], gift_in.at[d], gift_sem.at[0, d], gift_sem.at[1, d], friend, batch)

    def back_copy(r, d):
        return remote(tot_out.at[within(r, far)], back_in.at[d], gift_sem.at[2, d], gift_sem.at[3, d], friend, batch)

    def back_share(d):
        return remote(back_in.at[d], back_sib.at[d], gift_sem.at[4, d], gift_sem.at[5, d], section, sibling)

    def store_back(d, source, who, k):
        j, row, col = place(4 * d + 2 + who)
        return pltpu.make_async_copy(
            source.at[d], wide_out.at[j, pl.ds(row, high), pl.ds(col, broad)], gift_sem.at[k, d]
        )

    def up_copy(k):
        k = within(k, far)
        return remote(up_out.at[k], up_in.at[k], far_sem.at[0, k], far_sem.at[1, k], section, inner)

    def mirror_copy(k):
        k = within(k, far)
        return remote(up_out.at[k], ret_in.at[k], far_sem.at[0, k], far_sem.at[2, k], section, inner)

    def ret_copy(k):
        k = within(k, far)
        return remote(tot_out.at[k], ret_in.at[k], far_sem.at[3, k], far_sem.at[2, k], section, outer)

    def share_copy(r):
        k, at = within(r, far), within(own_index(r), near)
        return remote(tot_out.at[k], tot_in.at[at], far_sem.at[4, k], near_sem.at[2, at], section, sibling)

    def piece_of(r):
        return jnp.where(r < give, 2 * r, own_index(r) + give)

    def store_own(r):
        j, row, col = place(2 * piece_of(r) + core)
        k = within(r, far)
        return pltpu.make_async_copy(
            tot_out.at[k], wide_out.at[j, pl.ds(row, high), pl.ds(col, broad)], far_sem.at[5, k]
        )

    def store_other(r):
        j, row, col = place(2 * piece_of(r) + 1 - core)
        k = within(own_index(r), near)
        return pltpu.make_async_copy(
            tot_in.at[k], wide_out.at[j, pl.ds(row, high), pl.ds(col, broad)], near_sem.at[3, k]
        )

    def is_result(r):
        return (r >= 0) & (r < pieces - give + take)

    lag = jnp.minimum(4 + 8 * depth, LAG)
    most = LAG
    small_at = 2 + 4 * (half - 1 - depth)
    small_back = 2 + 4 * half + 4 * depth

    for k in range(2):
        small[0, k : k + 1, :] = jnp.sum(bias_acc[k], axis=0, keepdims=True)
    small[0, 2:3, 0:width] = jnp.sum(gain_acc[...], axis=0, keepdims=True)
    small[0, 2:3, width:] = jnp.zeros((1, hidden - width), F32)
    small[0, 3:8, :] = jnp.zeros((5, hidden), F32)

    def small_sib():
        return remote(small.at[0], small.at[1], small_sem.at[0], small_sem.at[1], section, sibling)

    def small_up(to):
        return remote(small.at[2], small.at[to], small_sem.at[2], small_sem.at[to], section, inner)

    def small_ret():
        return remote(small.at[5], small.at[4], small_sem.at[5], small_sem.at[4], section, outer)

    def small_step(t):
        @pl.when(t == 0)
        def _():
            small_sib().start()

        @pl.when(t == small_at)
        def _():
            small_sib().wait_recv()
            small[2] = small[0] + small[1]

            @pl.when(has_outer)
            def _():
                small_up(3).wait_recv()
                small[2] = small[2] + small[3]

            @pl.when(middle)
            def _():
                small_up(4).start()

            @pl.when(jnp.logical_not(middle))
            def _():
                small_up(3).start()

        @pl.when(t == small_back)
        def _():
            small_up(4).wait_recv()

            @pl.when(middle)
            def _():
                small[5] = small[2] + small[4]

            @pl.when(jnp.logical_not(middle))
            def _():
                small[5] = small[4]

            @pl.when(has_outer)
            def _():
                small_ret().start()

    @pl.loop(0, max(pieces + gifts + most + 6, 3 + 8 * half))
    def _(t):
        @pl.when((t < pieces + take) & jnp.logical_not(is_taken(t)))
        def _():
            i = own_index(t)
            own[within(i, 2)] = partial(i)
            sib_out[within(i, near)] = own[within(i, 2), pl.ds((1 - core) * high, high), :].astype(BF16)
            sib_copy(i).start()

        @pl.when((t >= 1) & (t <= pieces + take))
        def _():
            s = t - 1
            i = own_index(s)
            k = chain_index(s)
            slot = within(k, far)

            def onward(total):
                @pl.when(has_outer)
                def _():
                    up_copy(k).wait_recv()
                    up_out[slot] = (total + up_in[slot].astype(F32)).astype(BF16)

                @pl.when(jnp.logical_not(has_outer))
                def _():
                    up_out[slot] = total.astype(BF16)

                @pl.when(middle)
                def _():
                    mirror_copy(k).start()

                @pl.when(jnp.logical_not(middle))
                def _():
                    up_copy(k).start()

            @pl.when(jnp.logical_not(is_taken(s)))
            def _():
                sib_copy(i).wait()
                total = own[within(i, 2), pl.ds(core * high, high), :] + sib_in[within(i, near)].astype(F32)

                @pl.when(is_given(s))
                def _():
                    d = over(s, 2)
                    gift_out[d] = total.astype(BF16)
                    gift_copy(d).start()

                @pl.when(jnp.logical_not(is_given(s)))
                def _():
                    onward(total)

            @pl.when(is_taken(s))
            def _():
                d = s - start
                gift_copy(d).wait_recv()
                onward(gift_in[d].astype(F32))

        on = jnp.logical_not(is_given(t))
        r = chain_index(t) - lag
        slot = within(r, far)

        @pl.when(on & is_result(r))
        def _():
            mirror_copy(r).wait()

            @pl.when(middle)
            def _():
                tot_out[slot] = (up_out[slot].astype(F32) + ret_in[slot].astype(F32)).astype(BF16)

            @pl.when(jnp.logical_not(middle))
            def _():
                tot_out[slot] = ret_in[slot]

            @pl.when(has_outer)
            def _():
                ret_copy(r).start()

            @pl.when(is_taken(r))
            def _():
                back_copy(r, r - start).start()

            @pl.when(jnp.logical_not(is_taken(r)))
            def _():
                share_copy(r).start()
                store_own(r).start()

        r2 = r - 2

        @pl.when(on & is_result(r2) & jnp.logical_not(is_taken(r2)))
        def _():
            share_copy(r2).wait_recv()
            store_other(r2).start()

        r4 = r - 4

        @pl.when(on & is_result(r4))
        def _():
            @pl.when(has_outer)
            def _():
                ret_copy(r4).wait_send()

            @pl.when(is_taken(r4))
            def _():
                back_copy(r4, r4 - start).wait_send()

            @pl.when(jnp.logical_not(is_taken(r4)))
            def _():
                share_copy(r4).wait_send()
                store_own(r4).wait()
                store_other(r4).wait()

        d = t - LATE

        @pl.when((d >= 0) & (d < give))
        def _():
            gift_copy(d).wait_send()
            back_copy(r, d).wait_recv()
            back_share(d).start()
            store_back(d, back_in, core, 6).start()

        d2 = d - 2

        @pl.when((d2 >= 0) & (d2 < give))
        def _():
            back_share(d2).wait()
            store_back(d2, back_sib, 1 - core, 7).start()

        d4 = d - 4

        @pl.when((d4 >= 0) & (d4 < give))
        def _():
            store_back(d4, back_in, core, 6).wait()
            store_back(d4, back_sib, 1 - core, 7).wait()

        pl.when(t == 2 * gifts + 2)(lambda: homeward(lambda copy, far: copy.start()))
        small_step(t)

    small_out[...] = small[5] * (1.0 / math.sqrt(micro * rows * batches))

    small_sib().wait_send()
    small_up(3).wait_send()

    @pl.when(has_outer)
    def _():
        small_ret().wait_send()

    @pl.when(section != 0)
    def _():
        token_copy(section).wait_send()

    pl.when(section == 0)(lambda: side_copy().wait_send())
    pl.when(section == last - 1)(lambda: side_last().wait_send())

    @pl.when((section != last) & (section != 0))
    def _():
        cot_copy(section).wait_send()

    for c in range(SENDS):

        @pl.when(section != last)
        def _():
            fwd_copy(0, c).wait_send()

        @pl.when(section != 0)
        def _():
            bwd_copy(0, c).wait_send()

    homeward(lambda copy, far: copy.wait_send() if far else copy.wait())

    @pl.when(section != last)
    def _():
        home_copy(x_out, final_out, 0, section).wait_recv()

    @pl.when(section != 0)
    def _():
        home_copy(dx_out, grad_out, 1, section).wait_recv()


def finish_kernel(scale, wide, small, final_in, grad_in, final, grad, weight, bias, gain, full, turned, sem):
    depth = wide.shape[1] // CUTS
    stores = []
    for n in range(wide.shape[0] * CUTS):
        j, span = n // CUTS, pl.ds((n % CUTS) * depth, depth)
        full[j, span, :] = wide[j, span, :].astype(F32) * scale
        stores.append(pltpu.make_async_copy(full.at[j, span], weight.at[0, j, span], sem.at[n]))
        stores[-1].start()
    order = order_matrix(PART, True)
    for k, (source, result) in enumerate(((final_in, final), (grad_in, grad))):
        for c in range(source.shape[1] // PART):
            span = slice(c * PART, (c + 1) * PART)
            turned[k, span, :] = dot(order, source[0, span, :]).astype(BF16)
        stores.append(pltpu.make_async_copy(turned.at[k], result.at[0], sem.at[len(stores)]))
        stores[-1].start()
    bias[0] = small[0:2, :]
    gain[...] = small[2:3, 0 : gain.shape[1]]
    for copy in stores:
        copy.wait()


def local(tokens, cotangent, weights, biases, gains, lengths):
    micro = lengths.shape[0]
    _, rows, width = tokens.shape
    hidden = weights.shape[3]
    parts = rows // PART
    pieces = 4 * width * hidden // (TILE[0] * TILE[1]) // 2
    any_spec = pl.BlockSpec(memory_space=pl.ANY)
    vmem = pl.BlockSpec(memory_space=pltpu.VMEM)
    dma = pltpu.SemaphoreType.DMA
    relay = pltpu.VMEM((micro, rows, width), BF16)
    near = min(8, pieces)
    far = 16
    close = pltpu.VMEM((near, *TILE), BF16)
    wait = pltpu.VMEM((far, *TILE), BF16)
    final, grad, wide, small = pl.pallas_call(
        relay_kernel,
        name="relay",
        out_shape=(
            pltpu.VMEM(tokens.shape, BF16),
            pltpu.VMEM(tokens.shape, BF16),
            pltpu.VMEM((4, width, hidden), BF16),
            pltpu.VMEM((8, hidden), F32),
        ),
        in_specs=[vmem, *[any_spec] * 5],
        out_specs=(vmem, vmem, vmem, vmem),
        scratch_shapes=[
            pltpu.VMEM((4, width, hidden), BF16),
            pltpu.VMEM((4, hidden, width), BF16),
            pltpu.VMEM((2, hidden), F32),
            pltpu.VMEM((1, width), F32),
            pltpu.VMEM((5, rows, width), BF16),
            relay,
            relay,
            relay,
            relay,
            pltpu.VMEM((micro, rows, 128), F32),
            pltpu.VMEM((micro, rows, 128), F32),
            pltpu.VMEM((micro * rows, width), BF16),
            pltpu.VMEM((micro * rows, width), BF16),
            pltpu.VMEM((4, micro * rows, hidden), BF16),
            pltpu.VMEM((4, micro * rows, hidden), F32),
            pltpu.VMEM((8, hidden), F32),
            pltpu.VMEM((8, hidden), F32),
            pltpu.VMEM((8, width), F32),
            pltpu.VMEM((2, 8, hidden), F32),
            close,
            close,
            pltpu.VMEM((2, 2 * TILE[0], TILE[1]), F32),
            wait,
            wait,
            wait,
            wait,
            close,
            pltpu.VMEM((6, 8, hidden), F32),
            pltpu.VMEM((2, width, micro * rows), BF16),
            *[pltpu.VMEM((max(GIVE), *TILE), BF16)] * 4,
            dma((8,)),
            dma((4 + 2 * micro,)),
            dma((SENDS,)),
            dma((micro, parts)),
            dma((SENDS,)),
            dma((micro, parts // PAIR)),
            dma((2, micro + 1)),
            dma((4, near)),
            dma((6, far)),
            dma((8, max(GIVE))),
            dma((6,)),
        ],
        compiler_params=pltpu.CompilerParams(
            collective_id=0, has_side_effects=True, vmem_limit_bytes=55 * 2**20
        ),
    )(lengths.T, tokens, cotangent, weights, biases, gains)
    scale = 1.0 / math.sqrt(micro * rows * lax.axis_size("batch"))
    return pl.pallas_call(
        functools.partial(finish_kernel, scale),
        name="finish",
        out_shape=(
            jax.ShapeDtypeStruct(tokens.shape, BF16),
            jax.ShapeDtypeStruct(tokens.shape, BF16),
            jax.ShapeDtypeStruct(weights.shape, F32),
            jax.ShapeDtypeStruct(biases.shape, F32),
            jax.ShapeDtypeStruct(gains.shape, F32),
        ),
        in_specs=[vmem, vmem, vmem, vmem],
        out_specs=(any_spec, any_spec, any_spec, vmem, vmem),
        scratch_shapes=[
            pltpu.VMEM((4, width, hidden), F32),
            pltpu.VMEM((2, rows, width), BF16),
            dma((4 * CUTS + 2,)),
        ],
        compiler_params=pltpu.CompilerParams(vmem_limit_bytes=24 * 2**20),
    )(*[pltpu.with_memory_space_constraint(value, pltpu.VMEM) for value in (wide, small, final, grad)])


def solution(mesh):
    row = P("section", "batch", None)
    placed = (
        row,
        row,
        P("section", None, None, None),
        P("section", None, None),
        P("section", None),
        P(None, "batch"),
    )
    return jax.shard_map(
        local,
        mesh=mesh,
        in_specs=placed,
        out_specs=(row, row, *placed[2:5]),
        check_vma=False,
    )
```

```python
import functools
import math

import jax
import jax.numpy as jnp
from jax import lax
from jax.experimental import pallas as pl
from jax.experimental.pallas import tpu as pltpu
from jax.sharding import PartitionSpec as P

MESH = pl.DeviceIdType.MESH
EPS = 1e-05
PART = 64
PAIR = 2
GIVE = (10, 3)
JOIN = (24, 14)
LATE = 34
NEXT = 3
LAG = 14
CUTS = 4
SENDS = 2
LANES = 256
TILE = (128, 256)
F32 = jnp.float32
BF16 = jnp.bfloat16


def dot(a, b):
    return jnp.dot(a, b, preferred_element_type=F32)


def over(value, count):
    return lax.shift_right_logical(value, count.bit_length() - 1)


def within(value, count):
    return lax.bitwise_and(value, count - 1)


def order_matrix(rows, back):
    new = lax.broadcasted_iota(jnp.int32, (rows, rows), 1 if back else 0)
    old = lax.broadcasted_iota(jnp.int32, (rows, rows), 0 if back else 1)
    hit = (within(new, 8) * (rows // 8) + over(new, 8)) == old
    return jnp.where(hit, 1.0, 0.0).astype(BF16)


def groups(value):
    return [value[8 * g : 8 * g + 8] for g in range(value.shape[0] // 8)]


def chain(gain, add, carry, back):
    row = lax.broadcasted_iota(jnp.int32, gain.shape, 0)
    for step in (1, 2, 4):
        shift = 8 - step if back else step
        inside = (row < 8 - step) if back else (row >= step)
        add = jnp.where(inside, gain * pltpu.roll(add, shift, 0) + add, add)
        gain = jnp.where(inside, gain * pltpu.roll(gain, shift, 0), gain)
    whole = gain * carry + add
    edge = 7 if back else 0
    enter = jnp.where(row == edge, carry, pltpu.roll(whole, 7 if back else 1, 0))
    last = whole[0:1] if back else whole[7:8]
    return enter, jnp.broadcast_to(last, gain.shape)


def relay_kernel(
    lengths,
    tokens,
    cotangent,
    weights,
    biases,
    gains,
    final_out,
    grad_out,
    wide_out,
    small_out,
    w,
    wt,
    bias,
    gain,
    stage,
    x_in,
    do_in,
    x_out,
    dx_out,
    valid_s,
    keep_s,
    normed,
    down,
    right,
    coef,
    h_carry,
    e_carry,
    gain_acc,
    bias_acc,
    sib_out,
    sib_in,
    own,
    up_out,
    up_in,
    ret_in,
    tot_out,
    tot_in,
    small,
    left,
    gift_out,
    gift_in,
    back_in,
    back_sib,
    load_sem,
    tok_sem,
    fwd_send,
    fwd_recv,
    bwd_send,
    bwd_recv,
    around_sem,
    home_sem,
    near_sem,
    far_sem,
    gift_sem,
    small_sem,
):
    micro, rows, width = x_in.shape
    parts = rows // PART
    hidden = w.shape[2]
    section, batch = lax.axis_index("section"), lax.axis_index("batch")
    sections, batches = lax.axis_size("section"), lax.axis_size("batch")
    last = sections - 1
    mixer = lax.rem(section, 2) == 0
    feed = lax.rem(section, 2) == 1
    chips = batches // 2
    chip, core = batch // 2, lax.rem(batch, 2)
    sibling = batch + 1 - 2 * core
    half = chips // 2
    low_side = chip < half
    step_in = jnp.where(low_side, 2, -2)
    inner = batch + step_in
    outer = batch - step_in
    middle = (chip == half - 1) | (chip == half)
    has_outer = (chip > 0) & (chip < chips - 1)
    depth = jnp.where(low_side, half - 1 - chip, chip - half)

    def remote(src, dst, send, recv, to_section, to_batch):
        return pltpu.make_async_remote_copy(
            src_ref=src,
            dst_ref=dst,
            send_sem=send,
            recv_sem=recv,
            device_id=(to_section, to_batch),
            device_id_type=MESH,
        )

    sources = [
        (tokens.at[0], stage.at[0]),
        (cotangent.at[0], stage.at[1]),
        (biases.at[0], bias),
        (gains, gain),
        *[(weights.at[0, j], w.at[j]) for j in (3, 0, 1, 2)],
    ]
    loads = [pltpu.make_async_copy(src, dst, load_sem.at[i]) for i, (src, dst) in enumerate(sources)]
    for copy in loads:
        copy.start()

    barrier = pltpu.get_barrier_semaphore()
    for other in range(1, sections):
        pl.semaphore_signal(
            barrier, inc=1, device_id=(lax.rem(section + other, sections), batch), device_id_type=MESH
        )
    pl.semaphore_signal(barrier, inc=1, device_id=(section, sibling), device_id_type=MESH)
    pl.semaphore_signal(barrier, inc=1, device_id=(section, inner), device_id_type=MESH)

    @pl.when(has_outer)
    def _():
        pl.semaphore_signal(barrier, inc=1, device_id=(section, outer), device_id_type=MESH)

    spot = lax.broadcasted_iota(jnp.int32, (rows, 128), 0)
    spot_in = within(spot, PART)
    spot = spot - spot_in + within(spot_in, 8) * (PART // 8) + over(spot_in, 8)
    for m in range(micro):
        end = jnp.zeros((1, 1), jnp.int32)
        start_hit = jnp.zeros((rows, 128), F32)
        for k in range(lengths.shape[0]):
            start_hit = jnp.where(spot == end, 1.0, start_hit)
            end = end + lengths[k : k + 1, m : m + 1]
        valid = jnp.where(spot < end, 1.0, 0.0)
        valid_s[m] = valid
        keep_s[m] = valid * (1.0 - start_hit)
    h_carry[...] = jnp.zeros_like(h_carry)
    e_carry[...] = jnp.zeros_like(e_carry)
    gain_acc[...] = jnp.zeros_like(gain_acc)
    bias_acc[...] = jnp.zeros_like(bias_acc)

    perm = order_matrix(PART, False)
    loads[0].wait()
    for c in range(parts):
        span = pl.ds(c * PART, PART)
        ordered = dot(perm, stage[0, span, :]).astype(BF16)
        stage[2, span, :] = ordered

        @pl.when(section == 0)
        def _():
            x_in[0, span, :] = ordered

    loads[1].wait()
    for c in range(parts):
        span = pl.ds(c * PART, PART)
        ordered = dot(perm, stage[1, span, :]).astype(BF16)
        stage[3, span, :] = ordered

        @pl.when(section == last)
        def _():
            do_in[last, span, :] = ordered

    pl.semaphore_wait(barrier, sections + 1 + jnp.where(has_outer, 1, 0))

    def token_copy(m):
        return remote(stage.at[2], x_in.at[m], tok_sem.at[0], tok_sem.at[2 + m], 0, batch)

    def cot_copy(m):
        return remote(stage.at[3], do_in.at[m], tok_sem.at[1], tok_sem.at[2 + micro + m], last, batch)

    def side_copy():
        return remote(stage.at[3], stage.at[4], tok_sem.at[1], tok_sem.at[2 + 2 * micro], last - 1, batch)

    def side_last():
        return remote(stage.at[4], do_in.at[0], tok_sem.at[2 + 2 * micro + 1], tok_sem.at[2 + micro], last, batch)

    @pl.when(section != 0)
    def _():
        token_copy(section).start()

    pl.when(section == 0)(lambda: side_copy().start())

    @pl.when((section != last) & (section != 0))
    def _():
        cot_copy(section).start()

    for copy in loads[2:]:
        copy.wait()

    wt[3] = w[3].T

    def flip():
        for j in range(3):
            wt[j] = w[j].T

    pl.when(section > 0)(flip)

    @pl.when(section == last - 1)
    def _():
        side_copy().wait_recv()
        side_last().start()

    def wide(mask):
        return jnp.concatenate([mask] * (width // 128), axis=1)

    def slab(mask):
        return jnp.concatenate([mask] * (LANES // 128), axis=1)

    def fwd_copy(m, c):
        span = pl.ds(pl.multiple_of(c * PART, PART), PART)
        return remote(
            x_out.at[m, span],
            x_in.at[m, span],
            fwd_send.at[within(c, SENDS)],
            fwd_recv.at[m, c],
            jnp.minimum(section + 1, last),
            batch,
        )

    def bwd_copy(m, c):
        span = pl.ds(pl.multiple_of(c * PAIR * PART, PAIR * PART), PAIR * PART)
        return remote(
            dx_out.at[m, span],
            do_in.at[m, span],
            bwd_send.at[within(c, SENDS)],
            bwd_recv.at[m, c],
            jnp.maximum(section - 1, 0),
            batch,
        )

    def around_copy(c):
        span = pl.ds(pl.multiple_of(c * PAIR * PART, PAIR * PART), PAIR * PART)
        return remote(
            dx_out.at[0, span], stage.at[2, span], bwd_send.at[within(c, SENDS)], around_sem.at[0, c], 0, batch
        )

    def around_last(c):
        span = pl.ds(pl.multiple_of(c * PAIR * PART, PAIR * PART), PAIR * PART)
        return remote(stage.at[2, span], do_in.at[0, span], around_sem.at[1, c], bwd_recv.at[0, c], 1, batch)

    def home_copy(source, result, k, m):
        return remote(source.at[m], result.at[0], home_sem.at[k, m], home_sem.at[k, micro], m, batch)

    def keep_copy(source, result, k, m):
        return pltpu.make_async_copy(source.at[m], result.at[0], home_sem.at[k, m])

    def forward(m, c, count):
        size = count * PART
        span = pl.ds(pl.multiple_of(c * size, size), size)
        line = pl.ds(pl.multiple_of(m * rows + c * size, size), size)

        @pl.when(section > 0)
        def _():
            for k in range(count):
                fwd_copy(m, c * count + k).wait_recv()

        @pl.when((section == 0) & (c == 0) & (m > 0))
        def _():
            token_copy(m).wait_recv()

        x = x_in[m, span, :].astype(F32)
        valid = valid_s[m, span, :]
        scale = lax.rsqrt(jnp.mean(x * x, axis=-1, keepdims=True) + EPS)
        nb = (x * scale * gain[...]).astype(BF16)
        normed[line, :] = nb

        def mix():
            keep_l = slab(keep_s[m, span, :])
            valid_l = slab(valid)
            for blk in range(hidden // LANES):
                cols = slice(blk * LANES, (blk + 1) * LANES)
                zf = dot(nb, w[0, :, cols]) + bias[0:1, cols]
                zi = dot(nb, w[1, :, cols]) + bias[1:2, cols]
                zh = dot(nb, w[2, :, cols])
                low = jnp.minimum(jnp.minimum(zf, zi), 0.0)
                e0 = jnp.exp(low)
                ei, ef = jnp.exp(low - zi), jnp.exp(low - zf)
                top, bot = e0 + ei, e0 + ef
                inv = 1.0 / (top + bot)
                decay = top * inv
                admit = bot * inv
                a = keep_l * decay
                iv = valid_l * admit
                b = iv * zh
                a_g, b_g = groups(a), groups(b)
                state, product = b_g[0], a_g[0]
                states, products = [state], [product]
                for g in range(1, len(a_g)):
                    state = a_g[g] * state + b_g[g]
                    product = a_g[g] * product
                    states.append(state)
                    products.append(product)
                enter, leave = chain(product, state, h_carry[:, cols], False)
                h_carry[:, cols] = leave
                hs = [s + p * enter for s, p in zip(states, products)]
                h_prev = jnp.concatenate([enter] + hs[:-1], axis=0)
                right[3, line, cols] = jnp.concatenate(hs, axis=0).astype(BF16)
                turn = (keep_l * h_prev - valid_l * zh) * inv
                coef[0, line, cols] = a
                coef[1, line, cols] = decay * ef * turn
                coef[2, line, cols] = -admit * ei * turn
                coef[3, line, cols] = iv
            y = dot(right[3, line, :], wt[3])
            x_out[m, span, :] = (x + wide(valid) * y).astype(BF16)

        def feed_on():
            for k in range(2):
                for blk in range(hidden // LANES):
                    cols = slice(blk * LANES, (blk + 1) * LANES)
                    u = dot(nb, w[k, :, cols]) + bias[k : k + 1, cols]
                    phi = 0.5 + 0.5 * lax.erf(u * math.sqrt(0.5))
                    right[2 + k, line, cols] = (u * phi).astype(BF16)
                    coef[k, line, cols] = phi + u * jnp.exp(-0.5 * u * u) * (1.0 / math.sqrt(2.0 * math.pi))
            y = dot(right[2, line, :], wt[2]) + dot(right[3, line, :], wt[3])
            x_out[m, span, :] = (x + wide(valid) * y).astype(BF16)

        if count == 1:
            pl.when(mixer)(mix)
            pl.when(feed)(feed_on)

            @pl.when(m * parts + c >= SENDS)
            def _():
                fwd_copy(m, c).wait_send()

            fwd_copy(m, c).start()
        else:
            feed_on()
            x_out[m, span, :] = (x_out[m, span, :].astype(F32) * wide(valid)).astype(BF16)

    def backward(m, c):
        size = PAIR * PART
        span = pl.ds(pl.multiple_of(c * size, size), size)
        line = pl.ds(pl.multiple_of(m * rows + c * size, size), size)

        @pl.when(section < last)
        def _():
            bwd_copy(m, c).wait_recv()

        @pl.when((section == last) & (c == 0) & (m != last))
        def _():
            cot_copy(m).wait_recv()

        do = do_in[m, span, :].astype(F32) * wide(valid_s[m, span, :])
        dy = do.astype(BF16)
        down[line, :] = dy

        @pl.when(mixer)
        def _():
            for blk in range(hidden // LANES):
                cols = slice(blk * LANES, (blk + 1) * LANES)
                d_all, a_all = dot(dy, w[3, :, cols]), coef[0, line, cols]
                pieces_dh = []
                for part in range(PAIR - 1, -1, -1):
                    spot = slice(part * PART, (part + 1) * PART)
                    d_g, a_g = groups(d_all[spot]), groups(a_all[spot])
                    count = len(a_g)
                    dhs, spread = [None] * count, [None] * count
                    dhs[-1] = d_g[-1]
                    for g in range(count - 2, -1, -1):
                        dhs[g] = d_g[g] + a_g[g + 1] * dhs[g + 1]
                        spread[g] = a_g[g + 1] if g == count - 2 else a_g[g + 1] * spread[g + 1]
                    enter, leave = chain(a_g[0] * spread[0], a_g[0] * dhs[0], e_carry[:, cols], True)
                    e_carry[:, cols] = leave
                    dhs = [d + s * enter for d, s in zip(dhs[:-1], spread[:-1])] + [dhs[-1] + enter]
                    pieces_dh = dhs + pieces_dh
                dh = jnp.concatenate(pieces_dh, axis=0)
                for j in range(3):
                    dz = dh * coef[1 + j, line, cols]
                    right[j, line, cols] = dz.astype(BF16)
                    if j < 2:
                        bias_acc[j, :, cols] += sum(groups(dz))

        @pl.when(feed)
        def _():
            for k in range(2):
                for blk in range(hidden // LANES):
                    cols = slice(blk * LANES, (blk + 1) * LANES)
                    du = dot(dy, w[2 + k, :, cols]) * coef[k, line, cols]
                    right[k, line, cols] = du.astype(BF16)
                    bias_acc[k, :, cols] += sum(groups(du))

        def finish(dn):
            x = x_in[m, span, :].astype(F32)
            scale = lax.rsqrt(jnp.mean(x * x, axis=-1, keepdims=True) + EPS)
            xr = x * scale
            part = dn * xr
            gain_acc[...] += sum(groups(part))
            dng = dn * gain[...]
            mean = jnp.mean(dng * xr, axis=-1, keepdims=True)
            dx_out[m, span, :] = (do + scale * (dng - xr * mean)).astype(BF16)

        @pl.when(mixer)
        def _():
            finish(
                dot(right[0, line, :], wt[0])
                + dot(right[1, line, :], wt[1])
                + dot(right[2, line, :], wt[2])
            )

        @pl.when(feed)
        def _():
            finish(dot(right[0, line, :], wt[0]) + dot(right[1, line, :], wt[1]))

        @pl.when(section > 0)
        def _():
            @pl.when((m > 0) if SENDS >= parts // PAIR else (m * (parts // PAIR) + parts // PAIR - 1 - c >= SENDS))
            def _():
                bwd_copy(m, c).wait_send()

            by_side = (section == 2) & (m == 0)
            pl.when(by_side)(lambda: around_copy(c).start())
            pl.when(jnp.logical_not(by_side))(lambda: bwd_copy(m, c).start())

    halves = parts // PAIR

    @pl.loop(0, micro * (parts + halves))
    def _(step):
        pl.when((section == 0) & (step == parts))(flip)

        early = (section == 2) & (step >= (micro - 1) * parts)
        back_now = jnp.where(early, step < (micro - 1) * parts + halves, step >= micro * parts)
        back_now = back_now | (step >= micro * parts + halves)
        f_step = jnp.where(early, step - halves, step)
        late = jnp.where(early & (step < (micro - 1) * parts + halves), step - (micro - 1) * parts, step - micro * parts)

        @pl.when((section < last) & jnp.logical_not(back_now))
        def _():
            forward(over(f_step, parts), within(f_step, parts), 1)

        turn = over(step, 2)

        @pl.when((section == 0) & (step == micro * parts))
        def _():
            for c in range(halves - 1, -1, -1):
                around_copy(c).wait_recv()
                around_last(c).start()

        @pl.when((section == last) & (within(step, 2) == 0) & (turn < micro * halves))
        def _():
            forward(over(turn, halves), within(turn, halves), PAIR)

        @pl.when(jnp.where(section == last, (within(step, 2) == 1) & (turn < micro * halves), back_now))
        def _():
            q = jnp.where(section == last, turn, jnp.maximum(late, 0))
            c = within(q, halves)
            backward(over(q, halves), jnp.where(section == last, c, halves - 1 - c))

    def homeward(act):
        for m in range(micro):
            for k, source, result, at in ((0, x_out, final_out, last), (1, dx_out, grad_out, 0)):

                @pl.when((section == at) & (section != m))
                def _():
                    act(home_copy(source, result, k, m), True)

                @pl.when((section == at) & (section == m))
                def _():
                    act(keep_copy(source, result, k, m), False)

    high, broad = TILE
    down_n, across = width // high, hidden // broad
    pieces = 4 * down_n * across // 2
    near, far, gifts = sib_in.shape[0], up_in.shape[0], gift_in.shape[0]
    friend = last - section
    give = jnp.where(section == 0, GIVE[0], jnp.where(section == 1, GIVE[1], 0))
    take = jnp.where(friend == 0, GIVE[0], jnp.where(friend == 1, GIVE[1], 0))

    left[0] = normed[...].T
    left[1] = down[...].T

    start = jnp.where(section == last, JOIN[0], JOIN[1])

    def is_given(t):
        return (within(t, 2) == 1) & (over(t, 2) < give)

    def chain_index(t):
        return t - jnp.minimum(over(t, 2), give)

    def is_taken(t):
        return (t >= start) & (t < start + take)

    def own_index(t):
        return t - jnp.clip(t - start, 0, take)

    def place(piece):
        j = 3 - over(piece, down_n * across)
        rest = within(piece, down_n * across)
        row = pl.multiple_of(within(rest, down_n) * high, high)
        col = pl.multiple_of(over(rest, down_n) * broad, broad)
        return j, row, col

    def partial(t):
        j, row, col = place(2 * t)
        from_down = (j == 3) | (feed & (j == 2))
        return dot(left[jnp.where(from_down, 1, 0), pl.ds(row, 2 * high), :], right[j, :, pl.ds(col, broad)])

    def sib_copy(t):
        k = within(t, near)
        return remote(sib_out.at[k], sib_in.at[k], near_sem.at[0, k], near_sem.at[1, k], section, sibling)

    def gift_copy(d):
        return remote(gift_out.at[d], gift_in.at[d], gift_sem.at[0, d], gift_sem.at[1, d], friend, batch)

    def back_copy(r, d):
        return remote(tot_out.at[within(r, far)], back_in.at[d], gift_sem.at[2, d], gift_sem.at[3, d], friend, batch)

    def back_share(d):
        return remote(back_in.at[d], back_sib.at[d], gift_sem.at[4, d], gift_sem.at[5, d], section, sibling)

    def store_back(d, source, who, k):
        j, row, col = place(4 * d + 2 + who)
        return pltpu.make_async_copy(
            source.at[d], wide_out.at[j, pl.ds(row, high), pl.ds(col, broad)], gift_sem.at[k, d]
        )

    def up_copy(k):
        k = within(k, far)
        return remote(up_out.at[k], up_in.at[k], far_sem.at[0, k], far_sem.at[1, k], section, inner)

    def mirror_copy(k):
        k = within(k, far)
        return remote(up_out.at[k], ret_in.at[k], far_sem.at[0, k], far_sem.at[2, k], section, inner)

    def ret_copy(k):
        k = within(k, far)
        return remote(tot_out.at[k], ret_in.at[k], far_sem.at[3, k], far_sem.at[2, k], section, outer)

    def share_copy(r):
        k, at = within(r, far), within(own_index(r), near)
        return remote(tot_out.at[k], tot_in.at[at], far_sem.at[4, k], near_sem.at[2, at], section, sibling)

    def piece_of(r):
        return jnp.where(r < give, 2 * r, own_index(r) + give)

    def store_own(r):
        j, row, col = place(2 * piece_of(r) + core)
        k = within(r, far)
        return pltpu.make_async_copy(
            tot_out.at[k], wide_out.at[j, pl.ds(row, high), pl.ds(col, broad)], far_sem.at[5, k]
        )

    def store_other(r):
        j, row, col = place(2 * piece_of(r) + 1 - core)
        k = within(own_index(r), near)
        return pltpu.make_async_copy(
            tot_in.at[k], wide_out.at[j, pl.ds(row, high), pl.ds(col, broad)], near_sem.at[3, k]
        )

    def is_result(r):
        return (r >= 0) & (r < pieces - give + take)

    lag = jnp.minimum(NEXT + 3 + 8 * depth, LAG)
    most = LAG
    small_at = 2 + 4 * (half - 1 - depth)
    small_back = 2 + 4 * half + 4 * depth

    for k in range(2):
        small[0, k : k + 1, :] = jnp.sum(bias_acc[k], axis=0, keepdims=True)
    small[0, 2:3, 0:width] = jnp.sum(gain_acc[...], axis=0, keepdims=True)
    small[0, 2:3, width:] = jnp.zeros((1, hidden - width), F32)
    small[0, 3:8, :] = jnp.zeros((5, hidden), F32)

    def small_sib():
        return remote(small.at[0], small.at[1], small_sem.at[0], small_sem.at[1], section, sibling)

    def small_up(to):
        return remote(small.at[2], small.at[to], small_sem.at[2], small_sem.at[to], section, inner)

    def small_ret():
        return remote(small.at[5], small.at[4], small_sem.at[5], small_sem.at[4], section, outer)

    def small_step(t):
        @pl.when(t == 0)
        def _():
            small_sib().start()

        @pl.when(t == small_at)
        def _():
            small_sib().wait_recv()
            small[2] = small[0] + small[1]

            @pl.when(has_outer)
            def _():
                small_up(3).wait_recv()
                small[2] = small[2] + small[3]

            @pl.when(middle)
            def _():
                small_up(4).start()

            @pl.when(jnp.logical_not(middle))
            def _():
                small_up(3).start()

        @pl.when(t == small_back)
        def _():
            small_up(4).wait_recv()

            @pl.when(middle)
            def _():
                small[5] = small[2] + small[4]

            @pl.when(jnp.logical_not(middle))
            def _():
                small[5] = small[4]

            @pl.when(has_outer)
            def _():
                small_ret().start()

    @pl.loop(0, max(pieces + gifts + most + 6, 3 + 8 * half))
    def _(t):
        @pl.when((t < pieces + take) & jnp.logical_not(is_taken(t)))
        def _():
            i = own_index(t)
            own[within(i, 4)] = partial(i)
            sib_out[within(i, near)] = own[within(i, 4), pl.ds((1 - core) * high, high), :].astype(BF16)
            sib_copy(i).start()

        s = t - NEXT

        @pl.when((s >= 0) & (s < pieces + take))
        def _():
            i = own_index(s)
            k = chain_index(s)
            slot = within(k, far)

            def onward(total):
                @pl.when(has_outer)
                def _():
                    up_copy(k).wait_recv()
                    up_out[slot] = (total + up_in[slot].astype(F32)).astype(BF16)

                @pl.when(jnp.logical_not(has_outer))
                def _():
                    up_out[slot] = total.astype(BF16)

                @pl.when(middle)
                def _():
                    mirror_copy(k).start()

                @pl.when(jnp.logical_not(middle))
                def _():
                    up_copy(k).start()

            @pl.when(jnp.logical_not(is_taken(s)))
            def _():
                sib_copy(i).wait()
                total = own[within(i, 4), pl.ds(core * high, high), :] + sib_in[within(i, near)].astype(F32)

                @pl.when(is_given(s))
                def _():
                    d = over(s, 2)
                    gift_out[d] = total.astype(BF16)
                    gift_copy(d).start()

                @pl.when(jnp.logical_not(is_given(s)))
                def _():
                    onward(total)

            @pl.when(is_taken(s))
            def _():
                d = s - start
                gift_copy(d).wait_recv()
                onward(gift_in[d].astype(F32))

        on = jnp.logical_not(is_given(t))
        r = chain_index(t) - lag
        slot = within(r, far)

        @pl.when(on & is_result(r))
        def _():
            mirror_copy(r).wait()

            @pl.when(middle)
            def _():
                tot_out[slot] = (up_out[slot].astype(F32) + ret_in[slot].astype(F32)).astype(BF16)

            @pl.when(jnp.logical_not(middle))
            def _():
                tot_out[slot] = ret_in[slot]

            @pl.when(has_outer)
            def _():
                ret_copy(r).start()

            @pl.when(is_taken(r))
            def _():
                back_copy(r, r - start).start()

            @pl.when(jnp.logical_not(is_taken(r)))
            def _():
                share_copy(r).start()
                store_own(r).start()

        r2 = r - 2

        @pl.when(on & is_result(r2) & jnp.logical_not(is_taken(r2)))
        def _():
            share_copy(r2).wait_recv()
            store_other(r2).start()

        r4 = r - 4

        @pl.when(on & is_result(r4))
        def _():
            @pl.when(has_outer)
            def _():
                ret_copy(r4).wait_send()

            @pl.when(is_taken(r4))
            def _():
                back_copy(r4, r4 - start).wait_send()

            @pl.when(jnp.logical_not(is_taken(r4)))
            def _():
                share_copy(r4).wait_send()
                store_own(r4).wait()
                store_other(r4).wait()

        d = t - LATE

        @pl.when((d >= 0) & (d < give))
        def _():
            gift_copy(d).wait_send()
            back_copy(r, d).wait_recv()
            back_share(d).start()
            store_back(d, back_in, core, 6).start()

        d2 = d - 2

        @pl.when((d2 >= 0) & (d2 < give))
        def _():
            back_share(d2).wait()
            store_back(d2, back_sib, 1 - core, 7).start()

        d4 = d - 4

        @pl.when((d4 >= 0) & (d4 < give))
        def _():
            store_back(d4, back_in, core, 6).wait()
            store_back(d4, back_sib, 1 - core, 7).wait()

        pl.when(t == 2 * gifts + 2)(lambda: homeward(lambda copy, far: copy.start()))
        small_step(t)

    small_out[...] = small[5] * (1.0 / math.sqrt(micro * rows * batches))

    small_sib().wait_send()
    small_up(3).wait_send()

    @pl.when(has_outer)
    def _():
        small_ret().wait_send()

    @pl.when(section != 0)
    def _():
        token_copy(section).wait_send()

    pl.when(section == 0)(lambda: side_copy().wait_send())

    @pl.when(section == 0)
    def _():
        for c in range(halves):
            around_last(c).wait_send()

    pl.when(section == last - 1)(lambda: side_last().wait_send())

    @pl.when((section != last) & (section != 0))
    def _():
        cot_copy(section).wait_send()

    for c in range(SENDS):

        @pl.when(section != last)
        def _():
            fwd_copy(0, c).wait_send()

        @pl.when(section != 0)
        def _():
            bwd_copy(0, c).wait_send()

    homeward(lambda copy, far: copy.wait_send() if far else copy.wait())

    @pl.when(section != last)
    def _():
        home_copy(x_out, final_out, 0, section).wait_recv()

    @pl.when(section != 0)
    def _():
        home_copy(dx_out, grad_out, 1, section).wait_recv()


def finish_kernel(scale, wide, small, final_in, grad_in, final, grad, weight, bias, gain, full, turned, sem):
    depth = wide.shape[1] // CUTS
    stores = []
    for n in range(wide.shape[0] * CUTS):
        j, span = n // CUTS, pl.ds((n % CUTS) * depth, depth)
        full[j, span, :] = wide[j, span, :].astype(F32) * scale
        stores.append(pltpu.make_async_copy(full.at[j, span], weight.at[0, j, span], sem.at[n]))
        stores[-1].start()
    order = order_matrix(PART, True)
    for k, (source, result) in enumerate(((final_in, final), (grad_in, grad))):
        for c in range(source.shape[1] // PART):
            span = slice(c * PART, (c + 1) * PART)
            turned[k, span, :] = dot(order, source[0, span, :]).astype(BF16)
        stores.append(pltpu.make_async_copy(turned.at[k], result.at[0], sem.at[len(stores)]))
        stores[-1].start()
    bias[0] = small[0:2, :]
    gain[...] = small[2:3, 0 : gain.shape[1]]
    for copy in stores:
        copy.wait()


def local(tokens, cotangent, weights, biases, gains, lengths):
    micro = lengths.shape[0]
    _, rows, width = tokens.shape
    hidden = weights.shape[3]
    parts = rows // PART
    pieces = 4 * width * hidden // (TILE[0] * TILE[1]) // 2
    any_spec = pl.BlockSpec(memory_space=pl.ANY)
    vmem = pl.BlockSpec(memory_space=pltpu.VMEM)
    dma = pltpu.SemaphoreType.DMA
    relay = pltpu.VMEM((micro, rows, width), BF16)
    near = min(8, pieces)
    far = 16
    close = pltpu.VMEM((near, *TILE), BF16)
    wait = pltpu.VMEM((far, *TILE), BF16)
    final, grad, wide, small = pl.pallas_call(
        relay_kernel,
        name="relay",
        out_shape=(
            pltpu.VMEM(tokens.shape, BF16),
            pltpu.VMEM(tokens.shape, BF16),
            pltpu.VMEM((4, width, hidden), BF16),
            pltpu.VMEM((8, hidden), F32),
        ),
        in_specs=[vmem, *[any_spec] * 5],
        out_specs=(vmem, vmem, vmem, vmem),
        scratch_shapes=[
            pltpu.VMEM((4, width, hidden), BF16),
            pltpu.VMEM((4, hidden, width), BF16),
            pltpu.VMEM((2, hidden), F32),
            pltpu.VMEM((1, width), F32),
            pltpu.VMEM((5, rows, width), BF16),
            relay,
            relay,
            relay,
            relay,
            pltpu.VMEM((micro, rows, 128), F32),
            pltpu.VMEM((micro, rows, 128), F32),
            pltpu.VMEM((micro * rows, width), BF16),
            pltpu.VMEM((micro * rows, width), BF16),
            pltpu.VMEM((4, micro * rows, hidden), BF16),
            pltpu.VMEM((4, micro * rows, hidden), F32),
            pltpu.VMEM((8, hidden), F32),
            pltpu.VMEM((8, hidden), F32),
            pltpu.VMEM((8, width), F32),
            pltpu.VMEM((2, 8, hidden), F32),
            close,
            close,
            pltpu.VMEM((4, 2 * TILE[0], TILE[1]), F32),
            wait,
            wait,
            wait,
            wait,
            close,
            pltpu.VMEM((6, 8, hidden), F32),
            pltpu.VMEM((2, width, micro * rows), BF16),
            *[pltpu.VMEM((max(GIVE), *TILE), BF16)] * 4,
            dma((8,)),
            dma((4 + 2 * micro,)),
            dma((SENDS,)),
            dma((micro, parts)),
            dma((SENDS,)),
            dma((micro, parts // PAIR)),
            dma((2, parts // PAIR)),
            dma((2, micro + 1)),
            dma((4, near)),
            dma((6, far)),
            dma((8, max(GIVE))),
            dma((6,)),
        ],
        compiler_params=pltpu.CompilerParams(
            collective_id=0, has_side_effects=True, vmem_limit_bytes=55 * 2**20
        ),
    )(lengths.T, tokens, cotangent, weights, biases, gains)
    scale = 1.0 / math.sqrt(micro * rows * lax.axis_size("batch"))
    return pl.pallas_call(
        functools.partial(finish_kernel, scale),
        name="finish",
        out_shape=(
            jax.ShapeDtypeStruct(tokens.shape, BF16),
            jax.ShapeDtypeStruct(tokens.shape, BF16),
            jax.ShapeDtypeStruct(weights.shape, F32),
            jax.ShapeDtypeStruct(biases.shape, F32),
            jax.ShapeDtypeStruct(gains.shape, F32),
        ),
        in_specs=[vmem, vmem, vmem, vmem],
        out_specs=(any_spec, any_spec, any_spec, vmem, vmem),
        scratch_shapes=[
            pltpu.VMEM((4, width, hidden), F32),
            pltpu.VMEM((2, rows, width), BF16),
            dma((4 * CUTS + 2,)),
        ],
        compiler_params=pltpu.CompilerParams(vmem_limit_bytes=24 * 2**20),
    )(*[pltpu.with_memory_space_constraint(value, pltpu.VMEM) for value in (wide, small, final, grad)])


def solution(mesh):
    row = P("section", "batch", None)
    placed = (
        row,
        row,
        P("section", None, None, None),
        P("section", None, None),
        P("section", None),
        P(None, "batch"),
    )
    return jax.shard_map(
        local,
        mesh=mesh,
        in_specs=placed,
        out_specs=(row, row, *placed[2:5]),
        check_vma=False,
    )
```

```python
import functools
import math

import jax
import jax.numpy as jnp
from jax import lax
from jax.experimental import pallas as pl
from jax.experimental.pallas import tpu as pltpu
from jax.sharding import PartitionSpec as P

MESH = pl.DeviceIdType.MESH
EPS = 1e-05
PART = 64
PAIR = 2
GIVE = (9, 2)
JOIN = (24, 14)
LATE = 34
NEXT = 3
LAG = 14
CUTS = 4
SENDS = 2
LANES = 256
TILE = (128, 256)
F32 = jnp.float32
BF16 = jnp.bfloat16


def dot(a, b):
    return jnp.dot(a, b, preferred_element_type=F32)


def over(value, count):
    return lax.shift_right_logical(value, count.bit_length() - 1)


def within(value, count):
    return lax.bitwise_and(value, count - 1)


def order_matrix(rows, back):
    new = lax.broadcasted_iota(jnp.int32, (rows, rows), 1 if back else 0)
    old = lax.broadcasted_iota(jnp.int32, (rows, rows), 0 if back else 1)
    hit = (within(new, 8) * (rows // 8) + over(new, 8)) == old
    return jnp.where(hit, 1.0, 0.0).astype(BF16)


def groups(value):
    return [value[8 * g : 8 * g + 8] for g in range(value.shape[0] // 8)]


def chain(gain, add, carry, back):
    row = lax.broadcasted_iota(jnp.int32, gain.shape, 0)
    for step in (1, 2, 4):
        shift = 8 - step if back else step
        inside = (row < 8 - step) if back else (row >= step)
        add = jnp.where(inside, gain * pltpu.roll(add, shift, 0) + add, add)
        gain = jnp.where(inside, gain * pltpu.roll(gain, shift, 0), gain)
    whole = gain * carry + add
    edge = 7 if back else 0
    enter = jnp.where(row == edge, carry, pltpu.roll(whole, 7 if back else 1, 0))
    last = whole[0:1] if back else whole[7:8]
    return enter, jnp.broadcast_to(last, gain.shape)


def relay_kernel(
    lengths,
    tokens,
    cotangent,
    weights,
    biases,
    gains,
    final_out,
    grad_out,
    wide_out,
    small_out,
    w,
    wt,
    bias,
    gain,
    stage,
    x_in,
    do_in,
    x_out,
    dx_out,
    valid_s,
    keep_s,
    normed,
    down,
    right,
    coef,
    h_carry,
    e_carry,
    gain_acc,
    bias_acc,
    sib_out,
    sib_in,
    own,
    up_out,
    up_in,
    ret_in,
    tot_out,
    tot_in,
    small,
    left,
    gift_out,
    gift_in,
    back_in,
    back_sib,
    load_sem,
    tok_sem,
    fwd_send,
    fwd_recv,
    bwd_send,
    bwd_recv,
    around_sem,
    home_sem,
    near_sem,
    far_sem,
    gift_sem,
    mid_sem,
    short_sem,
    small_sem,
):
    micro, rows, width = x_in.shape
    parts = rows // PART
    hidden = w.shape[2]
    section, batch = lax.axis_index("section"), lax.axis_index("batch")
    sections, batches = lax.axis_size("section"), lax.axis_size("batch")
    last = sections - 1
    mixer = lax.rem(section, 2) == 0
    feed = lax.rem(section, 2) == 1
    chips = batches // 2
    chip, core = batch // 2, lax.rem(batch, 2)
    sibling = batch + 1 - 2 * core
    half = chips // 2
    low_side = chip < half
    step_in = jnp.where(low_side, 2, -2)
    inner = batch + step_in
    outer = batch - step_in
    middle = (chip == half - 1) | (chip == half)
    has_outer = (chip > 0) & (chip < chips - 1)
    depth = jnp.where(low_side, half - 1 - chip, chip - half)

    def remote(src, dst, send, recv, to_section, to_batch):
        return pltpu.make_async_remote_copy(
            src_ref=src,
            dst_ref=dst,
            send_sem=send,
            recv_sem=recv,
            device_id=(to_section, to_batch),
            device_id_type=MESH,
        )

    sources = [
        (tokens.at[0], stage.at[0]),
        (cotangent.at[0], stage.at[1]),
        (biases.at[0], bias),
        (gains, gain),
        *[(weights.at[0, j], w.at[j]) for j in (3, 0, 1, 2)],
    ]
    loads = [pltpu.make_async_copy(src, dst, load_sem.at[i]) for i, (src, dst) in enumerate(sources)]
    for copy in loads:
        copy.start()

    barrier = pltpu.get_barrier_semaphore()
    for other in range(1, sections):
        pl.semaphore_signal(
            barrier, inc=1, device_id=(lax.rem(section + other, sections), batch), device_id_type=MESH
        )
    pl.semaphore_signal(barrier, inc=1, device_id=(section, sibling), device_id_type=MESH)
    pl.semaphore_signal(barrier, inc=1, device_id=(section, inner), device_id_type=MESH)

    @pl.when(has_outer)
    def _():
        pl.semaphore_signal(barrier, inc=1, device_id=(section, outer), device_id_type=MESH)

    spot = lax.broadcasted_iota(jnp.int32, (rows, 128), 0)
    spot_in = within(spot, PART)
    spot = spot - spot_in + within(spot_in, 8) * (PART // 8) + over(spot_in, 8)
    for m in range(micro):
        end = jnp.zeros((1, 1), jnp.int32)
        start_hit = jnp.zeros((rows, 128), F32)
        for k in range(lengths.shape[0]):
            start_hit = jnp.where(spot == end, 1.0, start_hit)
            end = end + lengths[k : k + 1, m : m + 1]
        valid = jnp.where(spot < end, 1.0, 0.0)
        valid_s[m] = valid
        keep_s[m] = valid * (1.0 - start_hit)
    h_carry[...] = jnp.zeros_like(h_carry)
    e_carry[...] = jnp.zeros_like(e_carry)
    gain_acc[...] = jnp.zeros_like(gain_acc)
    bias_acc[...] = jnp.zeros_like(bias_acc)

    perm = order_matrix(PART, False)
    loads[0].wait()
    for c in range(parts):
        span = pl.ds(c * PART, PART)
        ordered = dot(perm, stage[0, span, :]).astype(BF16)
        stage[2, span, :] = ordered

        @pl.when(section == 0)
        def _():
            x_in[0, span, :] = ordered

    loads[1].wait()
    for c in range(parts):
        span = pl.ds(c * PART, PART)
        ordered = dot(perm, stage[1, span, :]).astype(BF16)
        stage[3, span, :] = ordered

        @pl.when(section == last)
        def _():
            do_in[last, span, :] = ordered

    pl.semaphore_wait(barrier, sections + 1 + jnp.where(has_outer, 1, 0))

    def token_copy(m):
        return remote(stage.at[2], x_in.at[m], tok_sem.at[0], tok_sem.at[2 + m], 0, batch)

    def cot_copy(m):
        return remote(stage.at[3], do_in.at[m], tok_sem.at[1], tok_sem.at[2 + micro + m], last, batch)

    def side_copy():
        return remote(stage.at[3], stage.at[4], tok_sem.at[1], tok_sem.at[2 + 2 * micro], last - 1, batch)

    def side_last():
        return remote(stage.at[4], do_in.at[0], tok_sem.at[2 + 2 * micro + 1], tok_sem.at[2 + micro], last, batch)

    @pl.when(section != 0)
    def _():
        token_copy(section).start()

    pl.when(section == 0)(lambda: side_copy().start())

    @pl.when((section != last) & (section != 0))
    def _():
        cot_copy(section).start()

    for copy in loads[2:]:
        copy.wait()

    wt[3] = w[3].T

    def flip():
        for j in range(3):
            wt[j] = w[j].T

    pl.when(section > 0)(flip)

    @pl.when(section == last - 1)
    def _():
        side_copy().wait_recv()
        side_last().start()

    def wide(mask):
        return jnp.concatenate([mask] * (width // 128), axis=1)

    def slab(mask):
        return jnp.concatenate([mask] * (LANES // 128), axis=1)

    def fwd_copy(m, c):
        span = pl.ds(pl.multiple_of(c * PART, PART), PART)
        return remote(
            x_out.at[m, span],
            x_in.at[m, span],
            fwd_send.at[within(c, SENDS)],
            fwd_recv.at[m, c],
            jnp.minimum(section + 1, last),
            batch,
        )

    def bwd_copy(m, c):
        span = pl.ds(pl.multiple_of(c * PAIR * PART, PAIR * PART), PAIR * PART)
        return remote(
            dx_out.at[m, span],
            do_in.at[m, span],
            bwd_send.at[within(c, SENDS)],
            bwd_recv.at[m, c],
            jnp.maximum(section - 1, 0),
            batch,
        )

    def around_copy(c):
        span = pl.ds(pl.multiple_of(c * PAIR * PART, PAIR * PART), PAIR * PART)
        return remote(
            dx_out.at[0, span], stage.at[2, span], bwd_send.at[within(c, SENDS)], around_sem.at[0, c], 0, batch
        )

    def around_last(c):
        span = pl.ds(pl.multiple_of(c * PAIR * PART, PAIR * PART), PAIR * PART)
        return remote(stage.at[2, span], do_in.at[0, span], around_sem.at[1, c], bwd_recv.at[0, c], 1, batch)

    def home_copy(source, result, k, m):
        return remote(source.at[m], result.at[0], home_sem.at[k, m], home_sem.at[k, micro], m, batch)

    def keep_copy(source, result, k, m):
        return pltpu.make_async_copy(source.at[m], result.at[0], home_sem.at[k, m])

    high, broad = TILE
    down_n, across = width // high, hidden // broad
    pieces = 4 * down_n * across // 2
    near, far, gifts = sib_in.shape[0], up_in.shape[0], gift_in.shape[0]
    friend = last - section
    give = jnp.where(section == 0, GIVE[0], jnp.where(section == 1, GIVE[1], 0))
    take = jnp.where(friend == 0, GIVE[0], jnp.where(friend == 1, GIVE[1], 0))
    start = jnp.where(section == last, JOIN[0], JOIN[1])

    def place(piece):
        j = 3 - over(piece, down_n * across)
        rest = within(piece, down_n * across)
        row = pl.multiple_of(within(rest, down_n) * high, high)
        col = pl.multiple_of(over(rest, down_n) * broad, broad)
        return j, row, col

    def partial(t):
        j, row, col = place(2 * t)
        from_down = (j == 3) | (feed & (j == 2))
        return dot(left[jnp.where(from_down, 1, 0), pl.ds(row, 2 * high), :], right[j, :, pl.ds(col, broad)])

    def sib_copy(t):
        k = within(t, near)
        return remote(sib_out.at[k], sib_in.at[k], short_sem.at[0, within(t, 4)], near_sem.at[0, k], section, sibling)

    def make(i):
        own[within(i, 4)] = partial(i)
        sib_out[within(i, near)] = own[within(i, 4), pl.ds((1 - core) * high, high), :].astype(BF16)
        sib_copy(i).start()

    def first_tiles():
        left[1] = down[...].T

        @pl.loop(0, NEXT)
        def _(t):
            make(t)

    def forward(m, c, count):
        size = count * PART
        span = pl.ds(pl.multiple_of(c * size, size), size)
        line = pl.ds(pl.multiple_of(m * rows + c * size, size), size)

        @pl.when(section > 0)
        def _():
            for k in range(count):
                fwd_copy(m, c * count + k).wait_recv()

        @pl.when((section == 0) & (c == 0) & (m > 0))
        def _():
            token_copy(m).wait_recv()

        x = x_in[m, span, :].astype(F32)
        valid = valid_s[m, span, :]
        scale = lax.rsqrt(jnp.mean(x * x, axis=-1, keepdims=True) + EPS)
        nb = (x * scale * gain[...]).astype(BF16)
        normed[line, :] = nb

        def mix():
            keep_l = slab(keep_s[m, span, :])
            valid_l = slab(valid)
            for blk in range(hidden // LANES):
                cols = slice(blk * LANES, (blk + 1) * LANES)
                zf = dot(nb, w[0, :, cols]) + bias[0:1, cols]
                zi = dot(nb, w[1, :, cols]) + bias[1:2, cols]
                zh = dot(nb, w[2, :, cols])
                low = jnp.minimum(jnp.minimum(zf, zi), 0.0)
                e0 = jnp.exp(low)
                ei, ef = jnp.exp(low - zi), jnp.exp(low - zf)
                top, bot = e0 + ei, e0 + ef
                inv = 1.0 / (top + bot)
                decay = top * inv
                admit = bot * inv
                a = keep_l * decay
                iv = valid_l * admit
                b = iv * zh
                a_g, b_g = groups(a), groups(b)
                state, product = b_g[0], a_g[0]
                states, products = [state], [product]
                for g in range(1, len(a_g)):
                    state = a_g[g] * state + b_g[g]
                    product = a_g[g] * product
                    states.append(state)
                    products.append(product)
                enter, leave = chain(product, state, h_carry[:, cols], False)
                h_carry[:, cols] = leave
                hs = [s + p * enter for s, p in zip(states, products)]
                h_prev = jnp.concatenate([enter] + hs[:-1], axis=0)
                right[3, line, cols] = jnp.concatenate(hs, axis=0).astype(BF16)
                turn = (keep_l * h_prev - valid_l * zh) * inv
                coef[0, line, cols] = a
                coef[1, line, cols] = decay * ef * turn
                coef[2, line, cols] = -admit * ei * turn
                coef[3, line, cols] = iv
            y = dot(right[3, line, :], wt[3])
            x_out[m, span, :] = (x + wide(valid) * y).astype(BF16)

        def feed_on():
            for k in range(2):
                for blk in range(hidden // LANES):
                    cols = slice(blk * LANES, (blk + 1) * LANES)
                    u = dot(nb, w[k, :, cols]) + bias[k : k + 1, cols]
                    phi = 0.5 + 0.5 * lax.erf(u * math.sqrt(0.5))
                    right[2 + k, line, cols] = (u * phi).astype(BF16)
                    coef[k, line, cols] = phi + u * jnp.exp(-0.5 * u * u) * (1.0 / math.sqrt(2.0 * math.pi))
            y = dot(right[2, line, :], wt[2]) + dot(right[3, line, :], wt[3])
            x_out[m, span, :] = (x + wide(valid) * y).astype(BF16)

        if count == 1:
            pl.when(mixer)(mix)
            pl.when(feed)(feed_on)

            @pl.when(m * parts + c >= SENDS)
            def _():
                fwd_copy(m, c).wait_send()

            fwd_copy(m, c).start()
        else:
            feed_on()
            x_out[m, span, :] = (x_out[m, span, :].astype(F32) * wide(valid)).astype(BF16)

    def backward(m, c):
        size = PAIR * PART
        span = pl.ds(pl.multiple_of(c * size, size), size)
        line = pl.ds(pl.multiple_of(m * rows + c * size, size), size)

        @pl.when(section < last)
        def _():
            bwd_copy(m, c).wait_recv()

        @pl.when((section == last) & (c == 0) & (m != last))
        def _():
            cot_copy(m).wait_recv()

        do = do_in[m, span, :].astype(F32) * wide(valid_s[m, span, :])
        dy = do.astype(BF16)
        down[line, :] = dy
        pl.when((section == 0) & (m == micro - 1) & (c == 0))(first_tiles)

        @pl.when(mixer)
        def _():
            for blk in range(hidden // LANES):
                cols = slice(blk * LANES, (blk + 1) * LANES)
                d_all, a_all = dot(dy, w[3, :, cols]), coef[0, line, cols]
                pieces_dh = []
                for part in range(PAIR - 1, -1, -1):
                    spot = slice(part * PART, (part + 1) * PART)
                    d_g, a_g = groups(d_all[spot]), groups(a_all[spot])
                    count = len(a_g)
                    dhs, spread = [None] * count, [None] * count
                    dhs[-1] = d_g[-1]
                    for g in range(count - 2, -1, -1):
                        dhs[g] = d_g[g] + a_g[g + 1] * dhs[g + 1]
                        spread[g] = a_g[g + 1] if g == count - 2 else a_g[g + 1] * spread[g + 1]
                    enter, leave = chain(a_g[0] * spread[0], a_g[0] * dhs[0], e_carry[:, cols], True)
                    e_carry[:, cols] = leave
                    dhs = [d + s * enter for d, s in zip(dhs[:-1], spread[:-1])] + [dhs[-1] + enter]
                    pieces_dh = dhs + pieces_dh
                dh = jnp.concatenate(pieces_dh, axis=0)
                for j in range(3):
                    dz = dh * coef[1 + j, line, cols]
                    right[j, line, cols] = dz.astype(BF16)
                    if j < 2:
                        bias_acc[j, :, cols] += sum(groups(dz))

        @pl.when(feed)
        def _():
            for k in range(2):
                for blk in range(hidden // LANES):
                    cols = slice(blk * LANES, (blk + 1) * LANES)
                    du = dot(dy, w[2 + k, :, cols]) * coef[k, line, cols]
                    right[k, line, cols] = du.astype(BF16)
                    bias_acc[k, :, cols] += sum(groups(du))

        def finish(dn):
            x = x_in[m, span, :].astype(F32)
            scale = lax.rsqrt(jnp.mean(x * x, axis=-1, keepdims=True) + EPS)
            xr = x * scale
            part = dn * xr
            gain_acc[...] += sum(groups(part))
            dng = dn * gain[...]
            mean = jnp.mean(dng * xr, axis=-1, keepdims=True)
            dx_out[m, span, :] = (do + scale * (dng - xr * mean)).astype(BF16)

        @pl.when(mixer)
        def _():
            finish(
                dot(right[0, line, :], wt[0])
                + dot(right[1, line, :], wt[1])
                + dot(right[2, line, :], wt[2])
            )

        @pl.when(feed)
        def _():
            finish(dot(right[0, line, :], wt[0]) + dot(right[1, line, :], wt[1]))

        @pl.when(section > 0)
        def _():
            @pl.when((m > 0) if SENDS >= parts // PAIR else (m * (parts // PAIR) + parts // PAIR - 1 - c >= SENDS))
            def _():
                bwd_copy(m, c).wait_send()

            by_side = (section == 2) & (m == 0)
            pl.when(by_side)(lambda: around_copy(c).start())
            pl.when(jnp.logical_not(by_side))(lambda: bwd_copy(m, c).start())

    halves = parts // PAIR

    @pl.loop(0, micro * (parts + halves))
    def _(step):
        pl.when((section == 0) & (step == parts))(flip)

        @pl.when(step == micro * parts + halves + 1)
        def _():
            left[0] = normed[...].T


        early = (section == 2) & (step >= (micro - 1) * parts)
        back_now = jnp.where(early, step < (micro - 1) * parts + halves, step >= micro * parts)
        back_now = back_now | (step >= micro * parts + halves)
        f_step = jnp.where(early, step - halves, step)
        late = jnp.where(early & (step < (micro - 1) * parts + halves), step - (micro - 1) * parts, step - micro * parts)

        @pl.when((section < last) & jnp.logical_not(back_now))
        def _():
            forward(over(f_step, parts), within(f_step, parts), 1)

        turn = over(step, 2)

        @pl.when((section == 0) & (step == micro * parts))
        def _():
            for c in range(halves - 1, -1, -1):
                around_copy(c).wait_recv()
                around_last(c).start()

        @pl.when((section == last) & (within(step, 2) == 0) & (turn < micro * halves))
        def _():
            forward(over(turn, halves), within(turn, halves), PAIR)

        @pl.when(jnp.where(section == last, (within(step, 2) == 1) & (turn < micro * halves), back_now))
        def _():
            q = jnp.where(section == last, turn, jnp.maximum(late, 0))
            c = within(q, halves)
            backward(over(q, halves), jnp.where(section == last, c, halves - 1 - c))

    def homeward(act):
        for m in range(micro):
            for k, source, result, at in ((0, x_out, final_out, last), (1, dx_out, grad_out, 0)):

                @pl.when((section == at) & (section != m))
                def _():
                    act(home_copy(source, result, k, m), True)

                @pl.when((section == at) & (section == m))
                def _():
                    act(keep_copy(source, result, k, m), False)

    def is_given(t):
        return (within(t, 2) == 1) & (over(t, 2) < give)

    def chain_index(t):
        return t - jnp.minimum(over(t, 2), give)

    def is_taken(t):
        return (t >= start) & (t < start + take)

    def own_index(t):
        return t - jnp.clip(t - start, 0, take)

    def gift_copy(d):
        return remote(gift_out.at[d], gift_in.at[d], gift_sem.at[0, d], gift_sem.at[1, d], friend, batch)

    def back_copy(r, d):
        return remote(
            tot_out.at[within(r, far)], back_in.at[d], mid_sem.at[3, within(d, 8)], gift_sem.at[2, d], friend, batch
        )

    def back_share(d):
        return remote(
            back_in.at[d], back_sib.at[d], short_sem.at[2, within(d, 4)], gift_sem.at[3, d], section, sibling
        )

    def store_back(d, source, who, sem):
        j, row, col = place(4 * d + 2 + who)
        return pltpu.make_async_copy(
            source.at[d], wide_out.at[j, pl.ds(row, high), pl.ds(col, broad)], sem
        )

    def up_copy(k):
        k = within(k, far)
        return remote(up_out.at[k], up_in.at[k], far_sem.at[0, k], far_sem.at[1, k], section, inner)

    def mirror_copy(k):
        k = within(k, far)
        return remote(up_out.at[k], ret_in.at[k], far_sem.at[0, k], far_sem.at[2, k], section, inner)

    def ret_copy(k):
        k = within(k, far)
        return remote(tot_out.at[k], ret_in.at[k], mid_sem.at[0, within(k, 8)], far_sem.at[2, k], section, outer)

    def share_copy(r):
        k, at = within(r, far), within(own_index(r), near)
        return remote(tot_out.at[k], tot_in.at[at], mid_sem.at[1, within(r, 8)], near_sem.at[1, at], section, sibling)

    def piece_of(r):
        return jnp.where(r < give, 2 * r, own_index(r) + give)

    def store_own(r):
        j, row, col = place(2 * piece_of(r) + core)
        k = within(r, far)
        return pltpu.make_async_copy(
            tot_out.at[k], wide_out.at[j, pl.ds(row, high), pl.ds(col, broad)], mid_sem.at[2, within(r, 8)]
        )

    def store_other(r):
        j, row, col = place(2 * piece_of(r) + 1 - core)
        k = within(own_index(r), near)
        return pltpu.make_async_copy(
            tot_in.at[k], wide_out.at[j, pl.ds(row, high), pl.ds(col, broad)], short_sem.at[1, within(k, 4)]
        )

    def is_result(r):
        return (r >= 0) & (r < pieces - give + take)

    lag = jnp.minimum(NEXT + 3 + 8 * depth, LAG)
    small_at = NEXT + 4 + 4 * (half - 1 - depth)
    small_back = NEXT + 4 + 4 * half + 4 * depth

    for k in range(2):
        small[0, k : k + 1, :] = jnp.sum(bias_acc[k], axis=0, keepdims=True)
    small[0, 2:3, 0:width] = jnp.sum(gain_acc[...], axis=0, keepdims=True)
    small[0, 2:3, width:] = jnp.zeros((1, hidden - width), F32)
    small[0, 3:8, :] = jnp.zeros((5, hidden), F32)

    def small_sib():
        return remote(small.at[0], small.at[1], small_sem.at[0], small_sem.at[1], section, sibling)

    def small_up(to):
        return remote(small.at[2], small.at[to], small_sem.at[2], small_sem.at[to], section, inner)

    def small_ret():
        return remote(small.at[5], small.at[4], small_sem.at[5], small_sem.at[4], section, outer)

    def small_step(t):
        @pl.when(t == NEXT)
        def _():
            small_sib().start()

        @pl.when(t == small_at)
        def _():
            small_sib().wait_recv()
            small[2] = small[0] + small[1]

            @pl.when(has_outer)
            def _():
                small_up(3).wait_recv()
                small[2] = small[2] + small[3]

            @pl.when(middle)
            def _():
                small_up(4).start()

            @pl.when(jnp.logical_not(middle))
            def _():
                small_up(3).start()

        @pl.when(t == small_back)
        def _():
            small_up(4).wait_recv()

            @pl.when(middle)
            def _():
                small[5] = small[2] + small[4]

            @pl.when(jnp.logical_not(middle))
            def _():
                small[5] = small[4]

            @pl.when(has_outer)
            def _():
                small_ret().start()

    pl.when(section > 0)(first_tiles)

    end = jnp.maximum(pieces + take + lag + 5, jnp.maximum(small_back + 1, LATE + give + 4))

    @pl.loop(NEXT, end)
    def _(t):
        @pl.when((t < pieces + take) & jnp.logical_not(is_taken(t)))
        def _():
            make(own_index(t))

        s = t - NEXT

        @pl.when((s >= 0) & (s < pieces + take))
        def _():
            i = own_index(s)
            k = chain_index(s)
            slot = within(k, far)

            def onward(total):
                @pl.when(has_outer)
                def _():
                    up_copy(k).wait_recv()
                    up_out[slot] = (total + up_in[slot].astype(F32)).astype(BF16)

                @pl.when(jnp.logical_not(has_outer))
                def _():
                    up_out[slot] = total.astype(BF16)

                @pl.when(middle)
                def _():
                    mirror_copy(k).start()

                @pl.when(jnp.logical_not(middle))
                def _():
                    up_copy(k).start()

            @pl.when(jnp.logical_not(is_taken(s)))
            def _():
                sib_copy(i).wait()
                total = own[within(i, 4), pl.ds(core * high, high), :] + sib_in[within(i, near)].astype(F32)

                @pl.when(is_given(s))
                def _():
                    d = over(s, 2)
                    gift_out[d] = total.astype(BF16)
                    gift_copy(d).start()

                @pl.when(jnp.logical_not(is_given(s)))
                def _():
                    onward(total)

            @pl.when(is_taken(s))
            def _():
                d = s - start
                gift_copy(d).wait_recv()
                onward(gift_in[d].astype(F32))

        on = jnp.logical_not(is_given(t))
        r = chain_index(t) - lag
        slot = within(r, far)

        @pl.when(on & is_result(r))
        def _():
            mirror_copy(r).wait()

            @pl.when(middle)
            def _():
                tot_out[slot] = (up_out[slot].astype(F32) + ret_in[slot].astype(F32)).astype(BF16)

            @pl.when(jnp.logical_not(middle))
            def _():
                tot_out[slot] = ret_in[slot]

            @pl.when(has_outer)
            def _():
                ret_copy(r).start()

            @pl.when(is_taken(r))
            def _():
                back_copy(r, r - start).start()

            @pl.when(jnp.logical_not(is_taken(r)))
            def _():
                share_copy(r).start()
                store_own(r).start()

        r2 = r - 2

        @pl.when(on & is_result(r2) & jnp.logical_not(is_taken(r2)))
        def _():
            share_copy(r2).wait_recv()
            store_other(r2).start()

        r4 = r - 4

        @pl.when(on & is_result(r4))
        def _():
            @pl.when(has_outer)
            def _():
                ret_copy(r4).wait_send()

            @pl.when(is_taken(r4))
            def _():
                back_copy(r4, r4 - start).wait_send()

            @pl.when(jnp.logical_not(is_taken(r4)))
            def _():
                share_copy(r4).wait_send()
                store_own(r4).wait()
                store_other(r4).wait()

        d = t - LATE

        @pl.when((d >= 0) & (d < give))
        def _():
            gift_copy(d).wait_send()
            back_copy(r, d).wait_recv()
            back_share(d).start()
            store_back(d, back_in, core, mid_sem.at[4, within(d, 8)]).start()

        d2 = d - 2

        @pl.when((d2 >= 0) & (d2 < give))
        def _():
            back_share(d2).wait()
            store_back(d2, back_sib, 1 - core, short_sem.at[3, within(d2, 4)]).start()

        d4 = d - 4

        @pl.when((d4 >= 0) & (d4 < give))
        def _():
            store_back(d4, back_in, core, mid_sem.at[4, within(d4, 8)]).wait()
            store_back(d4, back_sib, 1 - core, short_sem.at[3, within(d4, 4)]).wait()

        pl.when(t == 2 * gifts + 2)(lambda: homeward(lambda copy, far: copy.start()))
        small_step(t)

    small_out[...] = small[5] * (1.0 / math.sqrt(micro * rows * batches))

    small_sib().wait_send()
    small_up(3).wait_send()

    @pl.when(has_outer)
    def _():
        small_ret().wait_send()

    @pl.when(section != 0)
    def _():
        token_copy(section).wait_send()

    pl.when(section == 0)(lambda: side_copy().wait_send())

    @pl.when(section == 0)
    def _():
        for c in range(halves):
            around_last(c).wait_send()

    pl.when(section == last - 1)(lambda: side_last().wait_send())

    @pl.when((section != last) & (section != 0))
    def _():
        cot_copy(section).wait_send()

    for c in range(SENDS):

        @pl.when(section != last)
        def _():
            fwd_copy(0, c).wait_send()

        @pl.when(section != 0)
        def _():
            bwd_copy(0, c).wait_send()

    homeward(lambda copy, far: copy.wait_send() if far else copy.wait())

    @pl.when(section != last)
    def _():
        home_copy(x_out, final_out, 0, section).wait_recv()

    @pl.when(section != 0)
    def _():
        home_copy(dx_out, grad_out, 1, section).wait_recv()


def finish_kernel(scale, wide, small, final_in, grad_in, final, grad, weight, bias, gain, full, turned, sem):
    depth = wide.shape[1] // CUTS
    stores = []
    for n in range(wide.shape[0] * CUTS):
        j, span = n // CUTS, pl.ds((n % CUTS) * depth, depth)
        full[j, span, :] = wide[j, span, :].astype(F32) * scale
        stores.append(pltpu.make_async_copy(full.at[j, span], weight.at[0, j, span], sem.at[n]))
        stores[-1].start()
    order = order_matrix(PART, True)
    for k, (source, result) in enumerate(((final_in, final), (grad_in, grad))):
        for c in range(source.shape[1] // PART):
            span = slice(c * PART, (c + 1) * PART)
            turned[k, span, :] = dot(order, source[0, span, :]).astype(BF16)
        stores.append(pltpu.make_async_copy(turned.at[k], result.at[0], sem.at[len(stores)]))
        stores[-1].start()
    bias[0] = small[0:2, :]
    gain[...] = small[2:3, 0 : gain.shape[1]]
    for copy in stores:
        copy.wait()


def local(tokens, cotangent, weights, biases, gains, lengths):
    micro = lengths.shape[0]
    _, rows, width = tokens.shape
    hidden = weights.shape[3]
    parts = rows // PART
    pieces = 4 * width * hidden // (TILE[0] * TILE[1]) // 2
    any_spec = pl.BlockSpec(memory_space=pl.ANY)
    vmem = pl.BlockSpec(memory_space=pltpu.VMEM)
    dma = pltpu.SemaphoreType.DMA
    relay = pltpu.VMEM((micro, rows, width), BF16)
    near = min(8, pieces)
    far = 16
    close = pltpu.VMEM((near, *TILE), BF16)
    wait = pltpu.VMEM((far, *TILE), BF16)
    final, grad, wide, small = pl.pallas_call(
        relay_kernel,
        name="relay",
        out_shape=(
            pltpu.VMEM(tokens.shape, BF16),
            pltpu.VMEM(tokens.shape, BF16),
            pltpu.VMEM((4, width, hidden), BF16),
            pltpu.VMEM((8, hidden), F32),
        ),
        in_specs=[vmem, *[any_spec] * 5],
        out_specs=(vmem, vmem, vmem, vmem),
        scratch_shapes=[
            pltpu.VMEM((4, width, hidden), BF16),
            pltpu.VMEM((4, hidden, width), BF16),
            pltpu.VMEM((2, hidden), F32),
            pltpu.VMEM((1, width), F32),
            pltpu.VMEM((5, rows, width), BF16),
            relay,
            relay,
            relay,
            relay,
            pltpu.VMEM((micro, rows, 128), F32),
            pltpu.VMEM((micro, rows, 128), F32),
            pltpu.VMEM((micro * rows, width), BF16),
            pltpu.VMEM((micro * rows, width), BF16),
            pltpu.VMEM((4, micro * rows, hidden), BF16),
            pltpu.VMEM((4, micro * rows, hidden), F32),
            pltpu.VMEM((8, hidden), F32),
            pltpu.VMEM((8, hidden), F32),
            pltpu.VMEM((8, width), F32),
            pltpu.VMEM((2, 8, hidden), F32),
            close,
            close,
            pltpu.VMEM((4, 2 * TILE[0], TILE[1]), F32),
            wait,
            wait,
            wait,
            wait,
            close,
            pltpu.VMEM((6, 8, hidden), F32),
            pltpu.VMEM((2, width, micro * rows), BF16),
            *[pltpu.VMEM((max(GIVE), *TILE), BF16)] * 4,
            dma((8,)),
            dma((4 + 2 * micro,)),
            dma((SENDS,)),
            dma((micro, parts)),
            dma((SENDS,)),
            dma((micro, parts // PAIR)),
            dma((2, parts // PAIR)),
            dma((2, micro + 1)),
            dma((2, near)),
            dma((3, far)),
            dma((4, max(GIVE))),
            dma((5, 8)),
            dma((4, 4)),
            dma((6,)),
        ],
        compiler_params=pltpu.CompilerParams(
            collective_id=0, has_side_effects=True, vmem_limit_bytes=55 * 2**20
        ),
    )(lengths.T, tokens, cotangent, weights, biases, gains)
    scale = 1.0 / math.sqrt(micro * rows * lax.axis_size("batch"))
    return pl.pallas_call(
        functools.partial(finish_kernel, scale),
        name="finish",
        out_shape=(
            jax.ShapeDtypeStruct(tokens.shape, BF16),
            jax.ShapeDtypeStruct(tokens.shape, BF16),
            jax.ShapeDtypeStruct(weights.shape, F32),
            jax.ShapeDtypeStruct(biases.shape, F32),
            jax.ShapeDtypeStruct(gains.shape, F32),
        ),
        in_specs=[vmem, vmem, vmem, vmem],
        out_specs=(any_spec, any_spec, any_spec, vmem, vmem),
        scratch_shapes=[
            pltpu.VMEM((4, width, hidden), F32),
            pltpu.VMEM((2, rows, width), BF16),
            dma((4 * CUTS + 2,)),
        ],
        compiler_params=pltpu.CompilerParams(vmem_limit_bytes=24 * 2**20),
    )(*[pltpu.with_memory_space_constraint(value, pltpu.VMEM) for value in (wide, small, final, grad)])


def solution(mesh):
    row = P("section", "batch", None)
    placed = (
        row,
        row,
        P("section", None, None, None),
        P("section", None, None),
        P("section", None),
        P(None, "batch"),
    )
    return jax.shard_map(
        local,
        mesh=mesh,
        in_specs=placed,
        out_specs=(row, row, *placed[2:5]),
        check_vma=False,
    )
```

```python
import functools
import math

import jax
import jax.numpy as jnp
from jax import lax
from jax.experimental import pallas as pl
from jax.experimental.pallas import tpu as pltpu
from jax.sharding import PartitionSpec as P

MESH = pl.DeviceIdType.MESH
EPS = 1e-05
PART = 64
PAIR = 2
GIVE = (9, 2)
JOIN = (24, 14)
LATE = 34
NEXT = 3
LAG = 14
CUTS = 4
SENDS = 2
LANES = 256
TILE = (128, 256)
F32 = jnp.float32
BF16 = jnp.bfloat16


def dot(a, b):
    return jnp.dot(a, b, preferred_element_type=F32)


def over(value, count):
    return lax.shift_right_logical(value, count.bit_length() - 1)


def within(value, count):
    return lax.bitwise_and(value, count - 1)


def order_matrix(rows, back):
    new = lax.broadcasted_iota(jnp.int32, (rows, rows), 1 if back else 0)
    old = lax.broadcasted_iota(jnp.int32, (rows, rows), 0 if back else 1)
    hit = (within(new, 8) * (rows // 8) + over(new, 8)) == old
    return jnp.where(hit, 1.0, 0.0).astype(BF16)


def groups(value):
    return [value[8 * g : 8 * g + 8] for g in range(value.shape[0] // 8)]


def chain(gain, add, carry, back):
    row = lax.broadcasted_iota(jnp.int32, gain.shape, 0)
    for step in (1, 2, 4):
        shift = 8 - step if back else step
        inside = (row < 8 - step) if back else (row >= step)
        add = jnp.where(inside, gain * pltpu.roll(add, shift, 0) + add, add)
        gain = jnp.where(inside, gain * pltpu.roll(gain, shift, 0), gain)
    whole = gain * carry + add
    edge = 7 if back else 0
    enter = jnp.where(row == edge, carry, pltpu.roll(whole, 7 if back else 1, 0))
    last = whole[0:1] if back else whole[7:8]
    return enter, jnp.broadcast_to(last, gain.shape)


def relay_kernel(
    lengths_in,
    tokens,
    cotangent,
    weights,
    biases,
    gains,
    final_out,
    grad_out,
    wide_out,
    small_out,
    w,
    wt,
    lengths,
    bias,
    gain,
    stage,
    x_in,
    do_in,
    x_out,
    dx_out,
    valid_s,
    keep_s,
    normed,
    down,
    right,
    coef,
    h_carry,
    e_carry,
    gain_acc,
    bias_acc,
    sib_out,
    sib_in,
    own,
    up_out,
    up_in,
    ret_in,
    tot_out,
    tot_in,
    small,
    left,
    gift_out,
    gift_in,
    back_in,
    back_sib,
    load_sem,
    tok_sem,
    fwd_send,
    fwd_recv,
    bwd_send,
    bwd_recv,
    around_sem,
    home_sem,
    near_sem,
    far_sem,
    gift_sem,
    mid_sem,
    short_sem,
    small_sem,
):
    micro, rows, width = x_in.shape
    parts = rows // PART
    hidden = w.shape[2]
    section, batch = lax.axis_index("section"), lax.axis_index("batch")
    sections, batches = lax.axis_size("section"), lax.axis_size("batch")
    last = sections - 1
    mixer = lax.rem(section, 2) == 0
    feed = lax.rem(section, 2) == 1
    chips = batches // 2
    chip, core = batch // 2, lax.rem(batch, 2)
    sibling = batch + 1 - 2 * core
    half = chips // 2
    low_side = chip < half
    step_in = jnp.where(low_side, 2, -2)
    inner = batch + step_in
    outer = batch - step_in
    middle = (chip == half - 1) | (chip == half)
    has_outer = (chip > 0) & (chip < chips - 1)
    depth = jnp.where(low_side, half - 1 - chip, chip - half)

    def remote(src, dst, send, recv, to_section, to_batch):
        return pltpu.make_async_remote_copy(
            src_ref=src,
            dst_ref=dst,
            send_sem=send,
            recv_sem=recv,
            device_id=(to_section, to_batch),
            device_id_type=MESH,
        )

    sources = [
        (tokens.at[0], stage.at[0]),
        (cotangent.at[0], stage.at[1]),
        (lengths_in, lengths),
        (biases.at[0], bias),
        (gains, gain),
        *[(weights.at[0, j], w.at[j]) for j in (3, 0, 1, 2)],
    ]
    loads = [pltpu.make_async_copy(src, dst, load_sem.at[i]) for i, (src, dst) in enumerate(sources)]
    for copy in loads:
        copy.start()

    barrier = pltpu.get_barrier_semaphore()
    for other in range(1, sections):
        pl.semaphore_signal(
            barrier, inc=1, device_id=(lax.rem(section + other, sections), batch), device_id_type=MESH
        )
    pl.semaphore_signal(barrier, inc=1, device_id=(section, sibling), device_id_type=MESH)
    pl.semaphore_signal(barrier, inc=1, device_id=(section, inner), device_id_type=MESH)

    @pl.when(has_outer)
    def _():
        pl.semaphore_signal(barrier, inc=1, device_id=(section, outer), device_id_type=MESH)

    loads[2].wait()
    spot = lax.broadcasted_iota(jnp.int32, (rows, 128), 0)
    spot_in = within(spot, PART)
    spot = spot - spot_in + within(spot_in, 8) * (PART // 8) + over(spot_in, 8)
    for m in range(micro):
        end = jnp.zeros((1, 1), jnp.int32)
        start_hit = jnp.zeros((rows, 128), F32)
        for k in range(lengths.shape[0]):
            start_hit = jnp.where(spot == end, 1.0, start_hit)
            end = end + lengths[k : k + 1, m : m + 1]
        valid = jnp.where(spot < end, 1.0, 0.0)
        valid_s[m] = valid
        keep_s[m] = valid * (1.0 - start_hit)
    h_carry[...] = jnp.zeros_like(h_carry)
    e_carry[...] = jnp.zeros_like(e_carry)
    gain_acc[...] = jnp.zeros_like(gain_acc)
    bias_acc[...] = jnp.zeros_like(bias_acc)

    perm = order_matrix(PART, False)
    loads[0].wait()
    for c in range(parts):
        span = pl.ds(c * PART, PART)
        ordered = dot(perm, stage[0, span, :]).astype(BF16)
        stage[2, span, :] = ordered

        @pl.when(section == 0)
        def _():
            x_in[0, span, :] = ordered

    loads[1].wait()
    for c in range(parts):
        span = pl.ds(c * PART, PART)
        ordered = dot(perm, stage[1, span, :]).astype(BF16)
        stage[3, span, :] = ordered

        @pl.when(section == last)
        def _():
            do_in[last, span, :] = ordered

    pl.semaphore_wait(barrier, sections + 1 + jnp.where(has_outer, 1, 0))

    def token_copy(m):
        return remote(stage.at[2], x_in.at[m], tok_sem.at[0], tok_sem.at[2 + m], 0, batch)

    def cot_copy(m):
        return remote(stage.at[3], do_in.at[m], tok_sem.at[1], tok_sem.at[2 + micro + m], last, batch)

    def side_copy():
        return remote(stage.at[3], stage.at[4], tok_sem.at[1], tok_sem.at[2 + 2 * micro], last - 1, batch)

    def side_last():
        return remote(stage.at[4], do_in.at[0], tok_sem.at[2 + 2 * micro + 1], tok_sem.at[2 + micro], last, batch)

    @pl.when(section != 0)
    def _():
        token_copy(section).start()

    pl.when(section == 0)(lambda: side_copy().start())

    @pl.when((section != last) & (section != 0))
    def _():
        cot_copy(section).start()

    for copy in loads[3:]:
        copy.wait()

    wt[3] = w[3].T

    def flip():
        for j in range(3):
            wt[j] = w[j].T

    pl.when(section > 0)(flip)

    @pl.when(section == last - 1)
    def _():
        side_copy().wait_recv()
        side_last().start()

    def wide(mask):
        return jnp.concatenate([mask] * (width // 128), axis=1)

    def slab(mask):
        return jnp.concatenate([mask] * (LANES // 128), axis=1)

    def fwd_copy(m, c):
        span = pl.ds(pl.multiple_of(c * PART, PART), PART)
        return remote(
            x_out.at[m, span],
            x_in.at[m, span],
            fwd_send.at[within(c, SENDS)],
            fwd_recv.at[m, c],
            jnp.minimum(section + 1, last),
            batch,
        )

    def bwd_copy(m, c):
        span = pl.ds(pl.multiple_of(c * PAIR * PART, PAIR * PART), PAIR * PART)
        return remote(
            dx_out.at[m, span],
            do_in.at[m, span],
            bwd_send.at[within(c, SENDS)],
            bwd_recv.at[m, c],
            jnp.maximum(section - 1, 0),
            batch,
        )

    def around_copy(c):
        span = pl.ds(pl.multiple_of(c * PAIR * PART, PAIR * PART), PAIR * PART)
        return remote(
            dx_out.at[0, span], stage.at[2, span], bwd_send.at[within(c, SENDS)], around_sem.at[0, c], 0, batch
        )

    def around_last(c):
        span = pl.ds(pl.multiple_of(c * PAIR * PART, PAIR * PART), PAIR * PART)
        return remote(stage.at[2, span], do_in.at[0, span], around_sem.at[1, c], bwd_recv.at[0, c], 1, batch)

    def home_copy(source, result, k, m):
        return remote(source.at[m], result.at[0], home_sem.at[k, m], home_sem.at[k, micro], m, batch)

    def keep_copy(source, result, k, m):
        return pltpu.make_async_copy(source.at[m], result.at[0], home_sem.at[k, m])

    high, broad = TILE
    down_n, across = width // high, hidden // broad
    pieces = 4 * down_n * across // 2
    near, far, gifts = sib_in.shape[0], up_in.shape[0], gift_in.shape[0]
    friend = last - section
    give = jnp.where(section == 0, GIVE[0], jnp.where(section == 1, GIVE[1], 0))
    take = jnp.where(friend == 0, GIVE[0], jnp.where(friend == 1, GIVE[1], 0))
    start = jnp.where(section == last, JOIN[0], JOIN[1])

    def place(piece):
        j = 3 - over(piece, down_n * across)
        rest = within(piece, down_n * across)
        row = pl.multiple_of(within(rest, down_n) * high, high)
        col = pl.multiple_of(over(rest, down_n) * broad, broad)
        return j, row, col

    def partial(t):
        j, row, col = place(2 * t)
        from_down = (j == 3) | (feed & (j == 2))
        return dot(left[jnp.where(from_down, 1, 0), pl.ds(row, 2 * high), :], right[j, :, pl.ds(col, broad)])

    def sib_copy(t):
        k = within(t, near)
        return remote(sib_out.at[k], sib_in.at[k], short_sem.at[0, within(t, 4)], near_sem.at[0, k], section, sibling)

    def make(i):
        own[within(i, 4)] = partial(i)
        sib_out[within(i, near)] = own[within(i, 4), pl.ds((1 - core) * high, high), :].astype(BF16)
        sib_copy(i).start()

    def first_tiles():
        left[1] = down[...].T

        @pl.loop(0, NEXT)
        def _(t):
            make(t)

    def forward(m, c, count):
        size = count * PART
        span = pl.ds(pl.multiple_of(c * size, size), size)
        line = pl.ds(pl.multiple_of(m * rows + c * size, size), size)

        @pl.when(section > 0)
        def _():
            for k in range(count):
                fwd_copy(m, c * count + k).wait_recv()

        @pl.when((section == 0) & (c == 0) & (m > 0))
        def _():
            token_copy(m).wait_recv()

        x = x_in[m, span, :].astype(F32)
        valid = valid_s[m, span, :]
        scale = lax.rsqrt(jnp.mean(x * x, axis=-1, keepdims=True) + EPS)
        nb = (x * scale * gain[...]).astype(BF16)
        normed[line, :] = nb

        def mix():
            keep_l = slab(keep_s[m, span, :])
            valid_l = slab(valid)
            for blk in range(hidden // LANES):
                cols = slice(blk * LANES, (blk + 1) * LANES)
                zf = dot(nb, w[0, :, cols]) + bias[0:1, cols]
                zi = dot(nb, w[1, :, cols]) + bias[1:2, cols]
                zh = dot(nb, w[2, :, cols])
                low = jnp.minimum(jnp.minimum(zf, zi), 0.0)
                e0 = jnp.exp(low)
                ei, ef = jnp.exp(low - zi), jnp.exp(low - zf)
                top, bot = e0 + ei, e0 + ef
                inv = 1.0 / (top + bot)
                decay = top * inv
                admit = bot * inv
                a = keep_l * decay
                iv = valid_l * admit
                b = iv * zh
                a_g, b_g = groups(a), groups(b)
                state, product = b_g[0], a_g[0]
                states, products = [state], [product]
                for g in range(1, len(a_g)):
                    state = a_g[g] * state + b_g[g]
                    product = a_g[g] * product
                    states.append(state)
                    products.append(product)
                enter, leave = chain(product, state, h_carry[:, cols], False)
                h_carry[:, cols] = leave
                hs = [s + p * enter for s, p in zip(states, products)]
                h_prev = jnp.concatenate([enter] + hs[:-1], axis=0)
                right[3, line, cols] = jnp.concatenate(hs, axis=0).astype(BF16)
                turn = (keep_l * h_prev - valid_l * zh) * inv
                coef[0, line, cols] = a
                coef[1, line, cols] = decay * ef * turn
                coef[2, line, cols] = -admit * ei * turn
                coef[3, line, cols] = iv
            y = dot(right[3, line, :], wt[3])
            x_out[m, span, :] = (x + wide(valid) * y).astype(BF16)

        def feed_on():
            for k in range(2):
                for blk in range(hidden // LANES):
                    cols = slice(blk * LANES, (blk + 1) * LANES)
                    u = dot(nb, w[k, :, cols]) + bias[k : k + 1, cols]
                    phi = 0.5 + 0.5 * lax.erf(u * math.sqrt(0.5))
                    right[2 + k, line, cols] = (u * phi).astype(BF16)
                    coef[k, line, cols] = phi + u * jnp.exp(-0.5 * u * u) * (1.0 / math.sqrt(2.0 * math.pi))
            y = dot(right[2, line, :], wt[2]) + dot(right[3, line, :], wt[3])
            x_out[m, span, :] = (x + wide(valid) * y).astype(BF16)

        if count == 1:
            pl.when(mixer)(mix)
            pl.when(feed)(feed_on)

            @pl.when(m * parts + c >= SENDS)
            def _():
                fwd_copy(m, c).wait_send()

            fwd_copy(m, c).start()
        else:
            feed_on()
            x_out[m, span, :] = (x_out[m, span, :].astype(F32) * wide(valid)).astype(BF16)

    def backward(m, c):
        size = PAIR * PART
        span = pl.ds(pl.multiple_of(c * size, size), size)
        line = pl.ds(pl.multiple_of(m * rows + c * size, size), size)

        @pl.when(section < last)
        def _():
            bwd_copy(m, c).wait_recv()

        @pl.when((section == last) & (c == 0) & (m != last))
        def _():
            cot_copy(m).wait_recv()

        do = do_in[m, span, :].astype(F32) * wide(valid_s[m, span, :])
        dy = do.astype(BF16)
        down[line, :] = dy
        pl.when((section == 0) & (m == micro - 1) & (c == 0))(first_tiles)

        @pl.when(mixer)
        def _():
            for blk in range(hidden // LANES):
                cols = slice(blk * LANES, (blk + 1) * LANES)
                d_all, a_all = dot(dy, w[3, :, cols]), coef[0, line, cols]
                pieces_dh = []
                for part in range(PAIR - 1, -1, -1):
                    spot = slice(part * PART, (part + 1) * PART)
                    d_g, a_g = groups(d_all[spot]), groups(a_all[spot])
                    count = len(a_g)
                    dhs, spread = [None] * count, [None] * count
                    dhs[-1] = d_g[-1]
                    for g in range(count - 2, -1, -1):
                        dhs[g] = d_g[g] + a_g[g + 1] * dhs[g + 1]
                        spread[g] = a_g[g + 1] if g == count - 2 else a_g[g + 1] * spread[g + 1]
                    enter, leave = chain(a_g[0] * spread[0], a_g[0] * dhs[0], e_carry[:, cols], True)
                    e_carry[:, cols] = leave
                    dhs = [d + s * enter for d, s in zip(dhs[:-1], spread[:-1])] + [dhs[-1] + enter]
                    pieces_dh = dhs + pieces_dh
                dh = jnp.concatenate(pieces_dh, axis=0)
                for j in range(3):
                    dz = dh * coef[1 + j, line, cols]
                    right[j, line, cols] = dz.astype(BF16)
                    if j < 2:
                        bias_acc[j, :, cols] += sum(groups(dz))

        @pl.when(feed)
        def _():
            for k in range(2):
                for blk in range(hidden // LANES):
                    cols = slice(blk * LANES, (blk + 1) * LANES)
                    du = dot(dy, w[2 + k, :, cols]) * coef[k, line, cols]
                    right[k, line, cols] = du.astype(BF16)
                    bias_acc[k, :, cols] += sum(groups(du))

        def finish(dn):
            x = x_in[m, span, :].astype(F32)
            scale = lax.rsqrt(jnp.mean(x * x, axis=-1, keepdims=True) + EPS)
            xr = x * scale
            part = dn * xr
            gain_acc[...] += sum(groups(part))
            dng = dn * gain[...]
            mean = jnp.mean(dng * xr, axis=-1, keepdims=True)
            dx_out[m, span, :] = (do + scale * (dng - xr * mean)).astype(BF16)

        @pl.when(mixer)
        def _():
            finish(
                dot(right[0, line, :], wt[0])
                + dot(right[1, line, :], wt[1])
                + dot(right[2, line, :], wt[2])
            )

        @pl.when(feed)
        def _():
            finish(dot(right[0, line, :], wt[0]) + dot(right[1, line, :], wt[1]))

        @pl.when(section > 0)
        def _():
            @pl.when((m > 0) if SENDS >= parts // PAIR else (m * (parts // PAIR) + parts // PAIR - 1 - c >= SENDS))
            def _():
                bwd_copy(m, c).wait_send()

            by_side = (section == 2) & (m == 0)
            pl.when(by_side)(lambda: around_copy(c).start())
            pl.when(jnp.logical_not(by_side))(lambda: bwd_copy(m, c).start())

    halves = parts // PAIR

    @pl.loop(0, micro * (parts + halves))
    def _(step):
        pl.when((section == 0) & (step == parts))(flip)

        @pl.when(step == micro * parts + halves + 1)
        def _():
            left[0] = normed[...].T


        early = (section == 2) & (step >= (micro - 1) * parts)
        back_now = jnp.where(early, step < (micro - 1) * parts + halves, step >= micro * parts)
        back_now = back_now | (step >= micro * parts + halves)
        f_step = jnp.where(early, step - halves, step)
        late = jnp.where(early & (step < (micro - 1) * parts + halves), step - (micro - 1) * parts, step - micro * parts)

        @pl.when((section < last) & jnp.logical_not(back_now))
        def _():
            forward(over(f_step, parts), within(f_step, parts), 1)

        turn = over(step, 2)

        @pl.when((section == 0) & (step == micro * parts))
        def _():
            for c in range(halves - 1, -1, -1):
                around_copy(c).wait_recv()
                around_last(c).start()

        @pl.when((section == last) & (within(step, 2) == 0) & (turn < micro * halves))
        def _():
            forward(over(turn, halves), within(turn, halves), PAIR)

        @pl.when(jnp.where(section == last, (within(step, 2) == 1) & (turn < micro * halves), back_now))
        def _():
            q = jnp.where(section == last, turn, jnp.maximum(late, 0))
            c = within(q, halves)
            backward(over(q, halves), jnp.where(section == last, c, halves - 1 - c))

    def homeward(act):
        for m in range(micro):
            for k, source, result, at in ((0, x_out, final_out, last), (1, dx_out, grad_out, 0)):

                @pl.when((section == at) & (section != m))
                def _():
                    act(home_copy(source, result, k, m), True)

                @pl.when((section == at) & (section == m))
                def _():
                    act(keep_copy(source, result, k, m), False)

    def is_given(t):
        return (within(t, 2) == 1) & (over(t, 2) < give)

    def chain_index(t):
        return t - jnp.minimum(over(t, 2), give)

    def is_taken(t):
        return (t >= start) & (t < start + take)

    def own_index(t):
        return t - jnp.clip(t - start, 0, take)

    def gift_copy(d):
        return remote(gift_out.at[d], gift_in.at[d], gift_sem.at[0, d], gift_sem.at[1, d], friend, batch)

    def back_copy(r, d):
        return remote(
            tot_out.at[within(r, far)], back_in.at[d], mid_sem.at[3, within(d, 8)], gift_sem.at[2, d], friend, batch
        )

    def back_share(d):
        return remote(
            back_in.at[d], back_sib.at[d], short_sem.at[2, within(d, 4)], gift_sem.at[3, d], section, sibling
        )

    def store_back(d, source, who, sem):
        j, row, col = place(4 * d + 2 + who)
        return pltpu.make_async_copy(
            source.at[d], wide_out.at[j, pl.ds(row, high), pl.ds(col, broad)], sem
        )

    def up_copy(k):
        k = within(k, far)
        return remote(up_out.at[k], up_in.at[k], far_sem.at[0, k], far_sem.at[1, k], section, inner)

    def mirror_copy(k):
        k = within(k, far)
        return remote(up_out.at[k], ret_in.at[k], far_sem.at[0, k], far_sem.at[2, k], section, inner)

    def ret_copy(k):
        k = within(k, far)
        return remote(tot_out.at[k], ret_in.at[k], mid_sem.at[0, within(k, 8)], far_sem.at[2, k], section, outer)

    def share_copy(r):
        k, at = within(r, far), within(own_index(r), near)
        return remote(tot_out.at[k], tot_in.at[at], mid_sem.at[1, within(r, 8)], near_sem.at[1, at], section, sibling)

    def piece_of(r):
        return jnp.where(r < give, 2 * r, own_index(r) + give)

    def store_own(r):
        j, row, col = place(2 * piece_of(r) + core)
        k = within(r, far)
        return pltpu.make_async_copy(
            tot_out.at[k], wide_out.at[j, pl.ds(row, high), pl.ds(col, broad)], mid_sem.at[2, within(r, 8)]
        )

    def store_other(r):
        j, row, col = place(2 * piece_of(r) + 1 - core)
        k = within(own_index(r), near)
        return pltpu.make_async_copy(
            tot_in.at[k], wide_out.at[j, pl.ds(row, high), pl.ds(col, broad)], short_sem.at[1, within(k, 4)]
        )

    def is_result(r):
        return (r >= 0) & (r < pieces - give + take)

    lag = jnp.minimum(NEXT + 3 + 8 * depth, LAG)
    small_at = NEXT + 4 + 4 * (half - 1 - depth)
    small_back = NEXT + 4 + 4 * half + 4 * depth

    for k in range(2):
        small[0, k : k + 1, :] = jnp.sum(bias_acc[k], axis=0, keepdims=True)
    small[0, 2:3, 0:width] = jnp.sum(gain_acc[...], axis=0, keepdims=True)
    small[0, 2:3, width:] = jnp.zeros((1, hidden - width), F32)
    small[0, 3:8, :] = jnp.zeros((5, hidden), F32)

    def small_sib():
        return remote(small.at[0], small.at[1], small_sem.at[0], small_sem.at[1], section, sibling)

    def small_up(to):
        return remote(small.at[2], small.at[to], small_sem.at[2], small_sem.at[to], section, inner)

    def small_ret():
        return remote(small.at[5], small.at[4], small_sem.at[5], small_sem.at[4], section, outer)

    def small_step(t):
        @pl.when(t == NEXT)
        def _():
            small_sib().start()

        @pl.when(t == small_at)
        def _():
            small_sib().wait_recv()
            small[2] = small[0] + small[1]

            @pl.when(has_outer)
            def _():
                small_up(3).wait_recv()
                small[2] = small[2] + small[3]

            @pl.when(middle)
            def _():
                small_up(4).start()

            @pl.when(jnp.logical_not(middle))
            def _():
                small_up(3).start()

        @pl.when(t == small_back)
        def _():
            small_up(4).wait_recv()

            @pl.when(middle)
            def _():
                small[5] = small[2] + small[4]

            @pl.when(jnp.logical_not(middle))
            def _():
                small[5] = small[4]

            @pl.when(has_outer)
            def _():
                small_ret().start()

    pl.when(section > 0)(first_tiles)

    end = jnp.maximum(pieces + take + lag + 5, jnp.maximum(small_back + 1, LATE + give + 4))

    @pl.loop(NEXT, end)
    def _(t):
        @pl.when((t < pieces + take) & jnp.logical_not(is_taken(t)))
        def _():
            make(own_index(t))

        s = t - NEXT

        @pl.when((s >= 0) & (s < pieces + take))
        def _():
            i = own_index(s)
            k = chain_index(s)
            slot = within(k, far)

            def onward(total):
                @pl.when(has_outer)
                def _():
                    up_copy(k).wait_recv()
                    up_out[slot] = (total + up_in[slot].astype(F32)).astype(BF16)

                @pl.when(jnp.logical_not(has_outer))
                def _():
                    up_out[slot] = total.astype(BF16)

                @pl.when(middle)
                def _():
                    mirror_copy(k).start()

                @pl.when(jnp.logical_not(middle))
                def _():
                    up_copy(k).start()

            @pl.when(jnp.logical_not(is_taken(s)))
            def _():
                sib_copy(i).wait()
                total = own[within(i, 4), pl.ds(core * high, high), :] + sib_in[within(i, near)].astype(F32)

                @pl.when(is_given(s))
                def _():
                    d = over(s, 2)
                    gift_out[d] = total.astype(BF16)
                    gift_copy(d).start()

                @pl.when(jnp.logical_not(is_given(s)))
                def _():
                    onward(total)

            @pl.when(is_taken(s))
            def _():
                d = s - start
                gift_copy(d).wait_recv()
                onward(gift_in[d].astype(F32))

        on = jnp.logical_not(is_given(t))
        r = chain_index(t) - lag
        slot = within(r, far)

        @pl.when(on & is_result(r))
        def _():
            mirror_copy(r).wait()

            @pl.when(middle)
            def _():
                tot_out[slot] = (up_out[slot].astype(F32) + ret_in[slot].astype(F32)).astype(BF16)

            @pl.when(jnp.logical_not(middle))
            def _():
                tot_out[slot] = ret_in[slot]

            @pl.when(has_outer)
            def _():
                ret_copy(r).start()

            @pl.when(is_taken(r))
            def _():
                back_copy(r, r - start).start()

            @pl.when(jnp.logical_not(is_taken(r)))
            def _():
                share_copy(r).start()
                store_own(r).start()

        r2 = r - 2

        @pl.when(on & is_result(r2) & jnp.logical_not(is_taken(r2)))
        def _():
            share_copy(r2).wait_recv()
            store_other(r2).start()

        r4 = r - 4

        @pl.when(on & is_result(r4))
        def _():
            @pl.when(has_outer)
            def _():
                ret_copy(r4).wait_send()

            @pl.when(is_taken(r4))
            def _():
                back_copy(r4, r4 - start).wait_send()

            @pl.when(jnp.logical_not(is_taken(r4)))
            def _():
                share_copy(r4).wait_send()
                store_own(r4).wait()
                store_other(r4).wait()

        d = t - LATE

        @pl.when((d >= 0) & (d < give))
        def _():
            gift_copy(d).wait_send()
            back_copy(r, d).wait_recv()
            back_share(d).start()
            store_back(d, back_in, core, mid_sem.at[4, within(d, 8)]).start()

        d2 = d - 2

        @pl.when((d2 >= 0) & (d2 < give))
        def _():
            back_share(d2).wait()
            store_back(d2, back_sib, 1 - core, short_sem.at[3, within(d2, 4)]).start()

        d4 = d - 4

        @pl.when((d4 >= 0) & (d4 < give))
        def _():
            store_back(d4, back_in, core, mid_sem.at[4, within(d4, 8)]).wait()
            store_back(d4, back_sib, 1 - core, short_sem.at[3, within(d4, 4)]).wait()

        pl.when(t == 2 * gifts + 2)(lambda: homeward(lambda copy, far: copy.start()))
        small_step(t)

    small_out[...] = small[5] * (1.0 / math.sqrt(micro * rows * batches))

    small_sib().wait_send()
    small_up(3).wait_send()

    @pl.when(has_outer)
    def _():
        small_ret().wait_send()

    @pl.when(section != 0)
    def _():
        token_copy(section).wait_send()

    pl.when(section == 0)(lambda: side_copy().wait_send())

    @pl.when(section == 0)
    def _():
        for c in range(halves):
            around_last(c).wait_send()

    pl.when(section == last - 1)(lambda: side_last().wait_send())

    @pl.when((section != last) & (section != 0))
    def _():
        cot_copy(section).wait_send()

    for c in range(SENDS):

        @pl.when(section != last)
        def _():
            fwd_copy(0, c).wait_send()

        @pl.when(section != 0)
        def _():
            bwd_copy(0, c).wait_send()

    homeward(lambda copy, far: copy.wait_send() if far else copy.wait())

    @pl.when(section != last)
    def _():
        home_copy(x_out, final_out, 0, section).wait_recv()

    @pl.when(section != 0)
    def _():
        home_copy(dx_out, grad_out, 1, section).wait_recv()


def finish_kernel(scale, wide, small, final_in, grad_in, final, grad, weight, bias, gain, full, turned, sums, norms, sem):
    depth = wide.shape[1] // CUTS
    stores = []
    for n in range(wide.shape[0] * CUTS):
        j, span = n // CUTS, pl.ds((n % CUTS) * depth, depth)
        full[j, span, :] = wide[j, span, :].astype(F32) * scale
        stores.append(pltpu.make_async_copy(full.at[j, span], weight.at[0, j, span], sem.at[n]))
        stores[-1].start()
    sums[0] = small[0:2, :]
    norms[...] = small[2:3, 0 : norms.shape[1]]
    for source, result in ((sums, bias), (norms, gain)):
        stores.append(pltpu.make_async_copy(source, result, sem.at[len(stores)]))
        stores[-1].start()
    order = order_matrix(PART, True)
    for k, (source, result) in enumerate(((final_in, final), (grad_in, grad))):
        for c in range(source.shape[1] // PART):
            span = slice(c * PART, (c + 1) * PART)
            turned[k, span, :] = dot(order, source[0, span, :]).astype(BF16)
        stores.append(pltpu.make_async_copy(turned.at[k], result.at[0], sem.at[len(stores)]))
        stores[-1].start()
    for copy in stores:
        copy.wait()


def local(tokens, cotangent, weights, biases, gains, lengths):
    micro = lengths.shape[0]
    _, rows, width = tokens.shape
    hidden = weights.shape[3]
    parts = rows // PART
    pieces = 4 * width * hidden // (TILE[0] * TILE[1]) // 2
    any_spec = pl.BlockSpec(memory_space=pl.ANY)
    vmem = pl.BlockSpec(memory_space=pltpu.VMEM)
    dma = pltpu.SemaphoreType.DMA
    relay = pltpu.VMEM((micro, rows, width), BF16)
    near = min(8, pieces)
    far = 16
    close = pltpu.VMEM((near, *TILE), BF16)
    wait = pltpu.VMEM((far, *TILE), BF16)
    final, grad, wide, small = pl.pallas_call(
        relay_kernel,
        name="relay",
        out_shape=(
            pltpu.VMEM(tokens.shape, BF16),
            pltpu.VMEM(tokens.shape, BF16),
            pltpu.VMEM((4, width, hidden), BF16),
            pltpu.VMEM((8, hidden), F32),
        ),
        in_specs=[any_spec] * 6,
        out_specs=(vmem, vmem, vmem, vmem),
        scratch_shapes=[
            pltpu.VMEM((4, width, hidden), BF16),
            pltpu.VMEM((4, hidden, width), BF16),
            pltpu.VMEM(lengths.shape[::-1], jnp.int32),
            pltpu.VMEM((2, hidden), F32),
            pltpu.VMEM((1, width), F32),
            pltpu.VMEM((5, rows, width), BF16),
            relay,
            relay,
            relay,
            relay,
            pltpu.VMEM((micro, rows, 128), F32),
            pltpu.VMEM((micro, rows, 128), F32),
            pltpu.VMEM((micro * rows, width), BF16),
            pltpu.VMEM((micro * rows, width), BF16),
            pltpu.VMEM((4, micro * rows, hidden), BF16),
            pltpu.VMEM((4, micro * rows, hidden), F32),
            pltpu.VMEM((8, hidden), F32),
            pltpu.VMEM((8, hidden), F32),
            pltpu.VMEM((8, width), F32),
            pltpu.VMEM((2, 8, hidden), F32),
            close,
            close,
            pltpu.VMEM((4, 2 * TILE[0], TILE[1]), F32),
            wait,
            wait,
            wait,
            wait,
            close,
            pltpu.VMEM((6, 8, hidden), F32),
            pltpu.VMEM((2, width, micro * rows), BF16),
            *[pltpu.VMEM((max(GIVE), *TILE), BF16)] * 4,
            dma((9,)),
            dma((4 + 2 * micro,)),
            dma((SENDS,)),
            dma((micro, parts)),
            dma((SENDS,)),
            dma((micro, parts // PAIR)),
            dma((2, parts // PAIR)),
            dma((2, micro + 1)),
            dma((2, near)),
            dma((3, far)),
            dma((4, max(GIVE))),
            dma((5, 8)),
            dma((4, 4)),
            dma((6,)),
        ],
        compiler_params=pltpu.CompilerParams(
            collective_id=0, has_side_effects=True, vmem_limit_bytes=55 * 2**20
        ),
    )(lengths.T, tokens, cotangent, weights, biases, gains)
    scale = 1.0 / math.sqrt(micro * rows * lax.axis_size("batch"))
    return pl.pallas_call(
        functools.partial(finish_kernel, scale),
        name="finish",
        out_shape=(
            jax.ShapeDtypeStruct(tokens.shape, BF16),
            jax.ShapeDtypeStruct(tokens.shape, BF16),
            jax.ShapeDtypeStruct(weights.shape, F32),
            jax.ShapeDtypeStruct(biases.shape, F32),
            jax.ShapeDtypeStruct(gains.shape, F32),
        ),
        in_specs=[vmem, vmem, vmem, vmem],
        out_specs=(any_spec,) * 5,
        scratch_shapes=[
            pltpu.VMEM((4, width, hidden), F32),
            pltpu.VMEM((2, rows, width), BF16),
            pltpu.VMEM(biases.shape, F32),
            pltpu.VMEM(gains.shape, F32),
            dma((4 * CUTS + 4,)),
        ],
        compiler_params=pltpu.CompilerParams(vmem_limit_bytes=24 * 2**20),
    )(*[pltpu.with_memory_space_constraint(value, pltpu.VMEM) for value in (wide, small, final, grad)])


def solution(mesh):
    row = P("section", "batch", None)
    placed = (
        row,
        row,
        P("section", None, None, None),
        P("section", None, None),
        P("section", None),
        P(None, "batch"),
    )
    return jax.shard_map(
        local,
        mesh=mesh,
        in_specs=placed,
        out_specs=(row, row, *placed[2:5]),
        check_vma=False,
    )
```

```python
import functools
import math

import jax
import jax.numpy as jnp
from jax import lax
from jax.experimental import pallas as pl
from jax.experimental.pallas import tpu as pltpu
from jax.sharding import PartitionSpec as P

MESH = pl.DeviceIdType.MESH
EPS = 1e-05
PART = 64
PAIR = 2
GIVE = (9, 3)
JOIN = (24, 10)
LATE = 34
NEXT = 3
LAG = 14
CUTS = 4
SENDS = 2
LANES = 256
TILE = (128, 256)
F32 = jnp.float32
BF16 = jnp.bfloat16


def dot(a, b):
    return jnp.dot(a, b, preferred_element_type=F32)


def over(value, count):
    return lax.shift_right_logical(value, count.bit_length() - 1)


def within(value, count):
    return lax.bitwise_and(value, count - 1)


def order_matrix(rows, back):
    new = lax.broadcasted_iota(jnp.int32, (rows, rows), 1 if back else 0)
    old = lax.broadcasted_iota(jnp.int32, (rows, rows), 0 if back else 1)
    hit = (within(new, 8) * (rows // 8) + over(new, 8)) == old
    return jnp.where(hit, 1.0, 0.0).astype(BF16)


def groups(value):
    return [value[8 * g : 8 * g + 8] for g in range(value.shape[0] // 8)]


def chain(gain, add, carry, back):
    row = lax.broadcasted_iota(jnp.int32, gain.shape, 0)
    for step in (1, 2, 4):
        shift = 8 - step if back else step
        inside = (row < 8 - step) if back else (row >= step)
        add = jnp.where(inside, gain * pltpu.roll(add, shift, 0) + add, add)
        gain = jnp.where(inside, gain * pltpu.roll(gain, shift, 0), gain)
    whole = gain * carry + add
    edge = 7 if back else 0
    enter = jnp.where(row == edge, carry, pltpu.roll(whole, 7 if back else 1, 0))
    last = whole[0:1] if back else whole[7:8]
    return enter, jnp.broadcast_to(last, gain.shape)


def relay_kernel(
    lengths_in,
    tokens,
    cotangent,
    weights,
    biases,
    gains,
    final_out,
    grad_out,
    wide_out,
    small_out,
    w,
    wt,
    lengths,
    bias,
    gain,
    stage,
    x_in,
    do_in,
    x_out,
    dx_out,
    valid_s,
    keep_s,
    normed,
    down,
    right,
    coef,
    h_carry,
    e_carry,
    gain_acc,
    bias_acc,
    sib_out,
    sib_in,
    own,
    up_out,
    up_in,
    ret_in,
    tot_out,
    tot_in,
    small,
    left,
    gift_out,
    gift_in,
    back_in,
    back_sib,
    load_sem,
    tok_sem,
    fwd_send,
    fwd_recv,
    bwd_send,
    bwd_recv,
    around_sem,
    home_sem,
    near_sem,
    far_sem,
    gift_sem,
    mid_sem,
    short_sem,
    small_sem,
):
    micro, rows, width = x_in.shape
    parts = rows // PART
    hidden = w.shape[2]
    section, batch = lax.axis_index("section"), lax.axis_index("batch")
    sections, batches = lax.axis_size("section"), lax.axis_size("batch")
    last = sections - 1
    mixer = lax.rem(section, 2) == 0
    feed = lax.rem(section, 2) == 1
    chips = batches // 2
    chip, core = batch // 2, lax.rem(batch, 2)
    sibling = batch + 1 - 2 * core
    half = chips // 2
    low_side = chip < half
    step_in = jnp.where(low_side, 2, -2)
    inner = batch + step_in
    outer = batch - step_in
    middle = (chip == half - 1) | (chip == half)
    has_outer = (chip > 0) & (chip < chips - 1)
    depth = jnp.where(low_side, half - 1 - chip, chip - half)

    def remote(src, dst, send, recv, to_section, to_batch):
        return pltpu.make_async_remote_copy(
            src_ref=src,
            dst_ref=dst,
            send_sem=send,
            recv_sem=recv,
            device_id=(to_section, to_batch),
            device_id_type=MESH,
        )

    sources = [
        (tokens.at[0], stage.at[0]),
        (cotangent.at[0], stage.at[1]),
        (lengths_in, lengths),
        (biases.at[0], bias),
        (gains, gain),
        *[(weights.at[0, j], w.at[j]) for j in (3, 0, 1, 2)],
    ]
    loads = [pltpu.make_async_copy(src, dst, load_sem.at[i]) for i, (src, dst) in enumerate(sources)]
    for copy in loads:
        copy.start()

    barrier = pltpu.get_barrier_semaphore()
    for other in range(1, sections):
        pl.semaphore_signal(
            barrier, inc=1, device_id=(lax.rem(section + other, sections), batch), device_id_type=MESH
        )
    pl.semaphore_signal(barrier, inc=1, device_id=(section, sibling), device_id_type=MESH)
    pl.semaphore_signal(barrier, inc=1, device_id=(section, inner), device_id_type=MESH)

    @pl.when(has_outer)
    def _():
        pl.semaphore_signal(barrier, inc=1, device_id=(section, outer), device_id_type=MESH)

    loads[2].wait()
    spot = lax.broadcasted_iota(jnp.int32, (rows, 128), 0)
    spot_in = within(spot, PART)
    spot = spot - spot_in + within(spot_in, 8) * (PART // 8) + over(spot_in, 8)
    for m in range(micro):
        end = jnp.zeros((1, 1), jnp.int32)
        start_hit = jnp.zeros((rows, 128), F32)
        for k in range(lengths.shape[0]):
            start_hit = jnp.where(spot == end, 1.0, start_hit)
            end = end + lengths[k : k + 1, m : m + 1]
        valid = jnp.where(spot < end, 1.0, 0.0)
        valid_s[m] = valid
        keep_s[m] = valid * (1.0 - start_hit)
    h_carry[...] = jnp.zeros_like(h_carry)
    e_carry[...] = jnp.zeros_like(e_carry)
    gain_acc[...] = jnp.zeros_like(gain_acc)
    bias_acc[...] = jnp.zeros_like(bias_acc)

    perm = order_matrix(PART, False)
    loads[0].wait()
    for c in range(parts):
        span = pl.ds(c * PART, PART)
        ordered = dot(perm, stage[0, span, :]).astype(BF16)
        stage[2, span, :] = ordered

        @pl.when(section == 0)
        def _():
            x_in[0, span, :] = ordered

    loads[1].wait()
    for c in range(parts):
        span = pl.ds(c * PART, PART)
        ordered = dot(perm, stage[1, span, :]).astype(BF16)
        stage[3, span, :] = ordered

        @pl.when(section == last)
        def _():
            do_in[last, span, :] = ordered

    pl.semaphore_wait(barrier, sections + 1 + jnp.where(has_outer, 1, 0))

    def token_copy(m):
        return remote(stage.at[2], x_in.at[m], tok_sem.at[0], tok_sem.at[2 + m], 0, batch)

    def cot_copy(m):
        return remote(stage.at[3], do_in.at[m], tok_sem.at[1], tok_sem.at[2 + micro + m], last, batch)

    def side_copy():
        return remote(stage.at[3], stage.at[4], tok_sem.at[1], tok_sem.at[2 + 2 * micro], last - 1, batch)

    def side_last():
        return remote(stage.at[4], do_in.at[0], tok_sem.at[2 + 2 * micro + 1], tok_sem.at[2 + micro], last, batch)

    @pl.when(section != 0)
    def _():
        token_copy(section).start()

    pl.when(section == 0)(lambda: side_copy().start())

    @pl.when((section != last) & (section != 0))
    def _():
        cot_copy(section).start()

    for copy in loads[3:]:
        copy.wait()

    wt[3] = w[3].T

    def flip():
        for j in range(3):
            wt[j] = w[j].T

    pl.when(section > 0)(flip)

    @pl.when(section == last - 1)
    def _():
        side_copy().wait_recv()
        side_last().start()

    def wide(mask):
        return jnp.concatenate([mask] * (width // 128), axis=1)

    def slab(mask):
        return jnp.concatenate([mask] * (LANES // 128), axis=1)

    def fwd_copy(m, c):
        span = pl.ds(pl.multiple_of(c * PART, PART), PART)
        return remote(
            x_out.at[m, span],
            x_in.at[m, span],
            fwd_send.at[within(c, SENDS)],
            fwd_recv.at[m, c],
            jnp.minimum(section + 1, last),
            batch,
        )

    def bwd_copy(m, c):
        span = pl.ds(pl.multiple_of(c * PAIR * PART, PAIR * PART), PAIR * PART)
        return remote(
            dx_out.at[m, span],
            do_in.at[m, span],
            bwd_send.at[within(c, SENDS)],
            bwd_recv.at[m, c],
            jnp.maximum(section - 1, 0),
            batch,
        )

    def around_copy(c):
        span = pl.ds(pl.multiple_of(c * PAIR * PART, PAIR * PART), PAIR * PART)
        return remote(
            dx_out.at[0, span], stage.at[2, span], bwd_send.at[within(c, SENDS)], around_sem.at[0, c], 0, batch
        )

    def around_last(c):
        span = pl.ds(pl.multiple_of(c * PAIR * PART, PAIR * PART), PAIR * PART)
        return remote(stage.at[2, span], do_in.at[0, span], around_sem.at[1, c], bwd_recv.at[0, c], 1, batch)

    def home_copy(source, result, k, m):
        return remote(source.at[m], result.at[0], home_sem.at[k, m], home_sem.at[k, micro], m, batch)

    def keep_copy(source, result, k, m):
        return pltpu.make_async_copy(source.at[m], result.at[0], home_sem.at[k, m])

    high, broad = TILE
    down_n, across = width // high, hidden // broad
    pieces = 4 * down_n * across // 2
    near, far, gifts = sib_in.shape[0], up_in.shape[0], gift_in.shape[0]
    friend = last - section
    give = jnp.where(section == 0, GIVE[0], jnp.where(section == 1, GIVE[1], 0))
    take = jnp.where(friend == 0, GIVE[0], jnp.where(friend == 1, GIVE[1], 0))
    start = jnp.where(section == last, JOIN[0], JOIN[1])

    def place(piece):
        j = 3 - over(piece, down_n * across)
        rest = within(piece, down_n * across)
        row = pl.multiple_of(within(rest, down_n) * high, high)
        col = pl.multiple_of(over(rest, down_n) * broad, broad)
        return j, row, col

    def partial(t):
        j, row, col = place(2 * t)
        from_down = (j == 3) | (feed & (j == 2))
        return dot(left[jnp.where(from_down, 1, 0), pl.ds(row, 2 * high), :], right[j, :, pl.ds(col, broad)])

    def sib_copy(t):
        k = within(t, near)
        return remote(sib_out.at[k], sib_in.at[k], short_sem.at[0, within(t, 4)], near_sem.at[0, k], section, sibling)

    def make(i):
        own[within(i, 4)] = partial(i)
        sib_out[within(i, near)] = own[within(i, 4), pl.ds((1 - core) * high, high), :].astype(BF16)
        sib_copy(i).start()

    def first_tiles():
        left[1] = down[...].T

        @pl.loop(0, NEXT)
        def _(t):
            make(t)

    def forward(m, c, count):
        size = count * PART
        span = pl.ds(pl.multiple_of(c * size, size), size)
        line = pl.ds(pl.multiple_of(m * rows + c * size, size), size)

        @pl.when(section > 0)
        def _():
            for k in range(count):
                fwd_copy(m, c * count + k).wait_recv()

        @pl.when((section == 0) & (c == 0) & (m > 0))
        def _():
            token_copy(m).wait_recv()

        x = x_in[m, span, :].astype(F32)
        valid = valid_s[m, span, :]
        scale = lax.rsqrt(jnp.mean(x * x, axis=-1, keepdims=True) + EPS)
        nb = (x * scale * gain[...]).astype(BF16)
        normed[line, :] = nb

        def mix():
            keep_l = slab(keep_s[m, span, :])
            valid_l = slab(valid)
            for blk in range(hidden // LANES):
                cols = slice(blk * LANES, (blk + 1) * LANES)
                zf = dot(nb, w[0, :, cols]) + bias[0:1, cols]
                zi = dot(nb, w[1, :, cols]) + bias[1:2, cols]
                zh = dot(nb, w[2, :, cols])
                low = jnp.minimum(jnp.minimum(zf, zi), 0.0)
                e0 = jnp.exp(low)
                ei, ef = jnp.exp(low - zi), jnp.exp(low - zf)
                top, bot = e0 + ei, e0 + ef
                inv = 1.0 / (top + bot)
                decay = top * inv
                admit = bot * inv
                a = keep_l * decay
                iv = valid_l * admit
                b = iv * zh
                a_g, b_g = groups(a), groups(b)
                state, product = b_g[0], a_g[0]
                states, products = [state], [product]
                for g in range(1, len(a_g)):
                    state = a_g[g] * state + b_g[g]
                    product = a_g[g] * product
                    states.append(state)
                    products.append(product)
                enter, leave = chain(product, state, h_carry[:, cols], False)
                h_carry[:, cols] = leave
                hs = [s + p * enter for s, p in zip(states, products)]
                h_prev = jnp.concatenate([enter] + hs[:-1], axis=0)
                right[3, line, cols] = jnp.concatenate(hs, axis=0).astype(BF16)
                turn = (keep_l * h_prev - valid_l * zh) * inv
                coef[0, line, cols] = a
                coef[1, line, cols] = decay * ef * turn
                coef[2, line, cols] = -admit * ei * turn
                coef[3, line, cols] = iv
            y = dot(right[3, line, :], wt[3])
            x_out[m, span, :] = (x + wide(valid) * y).astype(BF16)

        def feed_on():
            for k in range(2):
                for blk in range(hidden // LANES):
                    cols = slice(blk * LANES, (blk + 1) * LANES)
                    u = dot(nb, w[k, :, cols]) + bias[k : k + 1, cols]
                    phi = 0.5 + 0.5 * lax.erf(u * math.sqrt(0.5))
                    right[2 + k, line, cols] = (u * phi).astype(BF16)
                    coef[k, line, cols] = phi + u * jnp.exp(-0.5 * u * u) * (1.0 / math.sqrt(2.0 * math.pi))
            y = dot(right[2, line, :], wt[2]) + dot(right[3, line, :], wt[3])
            x_out[m, span, :] = (x + wide(valid) * y).astype(BF16)

        if count == 1:
            pl.when(mixer)(mix)
            pl.when(feed)(feed_on)

            @pl.when(m * parts + c >= SENDS)
            def _():
                fwd_copy(m, c).wait_send()

            fwd_copy(m, c).start()
        else:
            feed_on()
            x_out[m, span, :] = (x_out[m, span, :].astype(F32) * wide(valid)).astype(BF16)

    def backward(m, c):
        size = PAIR * PART
        span = pl.ds(pl.multiple_of(c * size, size), size)
        line = pl.ds(pl.multiple_of(m * rows + c * size, size), size)

        @pl.when(section < last)
        def _():
            bwd_copy(m, c).wait_recv()

        @pl.when((section == last) & (c == 0) & (m != last))
        def _():
            cot_copy(m).wait_recv()

        do = do_in[m, span, :].astype(F32) * wide(valid_s[m, span, :])
        dy = do.astype(BF16)
        down[line, :] = dy
        pl.when((section == 0) & (m == micro - 1) & (c == 0))(first_tiles)

        @pl.when(mixer)
        def _():
            for blk in range(hidden // LANES):
                cols = slice(blk * LANES, (blk + 1) * LANES)
                d_all, a_all = dot(dy, w[3, :, cols]), coef[0, line, cols]
                pieces_dh = []
                for part in range(PAIR - 1, -1, -1):
                    spot = slice(part * PART, (part + 1) * PART)
                    d_g, a_g = groups(d_all[spot]), groups(a_all[spot])
                    count = len(a_g)
                    dhs, spread = [None] * count, [None] * count
                    dhs[-1] = d_g[-1]
                    for g in range(count - 2, -1, -1):
                        dhs[g] = d_g[g] + a_g[g + 1] * dhs[g + 1]
                        spread[g] = a_g[g + 1] if g == count - 2 else a_g[g + 1] * spread[g + 1]
                    enter, leave = chain(a_g[0] * spread[0], a_g[0] * dhs[0], e_carry[:, cols], True)
                    e_carry[:, cols] = leave
                    dhs = [d + s * enter for d, s in zip(dhs[:-1], spread[:-1])] + [dhs[-1] + enter]
                    pieces_dh = dhs + pieces_dh
                dh = jnp.concatenate(pieces_dh, axis=0)
                for j in range(3):
                    dz = dh * coef[1 + j, line, cols]
                    right[j, line, cols] = dz.astype(BF16)
                    if j < 2:
                        bias_acc[j, :, cols] += sum(groups(dz))

        @pl.when(feed)
        def _():
            for k in range(2):
                for blk in range(hidden // LANES):
                    cols = slice(blk * LANES, (blk + 1) * LANES)
                    du = dot(dy, w[2 + k, :, cols]) * coef[k, line, cols]
                    right[k, line, cols] = du.astype(BF16)
                    bias_acc[k, :, cols] += sum(groups(du))

        def finish(dn):
            x = x_in[m, span, :].astype(F32)
            scale = lax.rsqrt(jnp.mean(x * x, axis=-1, keepdims=True) + EPS)
            xr = x * scale
            part = dn * xr
            gain_acc[...] += sum(groups(part))
            dng = dn * gain[...]
            mean = jnp.mean(dng * xr, axis=-1, keepdims=True)
            dx_out[m, span, :] = (do + scale * (dng - xr * mean)).astype(BF16)

        @pl.when(mixer)
        def _():
            finish(
                dot(right[0, line, :], wt[0])
                + dot(right[1, line, :], wt[1])
                + dot(right[2, line, :], wt[2])
            )

        @pl.when(feed)
        def _():
            finish(dot(right[0, line, :], wt[0]) + dot(right[1, line, :], wt[1]))

        @pl.when(section > 0)
        def _():
            @pl.when((m > 0) if SENDS >= parts // PAIR else (m * (parts // PAIR) + parts // PAIR - 1 - c >= SENDS))
            def _():
                bwd_copy(m, c).wait_send()

            by_side = (section == 2) & (m == 0)
            pl.when(by_side)(lambda: around_copy(c).start())
            pl.when(jnp.logical_not(by_side))(lambda: bwd_copy(m, c).start())

    halves = parts // PAIR

    @pl.loop(0, micro * (parts + halves))
    def _(step):
        pl.when((section == 0) & (step == parts))(flip)

        @pl.when(step == micro * parts + halves + 1)
        def _():
            left[0] = normed[...].T


        early = (section == 2) & (step >= (micro - 1) * parts)
        back_now = jnp.where(early, step < (micro - 1) * parts + halves, step >= micro * parts)
        back_now = back_now | (step >= micro * parts + halves)
        f_step = jnp.where(early, step - halves, step)
        late = jnp.where(early & (step < (micro - 1) * parts + halves), step - (micro - 1) * parts, step - micro * parts)

        @pl.when((section < last) & jnp.logical_not(back_now))
        def _():
            forward(over(f_step, parts), within(f_step, parts), 1)

        turn = over(step, 2)

        @pl.when((section == 0) & (step == micro * parts))
        def _():
            for c in range(halves - 1, -1, -1):
                around_copy(c).wait_recv()
                around_last(c).start()

        @pl.when((section == last) & (within(step, 2) == 0) & (turn < micro * halves))
        def _():
            forward(over(turn, halves), within(turn, halves), PAIR)

        @pl.when(jnp.where(section == last, (within(step, 2) == 1) & (turn < micro * halves), back_now))
        def _():
            q = jnp.where(section == last, turn, jnp.maximum(late, 0))
            c = within(q, halves)
            backward(over(q, halves), jnp.where(section == last, c, halves - 1 - c))

    def homeward(act):
        for m in range(micro):
            for k, source, result, at in ((0, x_out, final_out, last), (1, dx_out, grad_out, 0)):

                @pl.when((section == at) & (section != m))
                def _():
                    act(home_copy(source, result, k, m), True)

                @pl.when((section == at) & (section == m))
                def _():
                    act(keep_copy(source, result, k, m), False)

    def is_given(t):
        return (within(t, 2) == 1) & (over(t, 2) < give)

    def chain_index(t):
        return t - jnp.minimum(over(t, 2), give)

    def is_taken(t):
        return (t >= start) & (t < start + take)

    def own_index(t):
        return t - jnp.clip(t - start, 0, take)

    def gift_copy(d):
        return remote(gift_out.at[d], gift_in.at[d], gift_sem.at[0, d], gift_sem.at[1, d], friend, batch)

    def back_copy(r, d):
        return remote(
            tot_out.at[within(r, far)], back_in.at[d], mid_sem.at[3, within(d, 8)], gift_sem.at[2, d], friend, batch
        )

    def back_share(d):
        return remote(
            back_in.at[d], back_sib.at[d], short_sem.at[2, within(d, 4)], gift_sem.at[3, d], section, sibling
        )

    def store_back(d, source, who, sem):
        j, row, col = place(4 * d + 2 + who)
        return pltpu.make_async_copy(
            source.at[d], wide_out.at[j, pl.ds(row, high), pl.ds(col, broad)], sem
        )

    def up_copy(k):
        k = within(k, far)
        return remote(up_out.at[k], up_in.at[k], far_sem.at[0, k], far_sem.at[1, k], section, inner)

    def mirror_copy(k):
        k = within(k, far)
        return remote(up_out.at[k], ret_in.at[k], far_sem.at[0, k], far_sem.at[2, k], section, inner)

    def ret_copy(k):
        k = within(k, far)
        return remote(tot_out.at[k], ret_in.at[k], mid_sem.at[0, within(k, 8)], far_sem.at[2, k], section, outer)

    def share_copy(r):
        k, at = within(r, far), within(own_index(r), near)
        return remote(tot_out.at[k], tot_in.at[at], mid_sem.at[1, within(r, 8)], near_sem.at[1, at], section, sibling)

    def piece_of(r):
        return jnp.where(r < give, 2 * r, own_index(r) + give)

    def store_own(r):
        j, row, col = place(2 * piece_of(r) + core)
        k = within(r, far)
        return pltpu.make_async_copy(
            tot_out.at[k], wide_out.at[j, pl.ds(row, high), pl.ds(col, broad)], mid_sem.at[2, within(r, 8)]
        )

    def store_other(r):
        j, row, col = place(2 * piece_of(r) + 1 - core)
        k = within(own_index(r), near)
        return pltpu.make_async_copy(
            tot_in.at[k], wide_out.at[j, pl.ds(row, high), pl.ds(col, broad)], short_sem.at[1, within(k, 4)]
        )

    def is_result(r):
        return (r >= 0) & (r < pieces - give + take)

    lag = jnp.minimum(NEXT + 3 + 8 * depth, LAG)
    small_at = NEXT + 4 + 4 * (half - 1 - depth)
    small_back = NEXT + 4 + 4 * half + 4 * depth

    def small_fill():
        for k in range(2):
            small[0, k : k + 1, :] = jnp.sum(bias_acc[k], axis=0, keepdims=True)
        small[0, 2:3, 0:width] = jnp.sum(gain_acc[...], axis=0, keepdims=True)
        small[0, 2:3, width:] = jnp.zeros((1, hidden - width), F32)
        small[0, 3:8, :] = jnp.zeros((5, hidden), F32)

    def small_sib():
        return remote(small.at[0], small.at[1], small_sem.at[0], small_sem.at[1], section, sibling)

    def small_up(to):
        return remote(small.at[2], small.at[to], small_sem.at[2], small_sem.at[to], section, inner)

    def small_ret():
        return remote(small.at[5], small.at[4], small_sem.at[5], small_sem.at[4], section, outer)

    def small_step(t):
        @pl.when(t == NEXT)
        def _():
            small_fill()
            small_sib().start()

        @pl.when(t == small_at)
        def _():
            small_sib().wait_recv()
            small[2] = small[0] + small[1]

            @pl.when(has_outer)
            def _():
                small_up(3).wait_recv()
                small[2] = small[2] + small[3]

            @pl.when(middle)
            def _():
                small_up(4).start()

            @pl.when(jnp.logical_not(middle))
            def _():
                small_up(3).start()

        @pl.when(t == small_back)
        def _():
            small_up(4).wait_recv()

            @pl.when(middle)
            def _():
                small[5] = small[2] + small[4]

            @pl.when(jnp.logical_not(middle))
            def _():
                small[5] = small[4]

            @pl.when(has_outer)
            def _():
                small_ret().start()

    pl.when(section > 0)(first_tiles)

    end = jnp.maximum(pieces + take + lag + 5, jnp.maximum(small_back + 1, LATE + give + 4))

    @pl.loop(NEXT, end)
    def _(t):
        @pl.when((t < pieces + take) & jnp.logical_not(is_taken(t)))
        def _():
            make(own_index(t))

        s = t - NEXT

        @pl.when((s >= 0) & (s < pieces + take))
        def _():
            i = own_index(s)
            k = chain_index(s)
            slot = within(k, far)

            def onward(total):
                @pl.when(has_outer)
                def _():
                    up_copy(k).wait_recv()
                    up_out[slot] = (total + up_in[slot].astype(F32)).astype(BF16)

                @pl.when(jnp.logical_not(has_outer))
                def _():
                    up_out[slot] = total.astype(BF16)

                @pl.when(middle)
                def _():
                    mirror_copy(k).start()

                @pl.when(jnp.logical_not(middle))
                def _():
                    up_copy(k).start()

            @pl.when(jnp.logical_not(is_taken(s)))
            def _():
                sib_copy(i).wait()
                total = own[within(i, 4), pl.ds(core * high, high), :] + sib_in[within(i, near)].astype(F32)

                @pl.when(is_given(s))
                def _():
                    d = over(s, 2)
                    gift_out[d] = total.astype(BF16)
                    gift_copy(d).start()

                @pl.when(jnp.logical_not(is_given(s)))
                def _():
                    onward(total)

            @pl.when(is_taken(s))
            def _():
                d = s - start
                gift_copy(d).wait_recv()
                onward(gift_in[d].astype(F32))

        on = jnp.logical_not(is_given(t))
        r = chain_index(t) - lag
        slot = within(r, far)

        @pl.when(on & is_result(r))
        def _():
            mirror_copy(r).wait()

            @pl.when(middle)
            def _():
                tot_out[slot] = (up_out[slot].astype(F32) + ret_in[slot].astype(F32)).astype(BF16)

            @pl.when(jnp.logical_not(middle))
            def _():
                tot_out[slot] = ret_in[slot]

            @pl.when(has_outer)
            def _():
                ret_copy(r).start()

            @pl.when(is_taken(r))
            def _():
                back_copy(r, r - start).start()

            @pl.when(jnp.logical_not(is_taken(r)))
            def _():
                share_copy(r).start()
                store_own(r).start()

        r2 = r - 2

        @pl.when(on & is_result(r2) & jnp.logical_not(is_taken(r2)))
        def _():
            share_copy(r2).wait_recv()
            store_other(r2).start()

        r4 = r - 4

        @pl.when(on & is_result(r4))
        def _():
            @pl.when(has_outer)
            def _():
                ret_copy(r4).wait_send()

            @pl.when(is_taken(r4))
            def _():
                back_copy(r4, r4 - start).wait_send()

            @pl.when(jnp.logical_not(is_taken(r4)))
            def _():
                share_copy(r4).wait_send()
                store_own(r4).wait()
                store_other(r4).wait()

        d = t - LATE

        @pl.when((d >= 0) & (d < give))
        def _():
            gift_copy(d).wait_send()
            back_copy(r, d).wait_recv()
            back_share(d).start()
            store_back(d, back_in, core, mid_sem.at[4, within(d, 8)]).start()

        d2 = d - 2

        @pl.when((d2 >= 0) & (d2 < give))
        def _():
            back_share(d2).wait()
            store_back(d2, back_sib, 1 - core, short_sem.at[3, within(d2, 4)]).start()

        d4 = d - 4

        @pl.when((d4 >= 0) & (d4 < give))
        def _():
            store_back(d4, back_in, core, mid_sem.at[4, within(d4, 8)]).wait()
            store_back(d4, back_sib, 1 - core, short_sem.at[3, within(d4, 4)]).wait()

        pl.when(t == 2 * gifts + 2)(lambda: homeward(lambda copy, far: copy.start()))
        small_step(t)

    small_out[...] = small[5] * (1.0 / math.sqrt(micro * rows * batches))

    small_sib().wait_send()
    small_up(3).wait_send()

    @pl.when(has_outer)
    def _():
        small_ret().wait_send()

    @pl.when(section != 0)
    def _():
        token_copy(section).wait_send()

    pl.when(section == 0)(lambda: side_copy().wait_send())

    @pl.when(section == 0)
    def _():
        for c in range(halves):
            around_last(c).wait_send()

    pl.when(section == last - 1)(lambda: side_last().wait_send())

    @pl.when((section != last) & (section != 0))
    def _():
        cot_copy(section).wait_send()

    for c in range(SENDS):

        @pl.when(section != last)
        def _():
            fwd_copy(0, c).wait_send()

        @pl.when(section != 0)
        def _():
            bwd_copy(0, c).wait_send()

    homeward(lambda copy, far: copy.wait_send() if far else copy.wait())

    @pl.when(section != last)
    def _():
        home_copy(x_out, final_out, 0, section).wait_recv()

    @pl.when(section != 0)
    def _():
        home_copy(dx_out, grad_out, 1, section).wait_recv()


def finish_kernel(scale, wide, small, final_in, grad_in, final, grad, weight, bias, gain, full, turned, sums, norms, sem):
    depth = wide.shape[1] // CUTS
    stores = []
    for n in range(wide.shape[0] * CUTS):
        j, span = n // CUTS, pl.ds((n % CUTS) * depth, depth)
        full[j, span, :] = wide[j, span, :].astype(F32) * scale
        stores.append(pltpu.make_async_copy(full.at[j, span], weight.at[0, j, span], sem.at[n]))
        stores[-1].start()
    sums[0] = small[0:2, :]
    norms[...] = small[2:3, 0 : norms.shape[1]]
    for source, result in ((sums, bias), (norms, gain)):
        stores.append(pltpu.make_async_copy(source, result, sem.at[len(stores)]))
        stores[-1].start()
    order = order_matrix(PART, True)
    for k, (source, result) in enumerate(((final_in, final), (grad_in, grad))):
        for c in range(source.shape[1] // PART):
            span = slice(c * PART, (c + 1) * PART)
            turned[k, span, :] = dot(order, source[0, span, :]).astype(BF16)
        stores.append(pltpu.make_async_copy(turned.at[k], result.at[0], sem.at[len(stores)]))
        stores[-1].start()
    for copy in stores:
        copy.wait()


def local(tokens, cotangent, weights, biases, gains, lengths):
    micro = lengths.shape[0]
    _, rows, width = tokens.shape
    hidden = weights.shape[3]
    parts = rows // PART
    pieces = 4 * width * hidden // (TILE[0] * TILE[1]) // 2
    any_spec = pl.BlockSpec(memory_space=pl.ANY)
    vmem = pl.BlockSpec(memory_space=pltpu.VMEM)
    dma = pltpu.SemaphoreType.DMA
    relay = pltpu.VMEM((micro, rows, width), BF16)
    near = min(8, pieces)
    far = 16
    close = pltpu.VMEM((near, *TILE), BF16)
    wait = pltpu.VMEM((far, *TILE), BF16)
    final, grad, wide, small = pl.pallas_call(
        relay_kernel,
        name="relay",
        out_shape=(
            pltpu.VMEM(tokens.shape, BF16),
            pltpu.VMEM(tokens.shape, BF16),
            pltpu.VMEM((4, width, hidden), BF16),
            pltpu.VMEM((8, hidden), F32),
        ),
        in_specs=[any_spec] * 6,
        out_specs=(vmem, vmem, vmem, vmem),
        scratch_shapes=[
            pltpu.VMEM((4, width, hidden), BF16),
            pltpu.VMEM((4, hidden, width), BF16),
            pltpu.VMEM(lengths.shape[::-1], jnp.int32),
            pltpu.VMEM((2, hidden), F32),
            pltpu.VMEM((1, width), F32),
            pltpu.VMEM((5, rows, width), BF16),
            relay,
            relay,
            relay,
            relay,
            pltpu.VMEM((micro, rows, 128), F32),
            pltpu.VMEM((micro, rows, 128), F32),
            pltpu.VMEM((micro * rows, width), BF16),
            pltpu.VMEM((micro * rows, width), BF16),
            pltpu.VMEM((4, micro * rows, hidden), BF16),
            pltpu.VMEM((4, micro * rows, hidden), F32),
            pltpu.VMEM((8, hidden), F32),
            pltpu.VMEM((8, hidden), F32),
            pltpu.VMEM((8, width), F32),
            pltpu.VMEM((2, 8, hidden), F32),
            close,
            close,
            pltpu.VMEM((4, 2 * TILE[0], TILE[1]), F32),
            wait,
            wait,
            wait,
            wait,
            close,
            pltpu.VMEM((6, 8, hidden), F32),
            pltpu.VMEM((2, width, micro * rows), BF16),
            *[pltpu.VMEM((max(GIVE), *TILE), BF16)] * 4,
            dma((9,)),
            dma((4 + 2 * micro,)),
            dma((SENDS,)),
            dma((micro, parts)),
            dma((SENDS,)),
            dma((micro, parts // PAIR)),
            dma((2, parts // PAIR)),
            dma((2, micro + 1)),
            dma((2, near)),
            dma((3, far)),
            dma((4, max(GIVE))),
            dma((5, 8)),
            dma((4, 4)),
            dma((6,)),
        ],
        compiler_params=pltpu.CompilerParams(
            collective_id=0, has_side_effects=True, vmem_limit_bytes=55 * 2**20
        ),
    )(lengths.T, tokens, cotangent, weights, biases, gains)
    scale = 1.0 / math.sqrt(micro * rows * lax.axis_size("batch"))
    return pl.pallas_call(
        functools.partial(finish_kernel, scale),
        name="finish",
        out_shape=(
            jax.ShapeDtypeStruct(tokens.shape, BF16),
            jax.ShapeDtypeStruct(tokens.shape, BF16),
            jax.ShapeDtypeStruct(weights.shape, F32),
            jax.ShapeDtypeStruct(biases.shape, F32),
            jax.ShapeDtypeStruct(gains.shape, F32),
        ),
        in_specs=[vmem, vmem, vmem, vmem],
        out_specs=(any_spec,) * 5,
        scratch_shapes=[
            pltpu.VMEM((4, width, hidden), F32),
            pltpu.VMEM((2, rows, width), BF16),
            pltpu.VMEM(biases.shape, F32),
            pltpu.VMEM(gains.shape, F32),
            dma((4 * CUTS + 4,)),
        ],
        compiler_params=pltpu.CompilerParams(vmem_limit_bytes=24 * 2**20),
    )(*[pltpu.with_memory_space_constraint(value, pltpu.VMEM) for value in (wide, small, final, grad)])


def solution(mesh):
    row = P("section", "batch", None)
    placed = (
        row,
        row,
        P("section", None, None, None),
        P("section", None, None),
        P("section", None),
        P(None, "batch"),
    )
    return jax.shard_map(
        local,
        mesh=mesh,
        in_specs=placed,
        out_specs=(row, row, *placed[2:5]),
        check_vma=False,
    )
```

```python
import functools
import math

import jax
import jax.numpy as jnp
from jax import lax
from jax.experimental import pallas as pl
from jax.experimental.pallas import tpu as pltpu
from jax.sharding import PartitionSpec as P

MESH = pl.DeviceIdType.MESH
EPS = 1e-05
PART = 64
PAIR = 2
GIVE = (9, 3)
JOIN = (24, 10)
LATE = 34
NEXT = 3
LAG = 14
CUTS = 4
SENDS = 2
LANES = 256
TILE = (128, 256)
F32 = jnp.float32
BF16 = jnp.bfloat16


def dot(a, b):
    return jnp.dot(a, b, preferred_element_type=F32)


def over(value, count):
    return lax.shift_right_logical(value, count.bit_length() - 1)


def within(value, count):
    return lax.bitwise_and(value, count - 1)


def order_matrix(rows, back):
    new = lax.broadcasted_iota(jnp.int32, (rows, rows), 1 if back else 0)
    old = lax.broadcasted_iota(jnp.int32, (rows, rows), 0 if back else 1)
    hit = (within(new, 8) * (rows // 8) + over(new, 8)) == old
    return jnp.where(hit, 1.0, 0.0).astype(BF16)


def groups(value):
    return [value[8 * g : 8 * g + 8] for g in range(value.shape[0] // 8)]


def chain(gain, add, carry, back):
    row = lax.broadcasted_iota(jnp.int32, gain.shape, 0)
    for step in (1, 2, 4):
        shift = 8 - step if back else step
        inside = (row < 8 - step) if back else (row >= step)
        add = jnp.where(inside, gain * pltpu.roll(add, shift, 0) + add, add)
        gain = jnp.where(inside, gain * pltpu.roll(gain, shift, 0), gain)
    whole = gain * carry + add
    edge = 7 if back else 0
    enter = jnp.where(row == edge, carry, pltpu.roll(whole, 7 if back else 1, 0))
    last = whole[0:1] if back else whole[7:8]
    return enter, jnp.broadcast_to(last, gain.shape)


def relay_kernel(
    lengths_in,
    tokens,
    cotangent,
    weights,
    biases,
    gains,
    final_out,
    grad_out,
    wide_out,
    small_out,
    w,
    wt,
    lengths,
    bias,
    gain,
    stage,
    x_in,
    do_in,
    x_out,
    dx_out,
    valid_s,
    keep_s,
    normed,
    down,
    right,
    coef,
    h_carry,
    e_carry,
    gain_acc,
    bias_acc,
    sib_out,
    sib_in,
    own,
    up_out,
    up_in,
    ret_in,
    tot_out,
    tot_in,
    small,
    left,
    gift_out,
    gift_in,
    back_in,
    back_sib,
    load_sem,
    tok_sem,
    fwd_send,
    fwd_recv,
    bwd_send,
    bwd_recv,
    around_sem,
    home_sem,
    near_sem,
    far_sem,
    gift_sem,
    mid_sem,
    short_sem,
    small_sem,
):
    micro, rows, width = x_in.shape
    parts = rows // PART
    hidden = w.shape[2]
    section, batch = lax.axis_index("section"), lax.axis_index("batch")
    sections, batches = lax.axis_size("section"), lax.axis_size("batch")
    last = sections - 1
    mixer = lax.rem(section, 2) == 0
    feed = lax.rem(section, 2) == 1
    chips = batches // 2
    chip, core = batch // 2, lax.rem(batch, 2)
    sibling = batch + 1 - 2 * core
    half = chips // 2
    low_side = chip < half
    step_in = jnp.where(low_side, 2, -2)
    inner = batch + step_in
    outer = batch - step_in
    middle = (chip == half - 1) | (chip == half)
    has_outer = (chip > 0) & (chip < chips - 1)
    depth = jnp.where(low_side, half - 1 - chip, chip - half)

    def remote(src, dst, send, recv, to_section, to_batch):
        return pltpu.make_async_remote_copy(
            src_ref=src,
            dst_ref=dst,
            send_sem=send,
            recv_sem=recv,
            device_id=(to_section, to_batch),
            device_id_type=MESH,
        )

    sources = [
        (tokens.at[0], stage.at[0]),
        (cotangent.at[0], stage.at[1]),
        (lengths_in, lengths),
        (biases.at[0], bias),
        (gains, gain),
        *[(weights.at[0, j], w.at[j]) for j in (3, 0, 1, 2)],
    ]
    loads = [pltpu.make_async_copy(src, dst, load_sem.at[i]) for i, (src, dst) in enumerate(sources)]
    for copy in loads:
        copy.start()

    barrier = pltpu.get_barrier_semaphore()
    for other in range(1, sections):
        pl.semaphore_signal(
            barrier, inc=1, device_id=(lax.rem(section + other, sections), batch), device_id_type=MESH
        )
    pl.semaphore_signal(barrier, inc=1, device_id=(section, sibling), device_id_type=MESH)
    pl.semaphore_signal(barrier, inc=1, device_id=(section, inner), device_id_type=MESH)

    @pl.when(has_outer)
    def _():
        pl.semaphore_signal(barrier, inc=1, device_id=(section, outer), device_id_type=MESH)

    loads[2].wait()
    spot = lax.broadcasted_iota(jnp.int32, (rows, 128), 0)
    spot_in = within(spot, PART)
    spot = spot - spot_in + within(spot_in, 8) * (PART // 8) + over(spot_in, 8)
    for m in range(micro):
        end = jnp.zeros((1, 1), jnp.int32)
        start_hit = jnp.zeros((rows, 128), F32)
        for k in range(lengths.shape[0]):
            start_hit = jnp.where(spot == end, 1.0, start_hit)
            end = end + lengths[k : k + 1, m : m + 1]
        valid = jnp.where(spot < end, 1.0, 0.0)
        valid_s[m] = valid
        keep_s[m] = valid * (1.0 - start_hit)
    h_carry[...] = jnp.zeros_like(h_carry)
    e_carry[...] = jnp.zeros_like(e_carry)
    gain_acc[...] = jnp.zeros_like(gain_acc)
    bias_acc[...] = jnp.zeros_like(bias_acc)

    perm = order_matrix(PART, False)
    loads[0].wait()
    for c in range(parts):
        span = pl.ds(c * PART, PART)
        ordered = dot(perm, stage[0, span, :]).astype(BF16)
        stage[2, span, :] = ordered

        @pl.when(section == 0)
        def _():
            x_in[0, span, :] = ordered

    loads[1].wait()
    for c in range(parts):
        span = pl.ds(c * PART, PART)
        ordered = dot(perm, stage[1, span, :]).astype(BF16)
        stage[3, span, :] = ordered

        @pl.when(section == last)
        def _():
            do_in[last, span, :] = ordered

    pl.semaphore_wait(barrier, sections + 1 + jnp.where(has_outer, 1, 0))

    def token_copy(m):
        return remote(stage.at[2], x_in.at[m], tok_sem.at[0], tok_sem.at[2 + m], 0, batch)

    def cot_copy(m):
        return remote(stage.at[3], do_in.at[m], tok_sem.at[1], tok_sem.at[2 + micro + m], last, batch)

    def side_copy():
        return remote(stage.at[3], stage.at[4], tok_sem.at[1], tok_sem.at[2 + 2 * micro], last - 1, batch)

    def side_last():
        return remote(stage.at[4], do_in.at[0], tok_sem.at[2 + 2 * micro + 1], tok_sem.at[2 + micro], last, batch)

    @pl.when(section != 0)
    def _():
        token_copy(section).start()

    pl.when(section == 0)(lambda: side_copy().start())

    @pl.when((section != last) & (section != 0))
    def _():
        cot_copy(section).start()

    for copy in loads[3:]:
        copy.wait()

    wt[3] = w[3].T

    def flip():
        for j in range(3):
            wt[j] = w[j].T

    pl.when(section > 0)(flip)

    @pl.when(section == last - 1)
    def _():
        side_copy().wait_recv()
        side_last().start()

    def wide(mask):
        return jnp.concatenate([mask] * (width // 128), axis=1)

    def slab(mask):
        return jnp.concatenate([mask] * (LANES // 128), axis=1)

    def fwd_copy(m, c):
        span = pl.ds(pl.multiple_of(c * PART, PART), PART)
        return remote(
            x_out.at[m, span],
            x_in.at[m, span],
            fwd_send.at[within(c, SENDS)],
            fwd_recv.at[m, c],
            jnp.minimum(section + 1, last),
            batch,
        )

    def bwd_copy(m, c):
        span = pl.ds(pl.multiple_of(c * PAIR * PART, PAIR * PART), PAIR * PART)
        return remote(
            dx_out.at[m, span],
            do_in.at[m, span],
            bwd_send.at[within(c, SENDS)],
            bwd_recv.at[m, c],
            jnp.maximum(section - 1, 0),
            batch,
        )

    def around_copy(c):
        span = pl.ds(pl.multiple_of(c * PAIR * PART, PAIR * PART), PAIR * PART)
        return remote(
            dx_out.at[0, span], stage.at[2, span], bwd_send.at[within(c, SENDS)], around_sem.at[0, c], 0, batch
        )

    def around_last(c):
        span = pl.ds(pl.multiple_of(c * PAIR * PART, PAIR * PART), PAIR * PART)
        return remote(stage.at[2, span], do_in.at[0, span], around_sem.at[1, c], bwd_recv.at[0, c], 1, batch)

    def home_copy(source, result, k, m):
        return remote(source.at[m], result.at[0], home_sem.at[k, m], home_sem.at[k, micro], m, batch)

    def keep_copy(source, result, k, m):
        return pltpu.make_async_copy(source.at[m], result.at[0], home_sem.at[k, m])

    high, broad = TILE
    down_n, across = width // high, hidden // broad
    pieces = 4 * down_n * across // 2
    near, far, gifts = sib_in.shape[0], up_in.shape[0], gift_in.shape[0]
    friend = last - section
    give = jnp.where(section == 0, GIVE[0], jnp.where(section == 1, GIVE[1], 0))
    take = jnp.where(friend == 0, GIVE[0], jnp.where(friend == 1, GIVE[1], 0))
    start = jnp.where(section == last, JOIN[0], JOIN[1])

    def place(piece):
        j = 3 - over(piece, down_n * across)
        rest = within(piece, down_n * across)
        row = pl.multiple_of(within(rest, down_n) * high, high)
        col = pl.multiple_of(over(rest, down_n) * broad, broad)
        return j, row, col

    def partial(t):
        j, row, col = place(2 * t)
        from_down = (j == 3) | (feed & (j == 2))
        return dot(left[jnp.where(from_down, 1, 0), pl.ds(row, 2 * high), :], right[j, :, pl.ds(col, broad)])

    def sib_copy(t):
        k = within(t, near)
        return remote(sib_out.at[k], sib_in.at[k], short_sem.at[0, within(t, 4)], near_sem.at[0, k], section, sibling)

    def make(i):
        own[within(i, 4)] = partial(i)
        sib_out[within(i, near)] = own[within(i, 4), pl.ds((1 - core) * high, high), :].astype(BF16)
        sib_copy(i).start()

    def first_tiles():
        left[1] = down[...].T

        @pl.loop(0, NEXT)
        def _(t):
            make(t)

    def forward(m, c, count):
        size = count * PART
        span = pl.ds(pl.multiple_of(c * size, size), size)
        line = pl.ds(pl.multiple_of(m * rows + c * size, size), size)

        @pl.when(section > 0)
        def _():
            for k in range(count):
                fwd_copy(m, c * count + k).wait_recv()

        @pl.when((section == 0) & (c == 0) & (m > 0))
        def _():
            token_copy(m).wait_recv()

        x = x_in[m, span, :].astype(F32)
        valid = valid_s[m, span, :]
        scale = lax.rsqrt(jnp.mean(x * x, axis=-1, keepdims=True) + EPS)
        nb = (x * scale * gain[...]).astype(BF16)
        normed[line, :] = nb

        def mix():
            keep_l = slab(keep_s[m, span, :])
            valid_l = slab(valid)
            for blk in range(hidden // LANES):
                cols = slice(blk * LANES, (blk + 1) * LANES)
                zf = dot(nb, w[0, :, cols]) + bias[0:1, cols]
                zi = dot(nb, w[1, :, cols]) + bias[1:2, cols]
                zh = dot(nb, w[2, :, cols])
                low = jnp.minimum(jnp.minimum(zf, zi), 0.0)
                e0 = jnp.exp(low)
                ei, ef = jnp.exp(low - zi), jnp.exp(low - zf)
                top, bot = e0 + ei, e0 + ef
                inv = 1.0 / (top + bot)
                decay = top * inv
                admit = bot * inv
                a = keep_l * decay
                iv = valid_l * admit
                b = iv * zh
                a_g, b_g = groups(a), groups(b)
                state, product = b_g[0], a_g[0]
                states, products = [state], [product]
                for g in range(1, len(a_g)):
                    state = a_g[g] * state + b_g[g]
                    product = a_g[g] * product
                    states.append(state)
                    products.append(product)
                enter, leave = chain(product, state, h_carry[:, cols], False)
                h_carry[:, cols] = leave
                hs = [s + p * enter for s, p in zip(states, products)]
                h_prev = jnp.concatenate([enter] + hs[:-1], axis=0)
                right[3, line, cols] = jnp.concatenate(hs, axis=0).astype(BF16)
                turn = (keep_l * h_prev - valid_l * zh) * inv
                coef[0, line, cols] = a
                coef[1, line, cols] = decay * ef * turn
                coef[2, line, cols] = -admit * ei * turn
                coef[3, line, cols] = iv
            y = dot(right[3, line, :], wt[3])
            x_out[m, span, :] = (x + wide(valid) * y).astype(BF16)

        def feed_on():
            for k in range(2):
                for blk in range(hidden // LANES):
                    cols = slice(blk * LANES, (blk + 1) * LANES)
                    u = dot(nb, w[k, :, cols]) + bias[k : k + 1, cols]
                    phi = 0.5 + 0.5 * lax.erf(u * math.sqrt(0.5))
                    right[2 + k, line, cols] = (u * phi).astype(BF16)
                    coef[k, line, cols] = phi + u * jnp.exp(-0.5 * u * u) * (1.0 / math.sqrt(2.0 * math.pi))
            y = dot(right[2, line, :], wt[2]) + dot(right[3, line, :], wt[3])
            x_out[m, span, :] = (x + wide(valid) * y).astype(BF16)

        if count == 1:
            pl.when(mixer)(mix)
            pl.when(feed)(feed_on)

            @pl.when(m * parts + c >= SENDS)
            def _():
                fwd_copy(m, c).wait_send()

            fwd_copy(m, c).start()
        else:
            feed_on()
            x_out[m, span, :] = (x_out[m, span, :].astype(F32) * wide(valid)).astype(BF16)

    def backward(m, c):
        size = PAIR * PART
        span = pl.ds(pl.multiple_of(c * size, size), size)
        line = pl.ds(pl.multiple_of(m * rows + c * size, size), size)

        @pl.when(section < last)
        def _():
            bwd_copy(m, c).wait_recv()

        @pl.when((section == last) & (c == 0) & (m != last))
        def _():
            cot_copy(m).wait_recv()

        do = do_in[m, span, :].astype(F32) * wide(valid_s[m, span, :])
        dy = do.astype(BF16)
        down[line, :] = dy
        pl.when((section == 0) & (m == micro - 1) & (c == 0))(first_tiles)

        @pl.when(mixer)
        def _():
            for blk in range(hidden // LANES):
                cols = slice(blk * LANES, (blk + 1) * LANES)
                d_all, a_all = dot(dy, w[3, :, cols]), coef[0, line, cols]
                pieces_dh = []
                for part in range(PAIR - 1, -1, -1):
                    spot = slice(part * PART, (part + 1) * PART)
                    d_g, a_g = groups(d_all[spot]), groups(a_all[spot])
                    count = len(a_g)
                    dhs, spread = [None] * count, [None] * count
                    dhs[-1] = d_g[-1]
                    for g in range(count - 2, -1, -1):
                        dhs[g] = d_g[g] + a_g[g + 1] * dhs[g + 1]
                        spread[g] = a_g[g + 1] if g == count - 2 else a_g[g + 1] * spread[g + 1]
                    enter, leave = chain(a_g[0] * spread[0], a_g[0] * dhs[0], e_carry[:, cols], True)
                    e_carry[:, cols] = leave
                    dhs = [d + s * enter for d, s in zip(dhs[:-1], spread[:-1])] + [dhs[-1] + enter]
                    pieces_dh = dhs + pieces_dh
                dh = jnp.concatenate(pieces_dh, axis=0)
                for j in range(3):
                    dz = dh * coef[1 + j, line, cols]
                    right[j, line, cols] = dz.astype(BF16)
                    if j < 2:
                        bias_acc[j, :, cols] += sum(groups(dz))

        @pl.when(feed)
        def _():
            for k in range(2):
                for blk in range(hidden // LANES):
                    cols = slice(blk * LANES, (blk + 1) * LANES)
                    du = dot(dy, w[2 + k, :, cols]) * coef[k, line, cols]
                    right[k, line, cols] = du.astype(BF16)
                    bias_acc[k, :, cols] += sum(groups(du))

        def finish(dn):
            x = x_in[m, span, :].astype(F32)
            scale = lax.rsqrt(jnp.mean(x * x, axis=-1, keepdims=True) + EPS)
            xr = x * scale
            part = dn * xr
            gain_acc[...] += sum(groups(part))
            dng = dn * gain[...]
            mean = jnp.mean(dng * xr, axis=-1, keepdims=True)
            dx_out[m, span, :] = (do + scale * (dng - xr * mean)).astype(BF16)

        @pl.when(mixer)
        def _():
            finish(
                dot(right[0, line, :], wt[0])
                + dot(right[1, line, :], wt[1])
                + dot(right[2, line, :], wt[2])
            )

        @pl.when(feed)
        def _():
            finish(dot(right[0, line, :], wt[0]) + dot(right[1, line, :], wt[1]))

        @pl.when(section > 0)
        def _():
            @pl.when((m > 0) if SENDS >= parts // PAIR else (m * (parts // PAIR) + parts // PAIR - 1 - c >= SENDS))
            def _():
                bwd_copy(m, c).wait_send()

            by_side = (section == 2) & (m == 0)
            pl.when(by_side)(lambda: around_copy(c).start())
            pl.when(jnp.logical_not(by_side))(lambda: bwd_copy(m, c).start())

    halves = parts // PAIR

    @pl.loop(0, jnp.where(section == last, 2 * micro * halves, micro * (parts + halves)))
    def _(step):
        pl.when((section == 0) & (step == parts))(flip)

        @pl.when(step == jnp.where(section == last, 2 * micro * halves - 1, micro * parts + halves + 1))
        def _():
            left[0] = normed[...].T


        early = (section == 2) & (step >= (micro - 1) * parts)
        back_now = jnp.where(early, step < (micro - 1) * parts + halves, step >= micro * parts)
        back_now = back_now | (step >= micro * parts + halves)
        f_step = jnp.where(early, step - halves, step)
        late = jnp.where(early & (step < (micro - 1) * parts + halves), step - (micro - 1) * parts, step - micro * parts)

        @pl.when((section < last) & jnp.logical_not(back_now))
        def _():
            forward(over(f_step, parts), within(f_step, parts), 1)

        turn = over(step, 2)

        @pl.when((section == 0) & (step == micro * parts))
        def _():
            for c in range(halves - 1, -1, -1):
                around_copy(c).wait_recv()
                around_last(c).start()

        @pl.when((section == last) & (within(step, 2) == 0) & (turn < micro * halves))
        def _():
            forward(over(turn, halves), within(turn, halves), PAIR)

        @pl.when(jnp.where(section == last, (within(step, 2) == 1) & (turn < micro * halves), back_now))
        def _():
            q = jnp.where(section == last, turn, jnp.maximum(late, 0))
            c = within(q, halves)
            backward(over(q, halves), jnp.where(section == last, c, halves - 1 - c))

    def homeward(act):
        for m in range(micro):
            for k, source, result, at in ((0, x_out, final_out, last), (1, dx_out, grad_out, 0)):

                @pl.when((section == at) & (section != m))
                def _():
                    act(home_copy(source, result, k, m), True)

                @pl.when((section == at) & (section == m))
                def _():
                    act(keep_copy(source, result, k, m), False)

    def is_given(t):
        return (within(t, 2) == 1) & (over(t, 2) < give)

    def chain_index(t):
        return t - jnp.minimum(over(t, 2), give)

    def is_taken(t):
        return (t >= start) & (t < start + take)

    def own_index(t):
        return t - jnp.clip(t - start, 0, take)

    def gift_copy(d):
        return remote(gift_out.at[d], gift_in.at[d], gift_sem.at[0, d], gift_sem.at[1, d], friend, batch)

    def back_copy(r, d):
        return remote(
            tot_out.at[within(r, far)], back_in.at[d], mid_sem.at[3, within(d, 8)], gift_sem.at[2, d], friend, batch
        )

    def back_share(d):
        return remote(
            back_in.at[d], back_sib.at[d], short_sem.at[2, within(d, 4)], gift_sem.at[3, d], section, sibling
        )

    def store_back(d, source, who, sem):
        j, row, col = place(4 * d + 2 + who)
        return pltpu.make_async_copy(
            source.at[d], wide_out.at[j, pl.ds(row, high), pl.ds(col, broad)], sem
        )

    def up_copy(k):
        k = within(k, far)
        return remote(up_out.at[k], up_in.at[k], far_sem.at[0, k], far_sem.at[1, k], section, inner)

    def mirror_copy(k):
        k = within(k, far)
        return remote(up_out.at[k], ret_in.at[k], far_sem.at[0, k], far_sem.at[2, k], section, inner)

    def ret_copy(k):
        k = within(k, far)
        return remote(tot_out.at[k], ret_in.at[k], mid_sem.at[0, within(k, 8)], far_sem.at[2, k], section, outer)

    def share_copy(r):
        k, at = within(r, far), within(own_index(r), near)
        return remote(tot_out.at[k], tot_in.at[at], mid_sem.at[1, within(r, 8)], near_sem.at[1, at], section, sibling)

    def piece_of(r):
        return jnp.where(r < give, 2 * r, own_index(r) + give)

    def store_own(r):
        j, row, col = place(2 * piece_of(r) + core)
        k = within(r, far)
        return pltpu.make_async_copy(
            tot_out.at[k], wide_out.at[j, pl.ds(row, high), pl.ds(col, broad)], mid_sem.at[2, within(r, 8)]
        )

    def store_other(r):
        j, row, col = place(2 * piece_of(r) + 1 - core)
        k = within(own_index(r), near)
        return pltpu.make_async_copy(
            tot_in.at[k], wide_out.at[j, pl.ds(row, high), pl.ds(col, broad)], short_sem.at[1, within(k, 4)]
        )

    def is_result(r):
        return (r >= 0) & (r < pieces - give + take)

    lag = jnp.minimum(NEXT + 3 + 8 * depth, LAG)
    small_at = NEXT + 4 + 4 * (half - 1 - depth)
    small_back = NEXT + 4 + 4 * half + 4 * depth

    def small_fill():
        for k in range(2):
            small[0, k : k + 1, :] = jnp.sum(bias_acc[k], axis=0, keepdims=True)
        small[0, 2:3, 0:width] = jnp.sum(gain_acc[...], axis=0, keepdims=True)
        small[0, 2:3, width:] = jnp.zeros((1, hidden - width), F32)
        small[0, 3:8, :] = jnp.zeros((5, hidden), F32)

    def small_sib():
        return remote(small.at[0], small.at[1], small_sem.at[0], small_sem.at[1], section, sibling)

    def small_up(to):
        return remote(small.at[2], small.at[to], small_sem.at[2], small_sem.at[to], section, inner)

    def small_ret():
        return remote(small.at[5], small.at[4], small_sem.at[5], small_sem.at[4], section, outer)

    def small_step(t):
        @pl.when(t == NEXT)
        def _():
            small_fill()
            small_sib().start()

        @pl.when(t == small_at)
        def _():
            small_sib().wait_recv()
            small[2] = small[0] + small[1]

            @pl.when(has_outer)
            def _():
                small_up(3).wait_recv()
                small[2] = small[2] + small[3]

            @pl.when(middle)
            def _():
                small_up(4).start()

            @pl.when(jnp.logical_not(middle))
            def _():
                small_up(3).start()

        @pl.when(t == small_back)
        def _():
            small_up(4).wait_recv()

            @pl.when(middle)
            def _():
                small[5] = small[2] + small[4]

            @pl.when(jnp.logical_not(middle))
            def _():
                small[5] = small[4]

            @pl.when(has_outer)
            def _():
                small_ret().start()

    pl.when(section > 0)(first_tiles)

    end = jnp.maximum(pieces + take + lag + 5, jnp.maximum(small_back + 1, LATE + give + 4))

    @pl.loop(NEXT, end)
    def _(t):
        @pl.when((t < pieces + take) & jnp.logical_not(is_taken(t)))
        def _():
            make(own_index(t))

        s = t - NEXT

        @pl.when((s >= 0) & (s < pieces + take))
        def _():
            i = own_index(s)
            k = chain_index(s)
            slot = within(k, far)

            def onward(total):
                @pl.when(has_outer)
                def _():
                    up_copy(k).wait_recv()
                    up_out[slot] = (total + up_in[slot].astype(F32)).astype(BF16)

                @pl.when(jnp.logical_not(has_outer))
                def _():
                    up_out[slot] = total.astype(BF16)

                @pl.when(middle)
                def _():
                    mirror_copy(k).start()

                @pl.when(jnp.logical_not(middle))
                def _():
                    up_copy(k).start()

            @pl.when(jnp.logical_not(is_taken(s)))
            def _():
                sib_copy(i).wait()
                total = own[within(i, 4), pl.ds(core * high, high), :] + sib_in[within(i, near)].astype(F32)

                @pl.when(is_given(s))
                def _():
                    d = over(s, 2)
                    gift_out[d] = total.astype(BF16)
                    gift_copy(d).start()

                @pl.when(jnp.logical_not(is_given(s)))
                def _():
                    onward(total)

            @pl.when(is_taken(s))
            def _():
                d = s - start
                gift_copy(d).wait_recv()
                onward(gift_in[d].astype(F32))

        on = jnp.logical_not(is_given(t))
        r = chain_index(t) - lag
        slot = within(r, far)

        @pl.when(on & is_result(r))
        def _():
            mirror_copy(r).wait()

            @pl.when(middle)
            def _():
                tot_out[slot] = (up_out[slot].astype(F32) + ret_in[slot].astype(F32)).astype(BF16)

            @pl.when(jnp.logical_not(middle))
            def _():
                tot_out[slot] = ret_in[slot]

            @pl.when(has_outer)
            def _():
                ret_copy(r).start()

            @pl.when(is_taken(r))
            def _():
                back_copy(r, r - start).start()

            @pl.when(jnp.logical_not(is_taken(r)))
            def _():
                share_copy(r).start()
                store_own(r).start()

        r2 = r - 2

        @pl.when(on & is_result(r2) & jnp.logical_not(is_taken(r2)))
        def _():
            share_copy(r2).wait_recv()
            store_other(r2).start()

        r4 = r - 4

        @pl.when(on & is_result(r4))
        def _():
            @pl.when(has_outer)
            def _():
                ret_copy(r4).wait_send()

            @pl.when(is_taken(r4))
            def _():
                back_copy(r4, r4 - start).wait_send()

            @pl.when(jnp.logical_not(is_taken(r4)))
            def _():
                share_copy(r4).wait_send()
                store_own(r4).wait()
                store_other(r4).wait()

        d = t - LATE

        @pl.when((d >= 0) & (d < give))
        def _():
            gift_copy(d).wait_send()
            back_copy(r, d).wait_recv()
            back_share(d).start()
            store_back(d, back_in, core, mid_sem.at[4, within(d, 8)]).start()

        d2 = d - 2

        @pl.when((d2 >= 0) & (d2 < give))
        def _():
            back_share(d2).wait()
            store_back(d2, back_sib, 1 - core, short_sem.at[3, within(d2, 4)]).start()

        d4 = d - 4

        @pl.when((d4 >= 0) & (d4 < give))
        def _():
            store_back(d4, back_in, core, mid_sem.at[4, within(d4, 8)]).wait()
            store_back(d4, back_sib, 1 - core, short_sem.at[3, within(d4, 4)]).wait()

        pl.when(t == 2 * gifts + 2)(lambda: homeward(lambda copy, far: copy.start()))
        small_step(t)

    small_out[...] = small[5] * (1.0 / math.sqrt(micro * rows * batches))

    small_sib().wait_send()
    small_up(3).wait_send()

    @pl.when(has_outer)
    def _():
        small_ret().wait_send()

    @pl.when(section != 0)
    def _():
        token_copy(section).wait_send()

    pl.when(section == 0)(lambda: side_copy().wait_send())

    @pl.when(section == 0)
    def _():
        for c in range(halves):
            around_last(c).wait_send()

    pl.when(section == last - 1)(lambda: side_last().wait_send())

    @pl.when((section != last) & (section != 0))
    def _():
        cot_copy(section).wait_send()

    for c in range(SENDS):

        @pl.when(section != last)
        def _():
            fwd_copy(0, c).wait_send()

        @pl.when(section != 0)
        def _():
            bwd_copy(0, c).wait_send()

    homeward(lambda copy, far: copy.wait_send() if far else copy.wait())

    @pl.when(section != last)
    def _():
        home_copy(x_out, final_out, 0, section).wait_recv()

    @pl.when(section != 0)
    def _():
        home_copy(dx_out, grad_out, 1, section).wait_recv()


def finish_kernel(scale, wide, small, final_in, grad_in, final, grad, weight, bias, gain, full, turned, sums, norms, sem):
    depth = wide.shape[1] // CUTS
    stores = []
    for n in range(wide.shape[0] * CUTS):
        j, span = n // CUTS, pl.ds((n % CUTS) * depth, depth)
        full[j, span, :] = wide[j, span, :].astype(F32) * scale
        stores.append(pltpu.make_async_copy(full.at[j, span], weight.at[0, j, span], sem.at[n]))
        stores[-1].start()
    sums[0] = small[0:2, :]
    norms[...] = small[2:3, 0 : norms.shape[1]]
    for source, result in ((sums, bias), (norms, gain)):
        stores.append(pltpu.make_async_copy(source, result, sem.at[len(stores)]))
        stores[-1].start()
    order = order_matrix(PART, True)
    for k, (source, result) in enumerate(((final_in, final), (grad_in, grad))):
        for c in range(source.shape[1] // PART):
            span = slice(c * PART, (c + 1) * PART)
            turned[k, span, :] = dot(order, source[0, span, :]).astype(BF16)
        stores.append(pltpu.make_async_copy(turned.at[k], result.at[0], sem.at[len(stores)]))
        stores[-1].start()
    for copy in stores:
        copy.wait()


def local(tokens, cotangent, weights, biases, gains, lengths):
    micro = lengths.shape[0]
    _, rows, width = tokens.shape
    hidden = weights.shape[3]
    parts = rows // PART
    pieces = 4 * width * hidden // (TILE[0] * TILE[1]) // 2
    any_spec = pl.BlockSpec(memory_space=pl.ANY)
    vmem = pl.BlockSpec(memory_space=pltpu.VMEM)
    dma = pltpu.SemaphoreType.DMA
    relay = pltpu.VMEM((micro, rows, width), BF16)
    near = min(8, pieces)
    far = 16
    close = pltpu.VMEM((near, *TILE), BF16)
    wait = pltpu.VMEM((far, *TILE), BF16)
    final, grad, wide, small = pl.pallas_call(
        relay_kernel,
        name="relay",
        out_shape=(
            pltpu.VMEM(tokens.shape, BF16),
            pltpu.VMEM(tokens.shape, BF16),
            pltpu.VMEM((4, width, hidden), BF16),
            pltpu.VMEM((8, hidden), F32),
        ),
        in_specs=[any_spec] * 6,
        out_specs=(vmem, vmem, vmem, vmem),
        scratch_shapes=[
            pltpu.VMEM((4, width, hidden), BF16),
            pltpu.VMEM((4, hidden, width), BF16),
            pltpu.VMEM(lengths.shape[::-1], jnp.int32),
            pltpu.VMEM((2, hidden), F32),
            pltpu.VMEM((1, width), F32),
            pltpu.VMEM((5, rows, width), BF16),
            relay,
            relay,
            relay,
            relay,
            pltpu.VMEM((micro, rows, 128), F32),
            pltpu.VMEM((micro, rows, 128), F32),
            pltpu.VMEM((micro * rows, width), BF16),
            pltpu.VMEM((micro * rows, width), BF16),
            pltpu.VMEM((4, micro * rows, hidden), BF16),
            pltpu.VMEM((4, micro * rows, hidden), F32),
            pltpu.VMEM((8, hidden), F32),
            pltpu.VMEM((8, hidden), F32),
            pltpu.VMEM((8, width), F32),
            pltpu.VMEM((2, 8, hidden), F32),
            close,
            close,
            pltpu.VMEM((4, 2 * TILE[0], TILE[1]), F32),
            wait,
            wait,
            wait,
            wait,
            close,
            pltpu.VMEM((6, 8, hidden), F32),
            pltpu.VMEM((2, width, micro * rows), BF16),
            *[pltpu.VMEM((max(GIVE), *TILE), BF16)] * 4,
            dma((9,)),
            dma((4 + 2 * micro,)),
            dma((SENDS,)),
            dma((micro, parts)),
            dma((SENDS,)),
            dma((micro, parts // PAIR)),
            dma((2, parts // PAIR)),
            dma((2, micro + 1)),
            dma((2, near)),
            dma((3, far)),
            dma((4, max(GIVE))),
            dma((5, 8)),
            dma((4, 4)),
            dma((6,)),
        ],
        compiler_params=pltpu.CompilerParams(
            collective_id=0, has_side_effects=True, vmem_limit_bytes=55 * 2**20
        ),
    )(lengths.T, tokens, cotangent, weights, biases, gains)
    scale = 1.0 / math.sqrt(micro * rows * lax.axis_size("batch"))
    return pl.pallas_call(
        functools.partial(finish_kernel, scale),
        name="finish",
        out_shape=(
            jax.ShapeDtypeStruct(tokens.shape, BF16),
            jax.ShapeDtypeStruct(tokens.shape, BF16),
            jax.ShapeDtypeStruct(weights.shape, F32),
            jax.ShapeDtypeStruct(biases.shape, F32),
            jax.ShapeDtypeStruct(gains.shape, F32),
        ),
        in_specs=[vmem, vmem, vmem, vmem],
        out_specs=(any_spec,) * 5,
        scratch_shapes=[
            pltpu.VMEM((4, width, hidden), F32),
            pltpu.VMEM((2, rows, width), BF16),
            pltpu.VMEM(biases.shape, F32),
            pltpu.VMEM(gains.shape, F32),
            dma((4 * CUTS + 4,)),
        ],
        compiler_params=pltpu.CompilerParams(vmem_limit_bytes=24 * 2**20),
    )(*[pltpu.with_memory_space_constraint(value, pltpu.VMEM) for value in (wide, small, final, grad)])


def solution(mesh):
    row = P("section", "batch", None)
    placed = (
        row,
        row,
        P("section", None, None, None),
        P("section", None, None),
        P("section", None),
        P(None, "batch"),
    )
    return jax.shard_map(
        local,
        mesh=mesh,
        in_specs=placed,
        out_specs=(row, row, *placed[2:5]),
        check_vma=False,
    )
```

```python
import functools
import math

import jax
import jax.numpy as jnp
from jax import lax
from jax.experimental import pallas as pl
from jax.experimental.pallas import tpu as pltpu
from jax.sharding import PartitionSpec as P

MESH = pl.DeviceIdType.MESH
EPS = 1e-05
PART = 64
PAIR = 2
GIVE = (9, 3)
JOIN = (24, 10)
LATE = 36
NEXT = 3
LAG = 14
CUTS = 4
SENDS = 2
LANES = 256
TILE = (128, 256)
F32 = jnp.float32
BF16 = jnp.bfloat16


def dot(a, b):
    return jnp.dot(a, b, preferred_element_type=F32)


def over(value, count):
    return lax.shift_right_logical(value, count.bit_length() - 1)


def within(value, count):
    return lax.bitwise_and(value, count - 1)


def order_matrix(rows, back):
    new = lax.broadcasted_iota(jnp.int32, (rows, rows), 1 if back else 0)
    old = lax.broadcasted_iota(jnp.int32, (rows, rows), 0 if back else 1)
    hit = (within(new, 8) * (rows // 8) + over(new, 8)) == old
    return jnp.where(hit, 1.0, 0.0).astype(BF16)


def groups(value):
    return [value[8 * g : 8 * g + 8] for g in range(value.shape[0] // 8)]


def chain(gain, add, carry, back):
    row = lax.broadcasted_iota(jnp.int32, gain.shape, 0)
    for step in (1, 2, 4):
        shift = 8 - step if back else step
        inside = (row < 8 - step) if back else (row >= step)
        add = jnp.where(inside, gain * pltpu.roll(add, shift, 0) + add, add)
        gain = jnp.where(inside, gain * pltpu.roll(gain, shift, 0), gain)
    whole = gain * carry + add
    edge = 7 if back else 0
    enter = jnp.where(row == edge, carry, pltpu.roll(whole, 7 if back else 1, 0))
    last = whole[0:1] if back else whole[7:8]
    return enter, jnp.broadcast_to(last, gain.shape)


def relay_kernel(
    lengths_in,
    tokens,
    cotangent,
    weights,
    biases,
    gains,
    final_out,
    grad_out,
    wide_out,
    small_out,
    w,
    wt,
    lengths,
    bias,
    gain,
    stage,
    x_in,
    do_in,
    x_out,
    dx_out,
    valid_s,
    keep_s,
    normed,
    down,
    right,
    coef,
    h_carry,
    e_carry,
    gain_acc,
    bias_acc,
    sib_out,
    sib_in,
    own,
    up_out,
    up_in,
    ret_in,
    tot_out,
    tot_in,
    small,
    left,
    gift_out,
    gift_in,
    back_in,
    back_sib,
    load_sem,
    tok_sem,
    fwd_send,
    fwd_recv,
    bwd_send,
    bwd_recv,
    around_sem,
    home_sem,
    near_sem,
    far_sem,
    gift_sem,
    mid_sem,
    short_sem,
    small_sem,
):
    micro, rows, width = x_in.shape
    parts = rows // PART
    hidden = w.shape[2]
    section, batch = lax.axis_index("section"), lax.axis_index("batch")
    sections, batches = lax.axis_size("section"), lax.axis_size("batch")
    last = sections - 1
    mixer = lax.rem(section, 2) == 0
    feed = lax.rem(section, 2) == 1
    chips = batches // 2
    chip, core = batch // 2, lax.rem(batch, 2)
    sibling = batch + 1 - 2 * core
    half = chips // 2
    low_side = chip < half
    step_in = jnp.where(low_side, 2, -2)
    inner = batch + step_in
    outer = batch - step_in
    middle = (chip == half - 1) | (chip == half)
    has_outer = (chip > 0) & (chip < chips - 1)
    depth = jnp.where(low_side, half - 1 - chip, chip - half)

    def remote(src, dst, send, recv, to_section, to_batch):
        return pltpu.make_async_remote_copy(
            src_ref=src,
            dst_ref=dst,
            send_sem=send,
            recv_sem=recv,
            device_id=(to_section, to_batch),
            device_id_type=MESH,
        )

    sources = [
        (tokens.at[0], stage.at[0]),
        (cotangent.at[0], stage.at[1]),
        (lengths_in, lengths),
        (biases.at[0], bias),
        (gains, gain),
        *[(weights.at[0, j], w.at[j]) for j in (3, 0, 1, 2)],
    ]
    loads = [pltpu.make_async_copy(src, dst, load_sem.at[i]) for i, (src, dst) in enumerate(sources)]
    for copy in loads:
        copy.start()

    barrier = pltpu.get_barrier_semaphore()
    for other in range(1, sections):
        pl.semaphore_signal(
            barrier, inc=1, device_id=(lax.rem(section + other, sections), batch), device_id_type=MESH
        )
    pl.semaphore_signal(barrier, inc=1, device_id=(section, sibling), device_id_type=MESH)
    pl.semaphore_signal(barrier, inc=1, device_id=(section, inner), device_id_type=MESH)

    @pl.when(has_outer)
    def _():
        pl.semaphore_signal(barrier, inc=1, device_id=(section, outer), device_id_type=MESH)

    loads[2].wait()
    spot = lax.broadcasted_iota(jnp.int32, (rows, 128), 0)
    spot_in = within(spot, PART)
    spot = spot - spot_in + within(spot_in, 8) * (PART // 8) + over(spot_in, 8)
    for m in range(micro):
        end = jnp.zeros((1, 1), jnp.int32)
        start_hit = jnp.zeros((rows, 128), F32)
        for k in range(lengths.shape[0]):
            start_hit = jnp.where(spot == end, 1.0, start_hit)
            end = end + lengths[k : k + 1, m : m + 1]
        valid = jnp.where(spot < end, 1.0, 0.0)
        valid_s[m] = valid
        keep_s[m] = valid * (1.0 - start_hit)
    h_carry[...] = jnp.zeros_like(h_carry)
    e_carry[...] = jnp.zeros_like(e_carry)
    gain_acc[...] = jnp.zeros_like(gain_acc)
    bias_acc[...] = jnp.zeros_like(bias_acc)

    perm = order_matrix(PART, False)
    loads[0].wait()
    for c in range(parts):
        span = pl.ds(c * PART, PART)
        ordered = dot(perm, stage[0, span, :]).astype(BF16)
        stage[2, span, :] = ordered

        @pl.when(section == 0)
        def _():
            x_in[0, span, :] = ordered

    loads[1].wait()
    for c in range(parts):
        span = pl.ds(c * PART, PART)
        ordered = dot(perm, stage[1, span, :]).astype(BF16)
        stage[3, span, :] = ordered

        @pl.when(section == last)
        def _():
            do_in[last, span, :] = ordered

    pl.semaphore_wait(barrier, sections + 1 + jnp.where(has_outer, 1, 0))

    def token_copy(m):
        return remote(stage.at[2], x_in.at[m], tok_sem.at[0], tok_sem.at[2 + m], 0, batch)

    def cot_copy(m):
        return remote(stage.at[3], do_in.at[m], tok_sem.at[1], tok_sem.at[2 + micro + m], last, batch)

    def side_copy():
        return remote(stage.at[3], stage.at[4], tok_sem.at[1], tok_sem.at[2 + 2 * micro], last - 1, batch)

    def side_last():
        return remote(stage.at[4], do_in.at[0], tok_sem.at[2 + 2 * micro + 1], tok_sem.at[2 + micro], last, batch)

    @pl.when(section != 0)
    def _():
        token_copy(section).start()

    pl.when(section == 0)(lambda: side_copy().start())

    @pl.when((section != last) & (section != 0))
    def _():
        cot_copy(section).start()

    for copy in loads[3:]:
        copy.wait()

    wt[3] = w[3].T

    def flip():
        for j in range(3):
            wt[j] = w[j].T

    pl.when(section > 0)(flip)

    @pl.when(section == last - 1)
    def _():
        side_copy().wait_recv()
        side_last().start()

    def wide(mask):
        return jnp.concatenate([mask] * (width // 128), axis=1)

    def slab(mask):
        return jnp.concatenate([mask] * (LANES // 128), axis=1)

    def fwd_copy(m, c):
        span = pl.ds(pl.multiple_of(c * PART, PART), PART)
        return remote(
            x_out.at[m, span],
            x_in.at[m, span],
            fwd_send.at[within(c, SENDS)],
            fwd_recv.at[m, c],
            jnp.minimum(section + 1, last),
            batch,
        )

    def bwd_copy(m, c):
        span = pl.ds(pl.multiple_of(c * PAIR * PART, PAIR * PART), PAIR * PART)
        return remote(
            dx_out.at[m, span],
            do_in.at[m, span],
            bwd_send.at[within(c, SENDS)],
            bwd_recv.at[m, c],
            jnp.maximum(section - 1, 0),
            batch,
        )

    def around_copy(c):
        span = pl.ds(pl.multiple_of(c * PAIR * PART, PAIR * PART), PAIR * PART)
        return remote(
            dx_out.at[0, span], stage.at[2, span], bwd_send.at[within(c, SENDS)], around_sem.at[0, c], 0, batch
        )

    def around_last(c):
        span = pl.ds(pl.multiple_of(c * PAIR * PART, PAIR * PART), PAIR * PART)
        return remote(stage.at[2, span], do_in.at[0, span], around_sem.at[1, c], bwd_recv.at[0, c], 1, batch)

    def home_copy(source, result, k, m):
        return remote(source.at[m], result.at[0], home_sem.at[k, m], home_sem.at[k, micro], m, batch)

    def keep_copy(source, result, k, m):
        return pltpu.make_async_copy(source.at[m], result.at[0], home_sem.at[k, m])

    high, broad = TILE
    down_n, across = width // high, hidden // broad
    pieces = 4 * down_n * across // 2
    near, far, gifts = sib_in.shape[0], up_in.shape[0], gift_in.shape[0]
    friend = last - section
    give = jnp.where(section == 0, GIVE[0], jnp.where(section == 1, GIVE[1], 0))
    take = jnp.where(friend == 0, GIVE[0], jnp.where(friend == 1, GIVE[1], 0))
    start = jnp.where(section == last, JOIN[0], JOIN[1])

    def place(piece):
        j = 3 - over(piece, down_n * across)
        rest = within(piece, down_n * across)
        row = pl.multiple_of(within(rest, down_n) * high, high)
        col = pl.multiple_of(over(rest, down_n) * broad, broad)
        return j, row, col

    def partial(t):
        j, row, col = place(2 * t)
        from_down = (j == 3) | (feed & (j == 2))
        return dot(left[jnp.where(from_down, 1, 0), pl.ds(row, 2 * high), :], right[j, :, pl.ds(col, broad)])

    def sib_copy(t):
        k = within(t, near)
        return remote(sib_out.at[k], sib_in.at[k], short_sem.at[0, within(t, 4)], near_sem.at[0, k], section, sibling)

    def make(i):
        own[within(i, 4)] = partial(i)
        sib_out[within(i, near)] = own[within(i, 4), pl.ds((1 - core) * high, high), :].astype(BF16)
        sib_copy(i).start()

    def first_tiles():
        left[1] = down[...].T

        @pl.loop(0, NEXT)
        def _(t):
            make(t)

    def forward(m, c, count):
        size = count * PART
        span = pl.ds(pl.multiple_of(c * size, size), size)
        line = pl.ds(pl.multiple_of(m * rows + c * size, size), size)

        @pl.when(section > 0)
        def _():
            for k in range(count):
                fwd_copy(m, c * count + k).wait_recv()

        @pl.when((section == 0) & (c == 0) & (m > 0))
        def _():
            token_copy(m).wait_recv()

        x = x_in[m, span, :].astype(F32)
        valid = valid_s[m, span, :]
        scale = lax.rsqrt(jnp.mean(x * x, axis=-1, keepdims=True) + EPS)
        nb = (x * scale * gain[...]).astype(BF16)
        normed[line, :] = nb

        def mix():
            keep_l = slab(keep_s[m, span, :])
            valid_l = slab(valid)
            for blk in range(hidden // LANES):
                cols = slice(blk * LANES, (blk + 1) * LANES)
                zf = dot(nb, w[0, :, cols]) + bias[0:1, cols]
                zi = dot(nb, w[1, :, cols]) + bias[1:2, cols]
                zh = dot(nb, w[2, :, cols])
                low = jnp.minimum(jnp.minimum(zf, zi), 0.0)
                e0 = jnp.exp(low)
                ei, ef = jnp.exp(low - zi), jnp.exp(low - zf)
                top, bot = e0 + ei, e0 + ef
                inv = 1.0 / (top + bot)
                decay = top * inv
                admit = bot * inv
                a = keep_l * decay
                iv = valid_l * admit
                b = iv * zh
                a_g, b_g = groups(a), groups(b)
                state, product = b_g[0], a_g[0]
                states, products = [state], [product]
                for g in range(1, len(a_g)):
                    state = a_g[g] * state + b_g[g]
                    product = a_g[g] * product
                    states.append(state)
                    products.append(product)
                enter, leave = chain(product, state, h_carry[:, cols], False)
                h_carry[:, cols] = leave
                hs = [s + p * enter for s, p in zip(states, products)]
                h_prev = jnp.concatenate([enter] + hs[:-1], axis=0)
                right[3, line, cols] = jnp.concatenate(hs, axis=0).astype(BF16)
                turn = (keep_l * h_prev - valid_l * zh) * inv
                coef[0, line, cols] = a
                coef[1, line, cols] = decay * ef * turn
                coef[2, line, cols] = -admit * ei * turn
                coef[3, line, cols] = iv
            y = dot(right[3, line, :], wt[3])
            x_out[m, span, :] = (x + wide(valid) * y).astype(BF16)

        def feed_on():
            for k in range(2):
                for blk in range(hidden // LANES):
                    cols = slice(blk * LANES, (blk + 1) * LANES)
                    u = dot(nb, w[k, :, cols]) + bias[k : k + 1, cols]
                    phi = 0.5 + 0.5 * lax.erf(u * math.sqrt(0.5))
                    right[2 + k, line, cols] = (u * phi).astype(BF16)
                    coef[k, line, cols] = phi + u * jnp.exp(-0.5 * u * u) * (1.0 / math.sqrt(2.0 * math.pi))
            y = dot(right[2, line, :], wt[2]) + dot(right[3, line, :], wt[3])
            x_out[m, span, :] = (x + wide(valid) * y).astype(BF16)

        if count == 1:
            pl.when(mixer)(mix)
            pl.when(feed)(feed_on)

            @pl.when(m * parts + c >= SENDS)
            def _():
                fwd_copy(m, c).wait_send()

            fwd_copy(m, c).start()
        else:
            feed_on()
            x_out[m, span, :] = (x_out[m, span, :].astype(F32) * wide(valid)).astype(BF16)

    def backward(m, c):
        size = PAIR * PART
        span = pl.ds(pl.multiple_of(c * size, size), size)
        line = pl.ds(pl.multiple_of(m * rows + c * size, size), size)

        @pl.when(section < last)
        def _():
            bwd_copy(m, c).wait_recv()

        @pl.when((section == last) & (c == 0) & (m != last))
        def _():
            cot_copy(m).wait_recv()

        do = do_in[m, span, :].astype(F32) * wide(valid_s[m, span, :])
        dy = do.astype(BF16)
        down[line, :] = dy
        pl.when((section == 0) & (m == micro - 1) & (c == 0))(first_tiles)

        @pl.when(mixer)
        def _():
            for blk in range(hidden // LANES):
                cols = slice(blk * LANES, (blk + 1) * LANES)
                d_all, a_all = dot(dy, w[3, :, cols]), coef[0, line, cols]
                pieces_dh = []
                for part in range(PAIR - 1, -1, -1):
                    spot = slice(part * PART, (part + 1) * PART)
                    d_g, a_g = groups(d_all[spot]), groups(a_all[spot])
                    count = len(a_g)
                    dhs, spread = [None] * count, [None] * count
                    dhs[-1] = d_g[-1]
                    for g in range(count - 2, -1, -1):
                        dhs[g] = d_g[g] + a_g[g + 1] * dhs[g + 1]
                        spread[g] = a_g[g + 1] if g == count - 2 else a_g[g + 1] * spread[g + 1]
                    enter, leave = chain(a_g[0] * spread[0], a_g[0] * dhs[0], e_carry[:, cols], True)
                    e_carry[:, cols] = leave
                    dhs = [d + s * enter for d, s in zip(dhs[:-1], spread[:-1])] + [dhs[-1] + enter]
                    pieces_dh = dhs + pieces_dh
                dh = jnp.concatenate(pieces_dh, axis=0)
                for j in range(3):
                    dz = dh * coef[1 + j, line, cols]
                    right[j, line, cols] = dz.astype(BF16)
                    if j < 2:
                        bias_acc[j, :, cols] += sum(groups(dz))

        @pl.when(feed)
        def _():
            for k in range(2):
                for blk in range(hidden // LANES):
                    cols = slice(blk * LANES, (blk + 1) * LANES)
                    du = dot(dy, w[2 + k, :, cols]) * coef[k, line, cols]
                    right[k, line, cols] = du.astype(BF16)
                    bias_acc[k, :, cols] += sum(groups(du))

        def finish(dn):
            x = x_in[m, span, :].astype(F32)
            scale = lax.rsqrt(jnp.mean(x * x, axis=-1, keepdims=True) + EPS)
            xr = x * scale
            part = dn * xr
            gain_acc[...] += sum(groups(part))
            dng = dn * gain[...]
            mean = jnp.mean(dng * xr, axis=-1, keepdims=True)
            dx_out[m, span, :] = (do + scale * (dng - xr * mean)).astype(BF16)

        @pl.when(mixer)
        def _():
            finish(
                dot(right[0, line, :], wt[0])
                + dot(right[1, line, :], wt[1])
                + dot(right[2, line, :], wt[2])
            )

        @pl.when(feed)
        def _():
            finish(dot(right[0, line, :], wt[0]) + dot(right[1, line, :], wt[1]))

        @pl.when(section > 0)
        def _():
            @pl.when((m > 0) if SENDS >= parts // PAIR else (m * (parts // PAIR) + parts // PAIR - 1 - c >= SENDS))
            def _():
                bwd_copy(m, c).wait_send()

            by_side = (section == 2) & (m == 0)
            pl.when(by_side)(lambda: around_copy(c).start())
            pl.when(jnp.logical_not(by_side))(lambda: bwd_copy(m, c).start())

    halves = parts // PAIR

    @pl.loop(0, micro * (parts + halves))
    def _(step):
        pl.when((section == 0) & (step == parts))(flip)

        @pl.when(step == micro * parts + halves + 1)
        def _():
            left[0] = normed[...].T


        early = (section == 2) & (step >= (micro - 1) * parts)
        back_now = jnp.where(early, step < (micro - 1) * parts + halves, step >= micro * parts)
        back_now = back_now | (step >= micro * parts + halves)
        f_step = jnp.where(early, step - halves, step)
        late = jnp.where(early & (step < (micro - 1) * parts + halves), step - (micro - 1) * parts, step - micro * parts)

        @pl.when((section < last) & jnp.logical_not(back_now))
        def _():
            forward(over(f_step, parts), within(f_step, parts), 1)

        turn = over(step, 2)

        @pl.when((section == 0) & (step == micro * parts))
        def _():
            for c in range(halves - 1, -1, -1):
                around_copy(c).wait_recv()
                around_last(c).start()

        @pl.when((section == last) & (within(step, 2) == 0) & (turn < micro * halves))
        def _():
            forward(over(turn, halves), within(turn, halves), PAIR)

        @pl.when(jnp.where(section == last, (within(step, 2) == 1) & (turn < micro * halves), back_now))
        def _():
            q = jnp.where(section == last, turn, jnp.maximum(late, 0))
            c = within(q, halves)
            backward(over(q, halves), jnp.where(section == last, c, halves - 1 - c))

    def homeward(act):
        for m in range(micro):
            for k, source, result, at in ((0, x_out, final_out, last), (1, dx_out, grad_out, 0)):

                @pl.when((section == at) & (section != m))
                def _():
                    act(home_copy(source, result, k, m), True)

                @pl.when((section == at) & (section == m))
                def _():
                    act(keep_copy(source, result, k, m), False)

    def is_given(t):
        return (within(t, 2) == 1) & (over(t, 2) < give)

    def chain_index(t):
        return t - jnp.minimum(over(t, 2), give)

    def is_taken(t):
        return (t >= start) & (t < start + take)

    def own_index(t):
        return t - jnp.clip(t - start, 0, take)

    def gift_copy(d):
        return remote(gift_out.at[d], gift_in.at[d], gift_sem.at[0, d], gift_sem.at[1, d], friend, batch)

    def back_copy(r, d):
        return remote(
            tot_out.at[within(r, far)], back_in.at[d], mid_sem.at[3, within(d, 8)], gift_sem.at[2, d], friend, batch
        )

    def back_share(d):
        return remote(
            back_in.at[d], back_sib.at[d], short_sem.at[2, within(d, 4)], gift_sem.at[3, d], section, sibling
        )

    def store_back(d, source, who, sem):
        j, row, col = place(4 * d + 2 + who)
        return pltpu.make_async_copy(
            source.at[d], wide_out.at[j, pl.ds(row, high), pl.ds(col, broad)], sem
        )

    def up_copy(k):
        k = within(k, far)
        return remote(up_out.at[k], up_in.at[k], far_sem.at[0, k], far_sem.at[1, k], section, inner)

    def mirror_copy(k):
        k = within(k, far)
        return remote(up_out.at[k], ret_in.at[k], far_sem.at[0, k], far_sem.at[2, k], section, inner)

    def ret_copy(k):
        k = within(k, far)
        return remote(tot_out.at[k], ret_in.at[k], mid_sem.at[0, within(k, 8)], far_sem.at[2, k], section, outer)

    def share_copy(r):
        k, at = within(r, far), within(own_index(r), near)
        return remote(tot_out.at[k], tot_in.at[at], mid_sem.at[1, within(r, 8)], near_sem.at[1, at], section, sibling)

    def piece_of(r):
        return jnp.where(r < give, 2 * r, own_index(r) + give)

    def store_own(r):
        j, row, col = place(2 * piece_of(r) + core)
        k = within(r, far)
        return pltpu.make_async_copy(
            tot_out.at[k], wide_out.at[j, pl.ds(row, high), pl.ds(col, broad)], mid_sem.at[2, within(r, 8)]
        )

    def store_other(r):
        j, row, col = place(2 * piece_of(r) + 1 - core)
        k = within(own_index(r), near)
        return pltpu.make_async_copy(
            tot_in.at[k], wide_out.at[j, pl.ds(row, high), pl.ds(col, broad)], short_sem.at[1, within(k, 4)]
        )

    def is_result(r):
        return (r >= 0) & (r < pieces - give + take)

    lag = jnp.minimum(NEXT + 3 + 8 * depth, LAG)
    small_at = NEXT + 4 + 4 * (half - 1 - depth)
    small_back = NEXT + 4 + 4 * half + 4 * depth

    def small_fill():
        for k in range(2):
            small[0, k : k + 1, :] = jnp.sum(bias_acc[k], axis=0, keepdims=True)
        small[0, 2:3, 0:width] = jnp.sum(gain_acc[...], axis=0, keepdims=True)
        small[0, 2:3, width:] = jnp.zeros((1, hidden - width), F32)
        small[0, 3:8, :] = jnp.zeros((5, hidden), F32)

    def small_sib():
        return remote(small.at[0], small.at[1], small_sem.at[0], small_sem.at[1], section, sibling)

    def small_up(to):
        return remote(small.at[2], small.at[to], small_sem.at[2], small_sem.at[to], section, inner)

    def small_ret():
        return remote(small.at[5], small.at[4], small_sem.at[5], small_sem.at[4], section, outer)

    def small_step(t):
        @pl.when(t == NEXT)
        def _():
            small_fill()
            small_sib().start()

        @pl.when(t == small_at)
        def _():
            small_sib().wait_recv()
            small[2] = small[0] + small[1]

            @pl.when(has_outer)
            def _():
                small_up(3).wait_recv()
                small[2] = small[2] + small[3]

            @pl.when(middle)
            def _():
                small_up(4).start()

            @pl.when(jnp.logical_not(middle))
            def _():
                small_up(3).start()

        @pl.when(t == small_back)
        def _():
            small_up(4).wait_recv()

            @pl.when(middle)
            def _():
                small[5] = small[2] + small[4]

            @pl.when(jnp.logical_not(middle))
            def _():
                small[5] = small[4]

            @pl.when(has_outer)
            def _():
                small_ret().start()

    pl.when(section > 0)(first_tiles)

    end = jnp.maximum(pieces + take + lag + 5, jnp.maximum(small_back + 1, LATE + give + 4))

    @pl.loop(NEXT, end)
    def _(t):
        @pl.when((t < pieces + take) & jnp.logical_not(is_taken(t)))
        def _():
            make(own_index(t))

        s = t - NEXT

        @pl.when((s >= 0) & (s < pieces + take))
        def _():
            i = own_index(s)
            k = chain_index(s)
            slot = within(k, far)

            def onward(total):
                @pl.when(has_outer)
                def _():
                    up_copy(k).wait_recv()
                    up_out[slot] = (total + up_in[slot].astype(F32)).astype(BF16)

                @pl.when(jnp.logical_not(has_outer))
                def _():
                    up_out[slot] = total.astype(BF16)

                @pl.when(middle)
                def _():
                    mirror_copy(k).start()

                @pl.when(jnp.logical_not(middle))
                def _():
                    up_copy(k).start()

            @pl.when(jnp.logical_not(is_taken(s)))
            def _():
                sib_copy(i).wait()
                total = own[within(i, 4), pl.ds(core * high, high), :] + sib_in[within(i, near)].astype(F32)

                @pl.when(is_given(s))
                def _():
                    d = over(s, 2)
                    gift_out[d] = total.astype(BF16)
                    gift_copy(d).start()

                @pl.when(jnp.logical_not(is_given(s)))
                def _():
                    onward(total)

            @pl.when(is_taken(s))
            def _():
                d = s - start
                gift_copy(d).wait_recv()
                onward(gift_in[d].astype(F32))

        on = jnp.logical_not(is_given(t))
        r = chain_index(t) - lag
        slot = within(r, far)

        @pl.when(on & is_result(r))
        def _():
            mirror_copy(r).wait()

            @pl.when(middle)
            def _():
                tot_out[slot] = (up_out[slot].astype(F32) + ret_in[slot].astype(F32)).astype(BF16)

            @pl.when(jnp.logical_not(middle))
            def _():
                tot_out[slot] = ret_in[slot]

            @pl.when(has_outer)
            def _():
                ret_copy(r).start()

            @pl.when(is_taken(r))
            def _():
                back_copy(r, r - start).start()

            @pl.when(jnp.logical_not(is_taken(r)))
            def _():
                share_copy(r).start()
                store_own(r).start()

        r2 = r - 2

        @pl.when(on & is_result(r2) & jnp.logical_not(is_taken(r2)))
        def _():
            share_copy(r2).wait_recv()
            store_other(r2).start()

        r4 = r - 4

        @pl.when(on & is_result(r4))
        def _():
            @pl.when(has_outer)
            def _():
                ret_copy(r4).wait_send()

            @pl.when(is_taken(r4))
            def _():
                back_copy(r4, r4 - start).wait_send()

            @pl.when(jnp.logical_not(is_taken(r4)))
            def _():
                share_copy(r4).wait_send()
                store_own(r4).wait()
                store_other(r4).wait()

        d = t - LATE

        @pl.when((d >= 0) & (d < give))
        def _():
            gift_copy(d).wait_send()
            back_copy(r, d).wait_recv()
            back_share(d).start()
            store_back(d, back_in, core, mid_sem.at[4, within(d, 8)]).start()

        d2 = d - 2

        @pl.when((d2 >= 0) & (d2 < give))
        def _():
            back_share(d2).wait()
            store_back(d2, back_sib, 1 - core, short_sem.at[3, within(d2, 4)]).start()

        d4 = d - 4

        @pl.when((d4 >= 0) & (d4 < give))
        def _():
            store_back(d4, back_in, core, mid_sem.at[4, within(d4, 8)]).wait()
            store_back(d4, back_sib, 1 - core, short_sem.at[3, within(d4, 4)]).wait()

        pl.when(t == 2 * gifts + 2)(lambda: homeward(lambda copy, far: copy.start()))
        small_step(t)

    small_out[...] = small[5] * (1.0 / math.sqrt(micro * rows * batches))

    small_sib().wait_send()
    small_up(3).wait_send()

    @pl.when(has_outer)
    def _():
        small_ret().wait_send()

    @pl.when(section != 0)
    def _():
        token_copy(section).wait_send()

    pl.when(section == 0)(lambda: side_copy().wait_send())

    @pl.when(section == 0)
    def _():
        for c in range(halves):
            around_last(c).wait_send()

    pl.when(section == last - 1)(lambda: side_last().wait_send())

    @pl.when((section != last) & (section != 0))
    def _():
        cot_copy(section).wait_send()

    for c in range(SENDS):

        @pl.when(section != last)
        def _():
            fwd_copy(0, c).wait_send()

        @pl.when(section != 0)
        def _():
            bwd_copy(0, c).wait_send()

    homeward(lambda copy, far: copy.wait_send() if far else copy.wait())

    @pl.when(section != last)
    def _():
        home_copy(x_out, final_out, 0, section).wait_recv()

    @pl.when(section != 0)
    def _():
        home_copy(dx_out, grad_out, 1, section).wait_recv()


def finish_kernel(scale, wide, small, final_in, grad_in, final, grad, weight, bias, gain, full, turned, sums, norms, sem):
    depth = wide.shape[1] // CUTS
    stores = []
    for n in range(wide.shape[0] * CUTS):
        j, span = n // CUTS, pl.ds((n % CUTS) * depth, depth)
        full[j, span, :] = wide[j, span, :].astype(F32) * scale
        stores.append(pltpu.make_async_copy(full.at[j, span], weight.at[0, j, span], sem.at[n]))
        stores[-1].start()
    sums[0] = small[0:2, :]
    norms[...] = small[2:3, 0 : norms.shape[1]]
    for source, result in ((sums, bias), (norms, gain)):
        stores.append(pltpu.make_async_copy(source, result, sem.at[len(stores)]))
        stores[-1].start()
    order = order_matrix(PART, True)
    for k, (source, result) in enumerate(((final_in, final), (grad_in, grad))):
        for c in range(source.shape[1] // PART):
            span = slice(c * PART, (c + 1) * PART)
            turned[k, span, :] = dot(order, source[0, span, :]).astype(BF16)
        stores.append(pltpu.make_async_copy(turned.at[k], result.at[0], sem.at[len(stores)]))
        stores[-1].start()
    for copy in stores:
        copy.wait()


def local(tokens, cotangent, weights, biases, gains, lengths):
    micro = lengths.shape[0]
    _, rows, width = tokens.shape
    hidden = weights.shape[3]
    parts = rows // PART
    pieces = 4 * width * hidden // (TILE[0] * TILE[1]) // 2
    any_spec = pl.BlockSpec(memory_space=pl.ANY)
    vmem = pl.BlockSpec(memory_space=pltpu.VMEM)
    dma = pltpu.SemaphoreType.DMA
    relay = pltpu.VMEM((micro, rows, width), BF16)
    near = min(8, pieces)
    far = 16
    close = pltpu.VMEM((near, *TILE), BF16)
    wait = pltpu.VMEM((far, *TILE), BF16)
    final, grad, wide, small = pl.pallas_call(
        relay_kernel,
        name="relay",
        out_shape=(
            pltpu.VMEM(tokens.shape, BF16),
            pltpu.VMEM(tokens.shape, BF16),
            pltpu.VMEM((4, width, hidden), BF16),
            pltpu.VMEM((8, hidden), F32),
        ),
        in_specs=[any_spec] * 6,
        out_specs=(vmem, vmem, vmem, vmem),
        scratch_shapes=[
            pltpu.VMEM((4, width, hidden), BF16),
            pltpu.VMEM((4, hidden, width), BF16),
            pltpu.VMEM(lengths.shape[::-1], jnp.int32),
            pltpu.VMEM((2, hidden), F32),
            pltpu.VMEM((1, width), F32),
            pltpu.VMEM((5, rows, width), BF16),
            relay,
            relay,
            relay,
            relay,
            pltpu.VMEM((micro, rows, 128), F32),
            pltpu.VMEM((micro, rows, 128), F32),
            pltpu.VMEM((micro * rows, width), BF16),
            pltpu.VMEM((micro * rows, width), BF16),
            pltpu.VMEM((4, micro * rows, hidden), BF16),
            pltpu.VMEM((4, micro * rows, hidden), F32),
            pltpu.VMEM((8, hidden), F32),
            pltpu.VMEM((8, hidden), F32),
            pltpu.VMEM((8, width), F32),
            pltpu.VMEM((2, 8, hidden), F32),
            close,
            close,
            pltpu.VMEM((4, 2 * TILE[0], TILE[1]), F32),
            wait,
            wait,
            wait,
            wait,
            close,
            pltpu.VMEM((6, 8, hidden), F32),
            pltpu.VMEM((2, width, micro * rows), BF16),
            *[pltpu.VMEM((max(GIVE), *TILE), BF16)] * 4,
            dma((9,)),
            dma((4 + 2 * micro,)),
            dma((SENDS,)),
            dma((micro, parts)),
            dma((SENDS,)),
            dma((micro, parts // PAIR)),
            dma((2, parts // PAIR)),
            dma((2, micro + 1)),
            dma((2, near)),
            dma((3, far)),
            dma((4, max(GIVE))),
            dma((5, 8)),
            dma((4, 4)),
            dma((6,)),
        ],
        compiler_params=pltpu.CompilerParams(
            collective_id=0, has_side_effects=True, vmem_limit_bytes=55 * 2**20
        ),
    )(lengths.T, tokens, cotangent, weights, biases, gains)
    scale = 1.0 / math.sqrt(micro * rows * lax.axis_size("batch"))
    return pl.pallas_call(
        functools.partial(finish_kernel, scale),
        name="finish",
        out_shape=(
            jax.ShapeDtypeStruct(tokens.shape, BF16),
            jax.ShapeDtypeStruct(tokens.shape, BF16),
            jax.ShapeDtypeStruct(weights.shape, F32),
            jax.ShapeDtypeStruct(biases.shape, F32),
            jax.ShapeDtypeStruct(gains.shape, F32),
        ),
        in_specs=[vmem, vmem, vmem, vmem],
        out_specs=(any_spec,) * 5,
        scratch_shapes=[
            pltpu.VMEM((4, width, hidden), F32),
            pltpu.VMEM((2, rows, width), BF16),
            pltpu.VMEM(biases.shape, F32),
            pltpu.VMEM(gains.shape, F32),
            dma((4 * CUTS + 4,)),
        ],
        compiler_params=pltpu.CompilerParams(vmem_limit_bytes=24 * 2**20),
    )(*[pltpu.with_memory_space_constraint(value, pltpu.VMEM) for value in (wide, small, final, grad)])


def solution(mesh):
    row = P("section", "batch", None)
    placed = (
        row,
        row,
        P("section", None, None, None),
        P("section", None, None),
        P("section", None),
        P(None, "batch"),
    )
    return jax.shard_map(
        local,
        mesh=mesh,
        in_specs=placed,
        out_specs=(row, row, *placed[2:5]),
        check_vma=False,
    )
```
